32 devices in a mesh: sp: 16 (over z, y, x), fl: 2 (over core).
Axes of the slice: x: 2, y: 2, z: 4, core: 2. Of those that a mesh axis runs over, the one named last changes fastest.
Arguments:
- volume: bfloat16 [16, 64, 16, 24, 512], P('sp'), may hold values from -6 to 6
- kernel_three: bfloat16 [128, 1728], P('fl'), may hold values from -0.15625 to 0.15625
- gain_three: float32 [128], P('fl'), may hold values from 0.1 to 1.9
- shift_three: float32 [128], P('fl'), may hold values from -0.5 to 0.5
- kernel_four: bfloat16 [256, 3456], P('fl'), may hold values from -0.109375 to 0.109375
- gain_four: float32 [256], P('fl'), may hold values from 0.1 to 1.9
- shift_four: float32 [256], P('fl'), may hold values from -0.5 to 0.5
Outputs:
- deep_features: bfloat16 [16, 256, 4, 6, 128], P('sp', 'fl')
The draws below stay inside these ranges and needn't reach their ends.
All inputs are finite; a program needn't handle non-finite values.
Results may differ from the reference program's by a relative error of at most 0.0048.
Values may be sent and summed in bfloat16 or wider, within the bound.
No kernel may reach another device: no remote copies, remote signals or barrier semaphores. Data moves between devices by JAX's collectives and lax.ppermute only.
A program may use at most 320 MiB of HBM per device.

```python
import jax
import jax.numpy as jnp
from jax import lax

C0 = 64
C1 = 128
C2 = 256
PD = 16
PR = 24
W = 512
DEPTH = 32
H = 192
N_SP = 16


def steps_of(key, shape, shards, low, high):
    loudness, own = 1.0, jax.random.fold_in(key, 6)
    for position, blocks in shards:
        steps = jnp.exp(jax.random.uniform(jax.random.fold_in(own, position), (blocks,), jnp.float32, low / len(shards), high / len(shards)))
        loudness = loudness * jnp.repeat(steps, shape[position] // blocks).reshape([-1 if axis == position else 1 for axis in range(len(shape))])
    return loudness


def gaussian(own_key, extent, deviation, most, cuts=(), kind=jnp.bfloat16):
    array = deviation * jax.random.normal(own_key, extent, jnp.float32)
    if cuts:
        array = array * steps_of(own_key, extent, cuts, -0.22, 0.18)
    return jnp.clip(array, -most, most).astype(kind)


def setup_inputs(seed: int = 0) -> dict:
    streams_of = jax.random.split(jax.random.key(seed), 8)
    volume = gaussian(streams_of[0], (N_SP, C0, PD, PR, W), 1.0, 6.0, ((0, 16),))
    kernel_three = gaussian(streams_of[1], (C1, C0 * 27), (C0 * 27) ** -0.5, 0.15625, ((0, 2),))
    gain_three = jnp.clip(1.0 + 0.18 * jax.random.normal(streams_of[2], (C1,), jnp.float32), 0.1, 1.9)
    shift_three = jnp.clip(jax.random.uniform(streams_of[3], (C1,), jnp.float32, -0.5, 0.5) * steps_of(streams_of[3], (C1,), ((0, 2),), -0.4, 0.0), -0.5, 0.5)
    kernel_four = gaussian(streams_of[4], (C2, C1 * 27), (C1 * 27) ** -0.5, 0.109375, ((0, 2),))
    gain_four = jnp.clip(1.0 + 0.18 * jax.random.normal(streams_of[5], (C2,), jnp.float32), 0.1, 1.9)
    shift_four = jnp.clip(jax.random.uniform(streams_of[6], (C2,), jnp.float32, -0.5, 0.5) * steps_of(streams_of[6], (C2,), ((0, 2),), -0.4, 0.0), -0.5, 0.5)
    return {"volume": volume, "kernel_three": kernel_three, "gain_three": gain_three, "shift_three": shift_three, "kernel_four": kernel_four, "gain_four": gain_four, "shift_four": shift_four}


def convolve(slab, kernel, pads):
    return lax.conv_general_dilated(slab[None], kernel, (2, 2, 2), pads, dimension_numbers=("NCDHW", "OIDHW", "NCDHW"), precision=lax.Precision.HIGHEST)[0]


def activate(conv_out, gain, shift):
    return jax.nn.relu(conv_out * gain[:, None, None, None] + shift[:, None, None, None]).astype(jnp.bfloat16)


def reference(volume, kernel_three, gain_three, shift_three, kernel_four, gain_four, shift_four):
    weights_three = kernel_three.astype(jnp.float32).reshape(C1, C0, 3, 3, 3)
    weights_four = kernel_four.astype(jnp.float32).reshape(C2, C1, 3, 3, 3)
    groups = N_SP // 8

    def layer_block(group):
        start = (group * 8).astype(jnp.int32)
        blocks = lax.dynamic_slice_in_dim(volume, start, 8, 0)
        inner = jnp.transpose(blocks, (1, 2, 0, 3, 4)).reshape(C0, PD, H, W)
        prior = lax.dynamic_slice_in_dim(volume, jnp.maximum(start - 8, 0).astype(jnp.int32), 8, 0)[:, :, PD - 1]
        prior = jnp.transpose(prior, (1, 0, 2, 3)).reshape(C0, 1, H, W)
        prior = prior * (group > 0).astype(volume.dtype)
        slab = jnp.concatenate([prior, inner], 1).astype(jnp.float32)
        return activate(convolve(slab, weights_three, ((0, 0), (1, 1), (1, 1))), gain_three, shift_three)

    pieces = lax.map(layer_block, jnp.arange(groups, dtype=jnp.int32))
    third = jnp.moveaxis(pieces, 0, 1).reshape(C1, DEPTH // 2, H // 2, W // 2)
    fourth = activate(convolve(third.astype(jnp.float32), weights_four, ((1, 1), (1, 1), (1, 1))), gain_four, shift_four)
    fourth = fourth.reshape(C2, groups, PD // 4, 8, PR // 4, W // 4)
    return jnp.transpose(fourth, (1, 3, 0, 2, 4, 5)).reshape(N_SP, C2, PD // 4, PR // 4, W // 4)
```

```python
import functools

import jax
import jax.numpy as jnp
import numpy as np
from jax import lax
from jax.experimental import pallas as pl
from jax.experimental.pallas import tpu as pltpu
from jax.sharding import PartitionSpec as P

F32 = jnp.float32
BF16 = jnp.bfloat16
LANES = 128
ROW_BLOCKS = 8
VMEM_LIMIT = 56 * 2**20


def even_odd(width):
    half = width // 2
    place = np.zeros((width, width), np.float32)
    place[np.arange(0, width, 2), np.arange(half)] = 1
    place[np.arange(1, width, 2), half + np.arange(half)] = 1
    return jnp.asarray(place, BF16)


def activate(total, gain, shift):
    return jnp.maximum(total * gain + shift, 0.0)


def shifted(odd):
    lane = lax.broadcasted_iota(jnp.int32, odd.shape, 1)
    return jnp.where(lane == 0, 0.0, pltpu.roll(odd, 1, 1))


def three_kernel(
    core_ref, x_ref, w_ref, place_ref, gain_ref, shift_ref,
    third_ref, plane_ref, row_ref, next_plane_ref, next_row_ref, next_corner_ref,
    split_ref, data_ref,
):
    step = pl.program_id(0)
    chans, rows, width = x_ref.shape[1], x_ref.shape[3], x_ref.shape[4]
    half = width // 2
    out_rows = rows // 2
    taps = 3 * chans
    group = 16

    @pl.when(step == 0)
    def _():
        data_ref[0] = jnp.zeros_like(data_ref[0])
        for slot in (1, 2):
            data_ref[slot, 0] = jnp.zeros_like(data_ref[slot, 0])
            data_ref[slot, rows + 1] = jnp.zeros_like(data_ref[slot, 0])
            data_ref[slot, rows + 2] = jnp.zeros_like(data_ref[slot, 0])

    @pl.when(step > 0)
    def _():
        data_ref[0] = data_ref[2]

    def separate(which, _):
        plane = which // (chans // group)
        first = (which % (chans // group)) * group
        x = x_ref[0, pl.ds(first, group), plane]
        x = x.astype(F32).reshape(group * rows, width).astype(BF16)
        quarter = half // 2
        for side in range(2):
            parts = jnp.dot(
                x[:, side * half : (side + 1) * half], place_ref[...], preferred_element_type=F32
            )
            for block in range(2 * quarter // LANES):
                odd, at = divmod(block, quarter // LANES)
                split_ref[odd, side * (quarter // LANES) + at] = parts[:, block * LANES : (block + 1) * LANES]
        for row in range(rows):
            even, odd = (
                jnp.concatenate(
                    [split_ref[odd, at, pl.ds(row, group, stride=rows), :] for at in range(half // LANES)], 1
                )
                for odd in range(2)
            )
            for tap, value in enumerate((shifted(odd), even, odd)):
                data_ref[plane + 1, row + 1, pl.ds(tap * chans + first, group), :] = value.astype(BF16)
        return 0

    lax.fori_loop(0, 2 * (chans // group), separate, 0)

    gain, shift = gain_ref[...], shift_ref[...]

    def sums(row):
        parts = [data_ref[slot, pl.ds(2 * row, 3)].reshape(3 * taps, half) for slot in range(3)]
        return jnp.dot(w_ref[...], jnp.concatenate(parts, 0), preferred_element_type=F32)

    def out_row(row, _):
        total = sums(row)
        third_ref[0, row] = activate(total, gain, shift).astype(BF16)

        @pl.when(step == 0)
        def _():
            plane_ref[row] = total

        @pl.when(row == 0)
        def _():
            row_ref[0] = total

        return 0

    lax.fori_loop(0, out_rows, out_row, 0)
    next_row_ref[0] = sums(out_rows).astype(BF16)

    @pl.when(step == pl.num_programs(0) - 1)
    def _():
        def beyond(row):
            return jnp.dot(
                w_ref[:, : 3 * taps],
                data_ref[2, pl.ds(2 * row, 3)].reshape(3 * taps, half),
                preferred_element_type=F32,
            ).astype(BF16)

        def plane_row(row, _):
            next_plane_ref[row] = beyond(row)
            return 0

        lax.fori_loop(0, out_rows, plane_row, 0)
        next_corner_ref[...] = beyond(out_rows)


def layer_three(volume, weights, gain, shift, core):
    _, chans, planes, rows, width = volume.shape
    outs = weights.shape[0]
    half = width // 2
    steps, out_rows = planes // 4, rows // 2
    full = lambda *shape: pl.BlockSpec(shape, lambda i, core: (0,) * len(shape))
    return pl.pallas_call(
        three_kernel,
        grid_spec=pltpu.PrefetchScalarGridSpec(
            num_scalar_prefetch=1,
            grid=(steps,),
            in_specs=[
                pl.BlockSpec((1, chans, 2, rows, width), lambda i, core: (0, 0, core[0] * steps + i, 0, 0)),
                full(*weights.shape),
                full(half, half),
                full(outs, 1),
                full(outs, 1),
            ],
            out_specs=[
                pl.BlockSpec((1, out_rows, outs, half), lambda i, core: (i, 0, 0, 0)),
                full(out_rows, outs, half),
                pl.BlockSpec((1, outs, half), lambda i, core: (i, 0, 0)),
                full(out_rows, outs, half),
                pl.BlockSpec((1, outs, half), lambda i, core: (i, 0, 0)),
                full(outs, half),
            ],
            scratch_shapes=[
                pltpu.VMEM((2, half // LANES, 16 * rows, LANES), F32),
                pltpu.VMEM((3, rows + 3, 3 * chans, half), BF16),
            ],
        ),
        out_shape=[
            jax.ShapeDtypeStruct((steps, out_rows, outs, half), BF16),
            jax.ShapeDtypeStruct((out_rows, outs, half), F32),
            jax.ShapeDtypeStruct((steps, outs, half), F32),
            jax.ShapeDtypeStruct((out_rows, outs, half), BF16),
            jax.ShapeDtypeStruct((steps, outs, half), BF16),
            jax.ShapeDtypeStruct((outs, half), BF16),
        ],
        compiler_params=pltpu.CompilerParams(vmem_limit_bytes=VMEM_LIMIT),
        name="layer_three",
    )(core, volume, weights, even_odd(half), gain, shift)


def four_kernel(
    third_ref, plane_ref, row_ref, halo_plane_ref, halo_row_ref, halo_corner_ref,
    w_ref, place_ref, gain_ref, shift_ref,
    sums_ref, next_plane_ref, next_row_ref, next_corner_ref,
    data_ref,
):
    planes, rows, chans, width = third_ref.shape
    half = width // 2
    out_rows = rows // 2
    count = planes // 2
    gain, shift = gain_ref[...], shift_ref[...]
    data_ref[:, 0] = jnp.zeros_like(data_ref[:, 0])
    for extra in (1, 2):
        data_ref[:, rows + extra] = jnp.zeros_like(data_ref[:, 0])
    data_ref[0, :, :, :half] = jnp.zeros_like(data_ref[0, :, :, :half])

    def place(plane, row, value):
        both = jnp.dot(value, place_ref[...], preferred_element_type=F32)
        even, odd = both[:, :half], both[:, half:]
        spots = [(1 + plane % 2, plane // 2)]
        if plane % 2 and plane // 2 + 1 < count:
            spots.append((0, plane // 2 + 1))
        for tap, part in enumerate((shifted(odd), even, odd)):
            for slot, lanes in spots:
                data_ref[slot, row + 1, tap * chans : (tap + 1) * chans, lanes * half : (lanes + 1) * half] = (
                    part.astype(BF16)
                )

    for plane in range(planes):
        if plane == 0:
            total = plane_ref[0] + halo_plane_ref[0].astype(F32) + halo_corner_ref[...].astype(F32)
        else:
            total = row_ref[plane]
        total = total + halo_row_ref[plane].astype(F32)
        place(plane, 0, activate(total, gain, shift).astype(BF16))

        def row_of(row, _, plane=plane):
            if plane == 0:
                total = plane_ref[row] + halo_plane_ref[row].astype(F32)
                value = activate(total, gain, shift).astype(BF16)
            else:
                value = third_ref[plane, row]
            place(plane, row, value)
            return 0

        lax.fori_loop(1, rows, row_of, 0)

    taps = 3 * chans

    def sums(row):
        parts = [data_ref[slot, pl.ds(2 * row, 3)].reshape(3 * taps, count * half) for slot in range(3)]
        return jnp.dot(w_ref[...], jnp.concatenate(parts, 0), preferred_element_type=F32)

    def beyond(row):
        part = data_ref[2, pl.ds(2 * row, 3), :, (count - 1) * half :].reshape(3 * taps, half)
        return jnp.dot(w_ref[:, : 3 * taps], part, preferred_element_type=F32).astype(BF16)

    def out_row(row, _):
        sums_ref[row] = sums(row)
        next_plane_ref[row] = beyond(row)
        return 0

    lax.fori_loop(0, out_rows, out_row, 0)
    next_row_ref[...] = sums(out_rows).astype(BF16)
    next_corner_ref[...] = beyond(out_rows)


def layer_four(third, plane, row, halos, weights, gain, shift):
    planes, rows, chans, width = third.shape
    outs = weights.shape[0]
    half = width // 2
    out_rows, count = rows // 2, planes // 2
    return pl.pallas_call(
        four_kernel,
        out_shape=[
            jax.ShapeDtypeStruct((out_rows, outs, count * half), F32),
            jax.ShapeDtypeStruct((out_rows, outs, half), BF16),
            jax.ShapeDtypeStruct((outs, count * half), BF16),
            jax.ShapeDtypeStruct((outs, half), BF16),
        ],
        scratch_shapes=[pltpu.VMEM((3, rows + 3, 3 * chans, count * half), BF16)],
        compiler_params=pltpu.CompilerParams(vmem_limit_bytes=VMEM_LIMIT),
        name="layer_four",
    )(third, plane, row, *halos, weights, even_odd(width), gain, shift)


def exchange(plane, row, corner):
    count = lax.axis_size("sp")
    axes = ("sp", "fl")
    blocks = range(count)
    inner = [b for b in blocks if b % ROW_BLOCKS != ROW_BLOCKS - 1]
    down = [(2 * b, 2 * b + 1) for b in blocks]
    down += [(2 * b + 1, 2 * (b + ROW_BLOCKS)) for b in blocks if b + ROW_BLOCKS < count]
    along = [(2 * b + core, 2 * (b + 1) + core) for b in inner for core in range(2)]
    both = [(2 * b, 2 * (b + 1) + 1) for b in inner]
    both += [(2 * b + 1, 2 * (b + 1 + ROW_BLOCKS)) for b in inner if b + ROW_BLOCKS < count]
    return (
        lax.ppermute(plane, axes, down),
        lax.ppermute(row, axes, along),
        lax.ppermute(corner, axes, both),
    )


def both_cores(value, core):
    other = lax.ppermute(value, "fl", [(0, 1), (1, 0)])
    return jnp.where(core == 0, jnp.concatenate([value, other], 0), jnp.concatenate([other, value], 0))


def tap_major(kernel, chans):
    outs = kernel.shape[0]
    return jnp.transpose(kernel.reshape(outs, chans, 27), (0, 2, 1)).reshape(outs, 27 * chans)


def shards(volume, kernel_three, gain_three, shift_three, kernel_four, gain_four, shift_four):
    core = lax.axis_index("fl")
    chans = volume.shape[1]
    mid = 2 * kernel_three.shape[0]
    scales_three = both_cores(jnp.stack([gain_three, shift_three], 1), core)
    scales_four = both_cores(jnp.stack([gain_four, shift_four], 1), core)
    weights_three = tap_major(both_cores(kernel_three, core), chans)
    weights_four = tap_major(both_cores(kernel_four, core), mid)
    gain, shift = scales_three[:, :1], scales_three[:, 1:]
    third, plane, row, *nexts = layer_three(volume, weights_three, gain, shift, core.reshape(1))
    halos = exchange(*nexts)
    total, *nexts = layer_four(third, plane, row, halos, weights_four, gain, shift)
    halo_plane, halo_row, halo_corner = exchange(*nexts)
    out_rows, outs, lanes = total.shape
    width = halo_plane.shape[2]
    total = total.reshape(out_rows, outs, lanes // width, width)
    total = total.at[:, :, 0].add(halo_plane.astype(F32))
    total = total.at[0].add(halo_row.reshape(outs, lanes // width, width).astype(F32))
    total = total.at[0, :, 0].add(halo_corner.astype(F32))
    fourth = activate(total, scales_four[:, :1, None], scales_four[:, 1:, None]).astype(BF16)
    fourth = jnp.transpose(fourth, (1, 2, 0, 3))
    half = outs // 2
    own = lax.dynamic_slice_in_dim(fourth, core * half, half, 0)
    theirs = lax.dynamic_slice_in_dim(fourth, (1 - core) * half, half, 0)
    other = lax.ppermute(theirs, "fl", [(0, 1), (1, 0)])
    return jnp.where(core == 0, jnp.concatenate([own, other], 1), jnp.concatenate([other, own], 1))[None]


def solution(mesh):
    return jax.shard_map(
        shards,
        mesh=mesh,
        in_specs=(
            P("sp", None, None, None, None),
            P("fl", None),
            P("fl"),
            P("fl"),
            P("fl", None),
            P("fl"),
            P("fl"),
        ),
        out_specs=P("sp", "fl", None, None, None),
        check_vma=False,
    )
```

```python
import functools

import jax
import jax.numpy as jnp
import numpy as np
from jax import lax
from jax.experimental import pallas as pl
from jax.experimental.pallas import tpu as pltpu
from jax.sharding import PartitionSpec as P

F32 = jnp.float32
BF16 = jnp.bfloat16
LANES = 128
ROW_BLOCKS = 8
SUB = 8
GROUP = 16
VMEM_LIMIT = 56 * 2**20


def even_odd(width):
    half = width // 2
    place = np.zeros((width, width), np.float32)
    place[np.arange(0, width, 2), np.arange(half)] = 1
    place[np.arange(1, width, 2), half + np.arange(half)] = 1
    return jnp.asarray(place, BF16)


def activate(total, gain, shift):
    return jnp.maximum(total * gain + shift, 0.0)


def shifted(odd):
    lane = lax.broadcasted_iota(jnp.int32, odd.shape, 1)
    return jnp.where(lane == 0, 0.0, pltpu.roll(odd, 1, 1))


def spread(sides, place):
    quarter = place.shape[0] // 2
    split = [jnp.dot(side, place, preferred_element_type=F32) for side in sides]
    even = jnp.concatenate([part[:, :quarter] for part in split], 1)
    odd = jnp.concatenate([part[:, quarter:] for part in split], 1)
    return shifted(odd), even, odd


def separate(x_ref, plane, place_ref, split_refs, store):
    chans, rows, width = x_ref.shape[1], x_ref.shape[3], x_ref.shape[4]
    half = width // 2
    quarter = half // 2
    for index, first in enumerate(range(0, chans, GROUP)):
        split_ref = split_refs[index % len(split_refs)]
        x = x_ref[0, pl.ds(first, GROUP), plane]
        x = x.astype(F32).reshape(GROUP * rows, width).astype(BF16)
        for side in range(2):
            parts = jnp.dot(
                x[:, side * half : (side + 1) * half], place_ref[...], preferred_element_type=F32
            )
            for block in range(half // LANES):
                odd, at = divmod(block, quarter // LANES)
                split_ref[odd, side * (quarter // LANES) + at] = parts[:, block * LANES : (block + 1) * LANES]
        for row in range(rows):
            even, odd = (
                jnp.concatenate(
                    [split_ref[odd, at, pl.ds(row, GROUP, stride=rows), :] for at in range(half // LANES)], 1
                )
                for odd in range(2)
            )
            for tap, value in enumerate((shifted(odd), even, odd)):
                store(tap, row, first, value.astype(BF16))


def three_edges_kernel(
    core_ref, last_ref, rim_ref, w_ref, place_ref,
    next_plane_ref, next_row_ref, next_corner_ref,
    *scratch,
):
    *split_refs, pick_ref, data_ref = scratch
    chans, rows, width = last_ref.shape[1], last_ref.shape[3], last_ref.shape[4]
    planes = rim_ref.shape[2]
    half = width // 2
    out_rows = rows // 2
    taps = 3 * chans
    rim = (rows - 1) % SUB

    picked = []
    for plane in range(planes):
        x = rim_ref[0, :, plane, :SUB].astype(F32).reshape(chans * SUB, width)
        for at in range(width // LANES):
            pick_ref[plane % 2, at] = x[:, at * LANES : (at + 1) * LANES]
        picked.append(
            jnp.concatenate(
                [pick_ref[plane % 2, at, pl.ds(rim, chans, stride=SUB), :] for at in range(width // LANES)], 1
            ).astype(BF16)
        )
    picked = jnp.concatenate(picked, 0)
    parts = spread((picked[:, :half], picked[:, half:]), place_ref[...])
    parts = [part.astype(BF16) for part in parts]

    def rim_data(plane):
        return jnp.concatenate([part[plane * chans : (plane + 1) * chans] for part in parts], 0)

    none = jnp.zeros((taps, half), BF16)
    for step in range(planes // 2):
        pieces = []
        for plane in range(2 * step - 1, 2 * step + 2):
            pieces += [none if plane < 0 else rim_data(plane), none, none]
        total = jnp.dot(w_ref[...], jnp.concatenate(pieces, 0), preferred_element_type=F32)
        next_row_ref[step] = total.astype(BF16)

    def beyond(data):
        return jnp.dot(w_ref[:, : 3 * taps], data, preferred_element_type=F32).astype(BF16)

    next_corner_ref[...] = beyond(jnp.concatenate([rim_data(planes - 1), none, none], 0))

    def store(tap, row, first, value):
        data_ref[row + 1, tap * chans + first : tap * chans + first + GROUP, :] = value

    data_ref[0] = jnp.zeros_like(data_ref[0])
    separate(last_ref, 0, place_ref, split_refs, store)
    for row in range(out_rows):
        next_plane_ref[row] = beyond(data_ref[2 * row : 2 * row + 3].reshape(3 * taps, half))


def three_edges(volume, weights, core):
    _, chans, planes, rows, width = volume.shape
    outs = weights.shape[0]
    half = width // 2
    own, out_rows = planes // 2, rows // 2
    full = lambda *shape: pl.BlockSpec(shape, lambda i, core: (0,) * len(shape))
    return pl.pallas_call(
        three_edges_kernel,
        grid_spec=pltpu.PrefetchScalarGridSpec(
            num_scalar_prefetch=1,
            grid=(1,),
            in_specs=[
                pl.BlockSpec((1, chans, 1, rows, width), lambda i, core: (0, 0, (core[0] + 1) * own - 1, 0, 0)),
                pl.BlockSpec((1, chans, own, 2 * SUB, width), lambda i, core: (0, 0, core[0], (rows - 1) // (2 * SUB), 0)),
                full(*weights.shape),
                full(half, half),
            ],
            out_specs=[
                full(out_rows, outs, half),
                full(own // 2, outs, half),
                full(outs, half),
            ],
            scratch_shapes=[pltpu.VMEM((2, half // LANES, GROUP * rows, LANES), F32)] * 4
            + [
                pltpu.VMEM((2, width // LANES, chans * SUB, LANES), F32),
                pltpu.VMEM((rows + 1, 3 * chans, half), BF16),
            ],
        ),
        out_shape=[
            jax.ShapeDtypeStruct((out_rows, outs, half), BF16),
            jax.ShapeDtypeStruct((own // 2, outs, half), BF16),
            jax.ShapeDtypeStruct((outs, half), BF16),
        ],
        compiler_params=pltpu.CompilerParams(vmem_limit_bytes=VMEM_LIMIT),
        cost_estimate=pl.CostEstimate(flops=2 * 10**9, bytes_accessed=8 * 10**6, transcendentals=0),
        name="three_edges",
    )(core, volume, volume, weights, even_odd(half))


def three_kernel(
    core_ref, x_ref, w_ref, place_ref, gain_ref, shift_ref,
    third_ref, plane_ref, row_ref,
    *scratch,
):
    *split_refs, data_ref, total_ref = scratch
    step = pl.program_id(0)
    chans, rows, width = x_ref.shape[1], x_ref.shape[3], x_ref.shape[4]
    half = width // 2
    out_rows = rows // 2
    taps = 3 * chans

    @pl.when(step == 0)
    def _():
        data_ref[0] = jnp.zeros_like(data_ref[0])
        for slot in (1, 2):
            data_ref[slot, 0] = jnp.zeros_like(data_ref[slot, 0])

    @pl.when(step > 0)
    def _():
        data_ref[0] = data_ref[2]

    for plane in range(2):

        def store(tap, row, first, value, slot=plane + 1):
            data_ref[slot, row + 1, tap * chans + first : tap * chans + first + GROUP, :] = value

        separate(x_ref, plane, place_ref, split_refs, store)

    gain, shift = gain_ref[...], shift_ref[...]
    for row in range(out_rows):
        parts = [data_ref[slot, 2 * row : 2 * row + 3].reshape(3 * taps, half) for slot in range(3)]
        total = jnp.dot(w_ref[...], jnp.concatenate(parts, 0), preferred_element_type=F32)
        third_ref[0, row] = activate(total, gain, shift).astype(BF16)
        total_ref[row] = total
    row_ref[0] = total_ref[0]

    @pl.when(step == 0)
    def _():
        plane_ref[...] = total_ref[...]


def layer_three(volume, weights, gain, shift, core):
    _, chans, planes, rows, width = volume.shape
    outs = weights.shape[0]
    half = width // 2
    steps, out_rows = planes // 4, rows // 2
    full = lambda *shape: pl.BlockSpec(shape, lambda i, core: (0,) * len(shape))
    return pl.pallas_call(
        three_kernel,
        grid_spec=pltpu.PrefetchScalarGridSpec(
            num_scalar_prefetch=1,
            grid=(steps,),
            in_specs=[
                pl.BlockSpec((1, chans, 2, rows, width), lambda i, core: (0, 0, core[0] * steps + i, 0, 0)),
                full(*weights.shape),
                full(half, half),
                full(outs, 1),
                full(outs, 1),
            ],
            out_specs=[
                pl.BlockSpec((1, out_rows, outs, half), lambda i, core: (i, 0, 0, 0)),
                full(out_rows, outs, half),
                pl.BlockSpec((1, outs, half), lambda i, core: (i, 0, 0)),
            ],
            scratch_shapes=[pltpu.VMEM((2, half // LANES, GROUP * rows, LANES), F32)] * 4
            + [
                pltpu.VMEM((3, rows + 1, 3 * chans, half), BF16),
                pltpu.VMEM((out_rows, outs, half), F32),
            ],
        ),
        out_shape=[
            jax.ShapeDtypeStruct((steps, out_rows, outs, half), BF16),
            jax.ShapeDtypeStruct((out_rows, outs, half), F32),
            jax.ShapeDtypeStruct((steps, outs, half), F32),
        ],
        compiler_params=pltpu.CompilerParams(vmem_limit_bytes=VMEM_LIMIT),
        cost_estimate=pl.CostEstimate(flops=10**10, bytes_accessed=2 * 10**7, transcendentals=0),
        name="layer_three",
    )(core, volume, weights, even_odd(half), gain, shift)


def third_value(refs, plane, row):
    third_ref, plane_ref, row_ref, halo_plane_ref, halo_row_ref, halo_corner_ref, gain_ref, shift_ref = refs
    if plane and row:
        return third_ref[plane, row]
    total = row_ref[plane] if plane else plane_ref[row] + halo_plane_ref[row].astype(F32)
    if not row:
        total = total + halo_row_ref[plane].astype(F32)
        if not plane:
            total = total + halo_corner_ref[...].astype(F32)
    return activate(total, gain_ref[...], shift_ref[...]).astype(BF16)


def four_edges_kernel(*refs):
    *thirds, w_ref, place_ref, next_plane_ref, next_row_ref, next_corner_ref = refs
    planes, rows, chans, width = thirds[0].shape
    half = width // 2
    out_rows, count = rows // 2, planes // 2
    taps = 3 * chans

    def data(spots):
        values = jnp.concatenate([third_value(thirds, *spot) for spot in spots], 0)
        parts = [part.astype(BF16) for part in spread((values,), place_ref[...])]
        return [
            jnp.concatenate([part[at * chans : (at + 1) * chans] for part in parts], 0) for at in range(len(spots))
        ]

    none = jnp.zeros((taps, half), BF16)
    rim = data([(plane, rows - 1) for plane in range(planes)])
    last = [none] + data([(planes - 1, row) for row in range(rows - 1)]) + [rim[planes - 1]]

    def beyond(pieces):
        return jnp.dot(w_ref[:, : 3 * taps], pieces, preferred_element_type=F32).astype(BF16)

    for row in range(0, out_rows, 2):
        pieces = [jnp.concatenate([last[2 * row + at], last[2 * row + 2 + at]], 1) for at in range(3)]
        both = beyond(jnp.concatenate(pieces, 0))
        next_plane_ref[row] = both[:, :half]
        next_plane_ref[row + 1] = both[:, half:]
    empty = jnp.zeros((taps, count * half), BF16)
    pieces = []
    for slot in range(3):
        pieces.append(
            jnp.concatenate([rim[2 * m + slot - 1] if 2 * m + slot else none for m in range(count)], 1)
        )
        pieces += [empty, empty]
    next_row_ref[...] = jnp.dot(
        w_ref[...], jnp.concatenate(pieces, 0), preferred_element_type=F32
    ).astype(BF16)
    next_corner_ref[...] = beyond(jnp.concatenate([rim[planes - 1], none, none], 0))


def four_edges(thirds, weights):
    planes, rows, chans, width = thirds[0].shape
    outs = weights.shape[0]
    half = width // 2
    return pl.pallas_call(
        four_edges_kernel,
        out_shape=[
            jax.ShapeDtypeStruct((rows // 2, outs, half), BF16),
            jax.ShapeDtypeStruct((outs, planes // 2 * half), BF16),
            jax.ShapeDtypeStruct((outs, half), BF16),
        ],
        compiler_params=pltpu.CompilerParams(vmem_limit_bytes=VMEM_LIMIT),
        cost_estimate=pl.CostEstimate(flops=2 * 10**9, bytes_accessed=8 * 10**6, transcendentals=0),
        name="four_edges",
    )(*thirds, weights, even_odd(width))


def four_kernel(*refs):
    *thirds, w_ref, place_ref, sums_ref, data_ref = refs
    planes, rows, chans, width = thirds[0].shape
    half = width // 2
    out_rows, count = rows // 2, planes // 2
    taps = 3 * chans
    data_ref[:, 0] = jnp.zeros_like(data_ref[:, 0])
    data_ref[0, :, :, :half] = jnp.zeros_like(data_ref[0, :, :, :half])
    batch = 4
    for plane in range(planes):
        spots = [(1 + plane % 2, plane // 2)]
        if plane % 2 and plane // 2 + 1 < count:
            spots.append((0, plane // 2 + 1))
        for first in range(0, rows, batch):
            values = jnp.concatenate([third_value(thirds, plane, row) for row in range(first, first + batch)], 0)
            for tap, part in enumerate(spread((values,), place_ref[...])):
                part = part.astype(BF16)
                for at in range(batch):
                    for slot, lanes in spots:
                        data_ref[
                            slot, first + at + 1, tap * chans : (tap + 1) * chans, lanes * half : (lanes + 1) * half
                        ] = part[at * chans : (at + 1) * chans]
    for row in range(out_rows):
        parts = [data_ref[slot, 2 * row : 2 * row + 3].reshape(3 * taps, count * half) for slot in range(3)]
        sums_ref[row] = jnp.dot(w_ref[...], jnp.concatenate(parts, 0), preferred_element_type=F32)


def layer_four(thirds, weights):
    planes, rows, chans, width = thirds[0].shape
    outs = weights.shape[0]
    half = width // 2
    out_rows, count = rows // 2, planes // 2
    return pl.pallas_call(
        four_kernel,
        out_shape=jax.ShapeDtypeStruct((out_rows, outs, count * half), F32),
        scratch_shapes=[pltpu.VMEM((3, rows + 1, 3 * chans, count * half), BF16)],
        compiler_params=pltpu.CompilerParams(vmem_limit_bytes=VMEM_LIMIT),
        cost_estimate=pl.CostEstimate(flops=8 * 10**9, bytes_accessed=10**7, transcendentals=0),
        name="layer_four",
    )(*thirds, weights, even_odd(width))


def exchange(plane, row, corner):
    count = lax.axis_size("sp")
    axes = ("sp", "fl")
    blocks = range(count)
    inner = [b for b in blocks if b % ROW_BLOCKS != ROW_BLOCKS - 1]
    down = [(2 * b, 2 * b + 1) for b in blocks]
    down += [(2 * b + 1, 2 * (b + ROW_BLOCKS)) for b in blocks if b + ROW_BLOCKS < count]
    along = [(2 * b + core, 2 * (b + 1) + core) for b in inner for core in range(2)]
    both = [(2 * b, 2 * (b + 1) + 1) for b in inner]
    both += [(2 * b + 1, 2 * (b + 1 + ROW_BLOCKS)) for b in inner if b + ROW_BLOCKS < count]
    return (
        lax.ppermute(plane, axes, down),
        lax.ppermute(row, axes, along),
        lax.ppermute(corner, axes, both),
    )


def both_cores(value, core):
    other = lax.ppermute(value, "fl", [(0, 1), (1, 0)])
    return jnp.where(core == 0, jnp.concatenate([value, other], 0), jnp.concatenate([other, value], 0))


def tap_major(kernel, chans):
    outs = kernel.shape[0]
    return jnp.transpose(kernel.reshape(outs, chans, 27), (0, 2, 1)).reshape(outs, 27 * chans)


def shards(volume, kernel_three, gain_three, shift_three, kernel_four, gain_four, shift_four):
    core = lax.axis_index("fl")
    chans = volume.shape[1]
    mid = 2 * kernel_three.shape[0]
    scales_three = both_cores(jnp.stack([gain_three, shift_three], 1), core)
    scales_four = both_cores(jnp.stack([gain_four, shift_four], 1), core)
    weights_three = tap_major(both_cores(kernel_three, core), chans)
    weights_four = tap_major(both_cores(kernel_four, core), mid)
    gain, shift = scales_three[:, :1], scales_three[:, 1:]
    index = core.reshape(1)
    halos = exchange(*three_edges(volume, weights_three, index))
    thirds = (*layer_three(volume, weights_three, gain, shift, index), *halos, gain, shift)
    halo_plane, halo_row, halo_corner = exchange(*four_edges(thirds, weights_four))
    total = layer_four(thirds, weights_four)
    out_rows, outs, lanes = total.shape
    width = halo_plane.shape[2]
    total = total.reshape(out_rows, outs, lanes // width, width)
    total = total.at[:, :, 0].add(halo_plane.astype(F32))
    total = total.at[0].add(halo_row.reshape(outs, lanes // width, width).astype(F32))
    total = total.at[0, :, 0].add(halo_corner.astype(F32))
    fourth = activate(total, scales_four[:, :1, None], scales_four[:, 1:, None]).astype(BF16)
    fourth = jnp.transpose(fourth, (1, 2, 0, 3))
    half = outs // 2
    own = lax.dynamic_slice_in_dim(fourth, core * half, half, 0)
    theirs = lax.dynamic_slice_in_dim(fourth, (1 - core) * half, half, 0)
    other = lax.ppermute(theirs, "fl", [(0, 1), (1, 0)])
    return jnp.where(core == 0, jnp.concatenate([own, other], 1), jnp.concatenate([other, own], 1))[None]


def solution(mesh):
    return jax.shard_map(
        shards,
        mesh=mesh,
        in_specs=(
            P("sp", None, None, None, None),
            P("fl", None),
            P("fl"),
            P("fl"),
            P("fl", None),
            P("fl"),
            P("fl"),
        ),
        out_specs=P("sp", "fl", None, None, None),
        check_vma=False,
    )
```

```python
import functools

import jax
import jax.numpy as jnp
import numpy as np
from jax import lax
from jax.experimental import pallas as pl
from jax.experimental.pallas import tpu as pltpu
from jax.sharding import PartitionSpec as P

F32 = jnp.float32
BF16 = jnp.bfloat16
LANES = 128
ROW_BLOCKS = 8
SUB = 8
TAPS = 27
GROUP = 16
VMEM_LIMIT = 56 * 2**20


def even_odd(width):
    half = width // 2
    place = np.zeros((width, width), np.float32)
    place[np.arange(0, width, 2), np.arange(half)] = 1
    place[np.arange(1, width, 2), half + np.arange(half)] = 1
    return jnp.asarray(place, BF16)


def activate(total, gain, shift):
    return jnp.maximum(total * gain + shift, 0.0)


def shifted(odd):
    lane = lax.broadcasted_iota(jnp.int32, odd.shape, 1)
    return jnp.where(lane == 0, 0.0, pltpu.roll(odd, 1, 1))


def spread(sides, place):
    quarter = place.shape[0] // 2
    split = [jnp.dot(side, place, preferred_element_type=F32) for side in sides]
    even = jnp.concatenate([part[:, :quarter] for part in split], 1)
    odd = jnp.concatenate([part[:, quarter:] for part in split], 1)
    return shifted(odd), even, odd


def separate(x_ref, plane, place_ref, split_refs, store):
    chans, rows, width = x_ref.shape[1], x_ref.shape[3], x_ref.shape[4]
    half = width // 2
    quarter = half // 2
    for index, first in enumerate(range(0, chans, GROUP)):
        split_ref = split_refs[index % len(split_refs)]
        x = x_ref[0, pl.ds(first, GROUP), plane]
        x = x.astype(F32).reshape(GROUP * rows, width).astype(BF16)
        for side in range(2):
            parts = jnp.dot(
                x[:, side * half : (side + 1) * half], place_ref[...], preferred_element_type=F32
            )
            for block in range(half // LANES):
                odd, at = divmod(block, quarter // LANES)
                split_ref[odd, side * (quarter // LANES) + at] = parts[:, block * LANES : (block + 1) * LANES]
        for row in range(rows):
            even, odd = (
                jnp.concatenate(
                    [split_ref[odd, at, pl.ds(row, GROUP, stride=rows), :] for at in range(half // LANES)], 1
                )
                for odd in range(2)
            )
            for tap, value in enumerate((shifted(odd), even, odd)):
                store(tap, row, first, value.astype(BF16))
        yield


def whole(own, other, core):
    first = jnp.where(core == 0, own, other)
    second = jnp.where(core == 0, other, own)
    return jnp.concatenate([first, second], 0)


def tap_major(kernel, turned_ref, w_ref, first):
    columns = kernel.shape[1]
    chans = columns // TAPS
    for at in range(0, columns, LANES):
        size = min(LANES, columns - at)
        turned_ref[at : at + size, :] = kernel[:, at : at + size].T
    for at in range(0, columns, LANES):
        size = min(LANES, columns - at)
        parts = [
            turned_ref[pl.ds(tap, chans, stride=TAPS), :] for tap in range(at // chans, (at + size) // chans)
        ]
        w_ref[first : first + LANES, at : at + size] = jnp.concatenate(parts, 0).T.astype(BF16)


def four_weights_kernel(core_ref, own_ref, other_ref, w_ref, *turned_refs):
    core = core_ref[0]
    for index, turned_ref in enumerate(turned_refs):
        kernel = jnp.where(core == index, own_ref[...].astype(F32), other_ref[...].astype(F32))
        tap_major(kernel, turned_ref, w_ref, index * LANES)


def four_weights(own, other, core):
    outs, columns = own.shape
    return pl.pallas_call(
        four_weights_kernel,
        out_shape=jax.ShapeDtypeStruct((2 * outs, columns), BF16),
        in_specs=[
            pl.BlockSpec(memory_space=pltpu.SMEM),
            pl.BlockSpec(memory_space=pltpu.VMEM),
            pl.BlockSpec(memory_space=pltpu.VMEM),
        ],
        scratch_shapes=[pltpu.VMEM((columns, LANES), F32)] * 2,
        compiler_params=pltpu.CompilerParams(vmem_limit_bytes=VMEM_LIMIT),
        cost_estimate=pl.CostEstimate(flops=10**6, bytes_accessed=4 * 10**6, transcendentals=0),
        name="four_weights",
    )(core, own, other)


def three_edges_kernel(
    core_ref, last_ref, rim_ref, own_ref, other_ref, own_scales_ref, other_scales_ref, place_ref,
    next_plane_ref, next_row_ref, next_corner_ref, w_ref, gain_ref, shift_ref, scales_ref,
    *scratch,
):
    *split_refs, turned_ref, pick_ref, data_ref = scratch
    core = core_ref[0]
    tap_major(whole(own_ref[...].astype(F32), other_ref[...].astype(F32), core), turned_ref, w_ref, 0)
    own_scales, other_scales = own_scales_ref[...], other_scales_ref[...]
    lines = own_scales.shape[0]
    scales = jnp.concatenate(
        [own_scales, other_scales, jnp.zeros((LANES - 2 * lines, LANES), F32)], 0
    ).T
    scales_ref[...] = scales
    share = own_ref.shape[0]
    for ref, at in ((gain_ref, 0), (shift_ref, share)):
        ref[...] = whole(scales[at : at + share, 0:1], scales[at : at + share, lines : lines + 1], core)
    chans, rows, width = last_ref.shape[1], last_ref.shape[3], last_ref.shape[4]
    planes = rim_ref.shape[2]
    half = width // 2
    out_rows = rows // 2
    taps = 3 * chans
    rim = (rows - 1) % SUB

    picked = []
    for plane in range(planes):
        x = rim_ref[0, :, plane, :SUB].astype(F32).reshape(chans * SUB, width)
        for at in range(width // LANES):
            pick_ref[plane % 2, at] = x[:, at * LANES : (at + 1) * LANES]
        picked.append(
            jnp.concatenate(
                [pick_ref[plane % 2, at, pl.ds(rim, chans, stride=SUB), :] for at in range(width // LANES)], 1
            ).astype(BF16)
        )
    picked = jnp.concatenate(picked, 0)
    parts = spread((picked[:, :half], picked[:, half:]), place_ref[...])
    parts = [part.astype(BF16) for part in parts]

    def rim_data(plane):
        return jnp.concatenate([part[plane * chans : (plane + 1) * chans] for part in parts], 0)

    none = jnp.zeros((taps, half), BF16)
    for step in range(planes // 2):
        pieces = []
        for plane in range(2 * step - 1, 2 * step + 2):
            pieces += [none if plane < 0 else rim_data(plane), none, none]
        total = jnp.dot(w_ref[...], jnp.concatenate(pieces, 0), preferred_element_type=F32)
        next_row_ref[step] = total.astype(BF16)

    def beyond(data):
        return jnp.dot(w_ref[:, : 3 * taps], data, preferred_element_type=F32).astype(BF16)

    next_corner_ref[...] = beyond(jnp.concatenate([rim_data(planes - 1), none, none], 0))

    def store(tap, row, first, value):
        data_ref[row + 1, tap * chans + first : tap * chans + first + GROUP, :] = value

    data_ref[0] = jnp.zeros_like(data_ref[0])
    for _ in separate(last_ref, 0, place_ref, split_refs, store):
        pass
    for row in range(out_rows):
        next_plane_ref[row] = beyond(data_ref[2 * row : 2 * row + 3].reshape(3 * taps, half))


def three_edges(volume, own, other, own_scales, other_scales, core):
    _, chans, planes, rows, width = volume.shape
    outs, columns = 2 * own.shape[0], own.shape[1]
    half = width // 2
    mine, out_rows = planes // 2, rows // 2
    full = lambda *shape: pl.BlockSpec(shape, lambda i, core: (0,) * len(shape))
    shapes = [
        ((out_rows, outs, half), BF16),
        ((mine // 2, outs, half), BF16),
        ((outs, half), BF16),
        ((outs, columns), BF16),
        ((outs, 1), F32),
        ((outs, 1), F32),
        ((LANES, LANES), F32),
    ]
    return pl.pallas_call(
        three_edges_kernel,
        grid_spec=pltpu.PrefetchScalarGridSpec(
            num_scalar_prefetch=1,
            grid=(1,),
            in_specs=[
                pl.BlockSpec((1, chans, 1, rows, width), lambda i, core: (0, 0, (core[0] + 1) * mine - 1, 0, 0)),
                pl.BlockSpec((1, chans, mine, 2 * SUB, width), lambda i, core: (0, 0, core[0], (rows - 1) // (2 * SUB), 0)),
                full(*own.shape),
                full(*other.shape),
                full(*own_scales.shape),
                full(*other_scales.shape),
                full(half, half),
            ],
            out_specs=[full(*shape) for shape, _ in shapes],
            scratch_shapes=[pltpu.VMEM((2, half // LANES, GROUP * rows, LANES), F32)] * 4
            + [
                pltpu.VMEM((columns, LANES), F32),
                pltpu.VMEM((2, width // LANES, chans * SUB, LANES), F32),
                pltpu.VMEM((rows + 1, 3 * chans, half), BF16),
            ],
        ),
        out_shape=[jax.ShapeDtypeStruct(*shape) for shape in shapes],
        compiler_params=pltpu.CompilerParams(vmem_limit_bytes=VMEM_LIMIT),
        cost_estimate=pl.CostEstimate(flops=2 * 10**9, bytes_accessed=8 * 10**6, transcendentals=0),
        name="three_edges",
    )(core, volume, volume, own, other, own_scales, other_scales, even_odd(half))


def three_kernel(
    core_ref, x_ref, w_ref, place_ref, gain_ref, shift_ref,
    third_ref, plane_ref, row_ref,
    *scratch,
):
    *split_refs, prior_ref, first_ref, second_ref, total_ref = scratch
    step, steps = pl.program_id(0), pl.num_programs(0) - 1
    chans, rows, width = x_ref.shape[1], x_ref.shape[3], x_ref.shape[4]
    half = width // 2
    out_rows = rows // 2
    taps = 3 * chans

    def splitting(pair_ref):
        for plane in range(2):

            def store(tap, row, first, value, plane=plane):
                pair_ref[plane, row + 1, tap * chans + first : tap * chans + first + GROUP, :] = value

            yield from separate(x_ref, plane, place_ref, split_refs, store)

    def summing(pair_ref):
        gain, shift = gain_ref[...], shift_ref[...]
        for row in range(out_rows):
            parts = [
                ref[2 * row : 2 * row + 3].reshape(3 * taps, half)
                for ref in (prior_ref, pair_ref.at[0], pair_ref.at[1])
            ]
            total = jnp.dot(w_ref[...], jnp.concatenate(parts, 0), preferred_element_type=F32)
            third_ref[0, row] = activate(total, gain, shift).astype(BF16)
            total_ref[row] = total
            yield
        row_ref[0] = total_ref[0]
        prior_ref[...] = pair_ref[1]
        yield

    @pl.when(step == 0)
    def _():
        prior_ref[...] = jnp.zeros_like(prior_ref)
        for ref in (first_ref, second_ref):
            ref[:, 0] = jnp.zeros_like(ref[:, 0])
        for _ in splitting(first_ref):
            pass

    def both(new_ref, old_ref):
        new, old = splitting(new_ref), summing(old_ref)
        for turn in range(2 * chans // GROUP):
            next(new, None)
            for _ in range(out_rows * (turn + 1) // (2 * chans // GROUP) - out_rows * turn // (2 * chans // GROUP)):
                next(old, None)
        for _ in new:
            pass
        for _ in old:
            pass

    for odd, (new_ref, old_ref) in enumerate(((first_ref, second_ref), (second_ref, first_ref))):

        @pl.when((step > 0) & (step < steps) & (step % 2 == odd))
        def _(new_ref=new_ref, old_ref=old_ref):
            both(new_ref, old_ref)

        @pl.when((step == steps) & (step % 2 == odd))
        def _(old_ref=old_ref):
            for _ in summing(old_ref):
                pass

    @pl.when(step == 1)
    def _():
        plane_ref[...] = total_ref[...]


def layer_three(volume, weights, gain, shift, core):
    _, chans, planes, rows, width = volume.shape
    outs = weights.shape[0]
    half = width // 2
    steps, out_rows = planes // 4, rows // 2
    full = lambda *shape: pl.BlockSpec(shape, lambda i, core: (0,) * len(shape))
    return pl.pallas_call(
        three_kernel,
        grid_spec=pltpu.PrefetchScalarGridSpec(
            num_scalar_prefetch=1,
            grid=(steps + 1,),
            in_specs=[
                pl.BlockSpec((1, chans, 2, rows, width), lambda i, core: (0, 0, core[0] * steps + jnp.minimum(i, steps - 1), 0, 0)),
                full(*weights.shape),
                full(half, half),
                full(outs, 1),
                full(outs, 1),
            ],
            out_specs=[
                pl.BlockSpec((1, out_rows, outs, half), lambda i, core: (jnp.maximum(i - 1, 0), 0, 0, 0)),
                full(out_rows, outs, half),
                pl.BlockSpec((1, outs, half), lambda i, core: (jnp.maximum(i - 1, 0), 0, 0)),
            ],
            scratch_shapes=[pltpu.VMEM((2, half // LANES, GROUP * rows, LANES), F32)] * 4
            + [
                pltpu.VMEM((rows + 1, 3 * chans, half), BF16),
                pltpu.VMEM((2, rows + 1, 3 * chans, half), BF16),
                pltpu.VMEM((2, rows + 1, 3 * chans, half), BF16),
                pltpu.VMEM((out_rows, outs, half), F32),
            ],
        ),
        out_shape=[
            jax.ShapeDtypeStruct((steps, out_rows, outs, half), BF16),
            jax.ShapeDtypeStruct((out_rows, outs, half), F32),
            jax.ShapeDtypeStruct((steps, outs, half), F32),
        ],
        compiler_params=pltpu.CompilerParams(vmem_limit_bytes=VMEM_LIMIT),
        cost_estimate=pl.CostEstimate(flops=10**10, bytes_accessed=2 * 10**7, transcendentals=0),
        name="layer_three",
    )(core, volume, weights, even_odd(half), gain, shift)


def third_value(refs, plane, row):
    third_ref, plane_ref, row_ref, halo_plane_ref, halo_row_ref, halo_corner_ref, gain_ref, shift_ref = refs
    if plane and row:
        return third_ref[plane, row]
    total = row_ref[plane] if plane else plane_ref[row] + halo_plane_ref[row].astype(F32)
    if not row:
        total = total + halo_row_ref[plane].astype(F32)
        if not plane:
            total = total + halo_corner_ref[...].astype(F32)
    return activate(total, gain_ref[...], shift_ref[...]).astype(BF16)


def four_edges_kernel(*refs):
    *thirds, w_ref, place_ref, next_plane_ref, next_row_ref, next_corner_ref = refs
    planes, rows, chans, width = thirds[0].shape
    half = width // 2
    out_rows, count = rows // 2, planes // 2
    taps = 3 * chans

    def data(spots):
        values = jnp.concatenate([third_value(thirds, *spot) for spot in spots], 0)
        parts = [part.astype(BF16) for part in spread((values,), place_ref[...])]
        return [
            jnp.concatenate([part[at * chans : (at + 1) * chans] for part in parts], 0) for at in range(len(spots))
        ]

    none = jnp.zeros((taps, half), BF16)
    rim = data([(plane, rows - 1) for plane in range(planes)])
    last = [none] + data([(planes - 1, row) for row in range(rows - 1)]) + [rim[planes - 1]]

    def beyond(pieces):
        return jnp.dot(w_ref[:, : 3 * taps], pieces, preferred_element_type=F32).astype(BF16)

    for row in range(0, out_rows, 2):
        pieces = [jnp.concatenate([last[2 * row + at], last[2 * row + 2 + at]], 1) for at in range(3)]
        both = beyond(jnp.concatenate(pieces, 0))
        next_plane_ref[row] = both[:, :half]
        next_plane_ref[row + 1] = both[:, half:]
    empty = jnp.zeros((taps, count * half), BF16)
    pieces = []
    for slot in range(3):
        pieces.append(
            jnp.concatenate([rim[2 * m + slot - 1] if 2 * m + slot else none for m in range(count)], 1)
        )
        pieces += [empty, empty]
    next_row_ref[...] = jnp.dot(
        w_ref[...], jnp.concatenate(pieces, 0), preferred_element_type=F32
    ).astype(BF16)
    next_corner_ref[...] = beyond(jnp.concatenate([rim[planes - 1], none, none], 0))


def four_edges(thirds, weights):
    planes, rows, chans, width = thirds[0].shape
    outs = weights.shape[0]
    half = width // 2
    return pl.pallas_call(
        four_edges_kernel,
        out_shape=[
            jax.ShapeDtypeStruct((rows // 2, outs, half), BF16),
            jax.ShapeDtypeStruct((outs, planes // 2 * half), BF16),
            jax.ShapeDtypeStruct((outs, half), BF16),
        ],
        compiler_params=pltpu.CompilerParams(vmem_limit_bytes=VMEM_LIMIT),
        cost_estimate=pl.CostEstimate(flops=2 * 10**9, bytes_accessed=8 * 10**6, transcendentals=0),
        name="four_edges",
    )(*thirds, weights, even_odd(width))


def four_kernel(*refs):
    *thirds, w_ref, place_ref, sums_ref, data_ref = refs
    planes, rows, chans, width = thirds[0].shape
    half = width // 2
    out_rows, count = rows // 2, planes // 2
    taps = 3 * chans
    data_ref[:, 0] = jnp.zeros_like(data_ref[:, 0])
    data_ref[0, :, :, :half] = jnp.zeros_like(data_ref[0, :, :, :half])
    batch = 4
    for plane in range(planes):
        spots = [(1 + plane % 2, plane // 2)]
        if plane % 2 and plane // 2 + 1 < count:
            spots.append((0, plane // 2 + 1))
        for first in range(0, rows, batch):
            values = jnp.concatenate([third_value(thirds, plane, row) for row in range(first, first + batch)], 0)
            for tap, part in enumerate(spread((values,), place_ref[...])):
                part = part.astype(BF16)
                for at in range(batch):
                    for slot, lanes in spots:
                        data_ref[
                            slot, first + at + 1, tap * chans : (tap + 1) * chans, lanes * half : (lanes + 1) * half
                        ] = part[at * chans : (at + 1) * chans]
    for row in range(out_rows):
        parts = [data_ref[slot, 2 * row : 2 * row + 3].reshape(3 * taps, count * half) for slot in range(3)]
        sums_ref[row] = jnp.dot(w_ref[...], jnp.concatenate(parts, 0), preferred_element_type=F32)


def layer_four(thirds, weights):
    planes, rows, chans, width = thirds[0].shape
    outs = weights.shape[0]
    half = width // 2
    out_rows, count = rows // 2, planes // 2
    return pl.pallas_call(
        four_kernel,
        out_shape=jax.ShapeDtypeStruct((out_rows, outs, count * half), F32),
        scratch_shapes=[pltpu.VMEM((3, rows + 1, 3 * chans, count * half), BF16)],
        compiler_params=pltpu.CompilerParams(vmem_limit_bytes=VMEM_LIMIT),
        cost_estimate=pl.CostEstimate(flops=8 * 10**9, bytes_accessed=10**7, transcendentals=0),
        name="layer_four",
    )(*thirds, weights, even_odd(width))


def finished(refs, row, first):
    sums_ref, halo_plane_ref, halo_row_ref, halo_corner_ref, gain, shift = refs
    chans = pl.ds(pl.multiple_of(first, LANES), LANES)
    width = halo_plane_ref.shape[2]
    total = sums_ref[row, chans]
    edge = halo_plane_ref[row, chans].astype(F32)
    if not row:
        total = total + halo_row_ref[chans].astype(F32)
        edge = edge + halo_corner_ref[chans].astype(F32)
    total = jnp.concatenate([total[:, :width] + edge, total[:, width:]], 1)
    return activate(total, gain, shift)


def theirs_kernel(core_ref, sums_ref, halo_plane_ref, halo_row_ref, halo_corner_ref, scales_ref, theirs_ref):
    refs = sums_ref, halo_plane_ref, halo_row_ref, halo_corner_ref, scales_ref[:, 4:5], scales_ref[:, 5:6]
    for row in range(sums_ref.shape[0]):
        theirs_ref[row] = finished(refs, row, (1 - core_ref[0]) * LANES).astype(BF16)


def assemble_kernel(
    core_ref, sums_ref, halo_plane_ref, halo_row_ref, halo_corner_ref, scales_ref, got_ref, out_ref, lines_ref
):
    core = core_ref[0]
    refs = sums_ref, halo_plane_ref, halo_row_ref, halo_corner_ref, scales_ref[:, 1:2], scales_ref[:, 2:3]
    rows, _, width = halo_plane_ref.shape
    count = sums_ref.shape[2] // width
    for row in range(rows):
        own, got = finished(refs, row, core * LANES), got_ref[row].astype(F32)
        for at, value in enumerate((jnp.where(core == 0, own, got), jnp.where(core == 0, got, own))):
            for m in range(count):
                place = row * 2 * count + at * count + m
                lines_ref[pl.ds(place, LANES, stride=rows * 2 * count), :] = value[:, m * width : (m + 1) * width]
    out_ref[...] = lines_ref[...].astype(BF16)


def last_stage(core, sums, halos, scales):
    rows, outs, lanes = sums.shape
    in_specs = [pl.BlockSpec(memory_space=pltpu.SMEM)] + [pl.BlockSpec(memory_space=pltpu.VMEM)] * 5
    params = pltpu.CompilerParams(vmem_limit_bytes=VMEM_LIMIT)
    theirs = pl.pallas_call(
        theirs_kernel,
        out_shape=jax.ShapeDtypeStruct((rows, outs // 2, lanes), BF16),
        in_specs=in_specs,
        compiler_params=params,
        name="theirs",
    )(core, sums, *halos, scales)
    got = lax.ppermute(theirs, "fl", [(0, 1), (1, 0)])
    lines = (outs // 2 * rows * lanes * 2 // LANES, LANES)
    return pl.pallas_call(
        assemble_kernel,
        out_shape=jax.ShapeDtypeStruct(lines, BF16),
        in_specs=in_specs + [pl.BlockSpec(memory_space=pltpu.VMEM)],
        scratch_shapes=[pltpu.VMEM(lines, F32)],
        compiler_params=params,
        name="assemble",
    )(core, sums, *halos, scales, got)


def exchange(plane, row, corner):
    count = lax.axis_size("sp")
    axes = ("sp", "fl")
    blocks = range(count)
    inner = [b for b in blocks if b % ROW_BLOCKS != ROW_BLOCKS - 1]
    down = [(2 * b, 2 * b + 1) for b in blocks]
    down += [(2 * b + 1, 2 * (b + ROW_BLOCKS)) for b in blocks if b + ROW_BLOCKS < count]
    along = [(2 * b + core, 2 * (b + 1) + core) for b in inner for core in range(2)]
    both = [(2 * b, 2 * (b + 1) + 1) for b in inner]
    both += [(2 * b + 1, 2 * (b + 1 + ROW_BLOCKS)) for b in inner if b + ROW_BLOCKS < count]
    return (
        lax.ppermute(plane, axes, down),
        lax.ppermute(row, axes, along),
        lax.ppermute(corner, axes, both),
    )


def swapped(value):
    return lax.ppermute(value, "fl", [(0, 1), (1, 0)])


def shards(volume, kernel_three, gain_three, shift_three, kernel_four, gain_four, shift_four):
    core = lax.axis_index("fl").reshape(1)
    own_scales = jnp.concatenate([gain_three, shift_three, gain_four, shift_four]).reshape(-1, LANES)
    *nexts, weights_three, gain, shift, scales = three_edges(
        volume, kernel_three, swapped(kernel_three), own_scales, swapped(own_scales), core
    )
    halos = exchange(*nexts)
    thirds = (*layer_three(volume, weights_three, gain, shift, core), *halos, gain, shift)
    weights_four = four_weights(kernel_four, swapped(kernel_four), core)
    halos = exchange(*four_edges(thirds, weights_four))
    sums = layer_four(thirds, weights_four)
    lines = last_stage(core, sums, halos, scales)
    out_rows, outs, lanes = sums.shape
    fourth = lines.reshape(outs // 2, out_rows, 2 * lanes // LANES, LANES)
    return jnp.transpose(fourth, (0, 2, 1, 3))[None]


def solution(mesh):
    return jax.shard_map(
        shards,
        mesh=mesh,
        in_specs=(
            P("sp", None, None, None, None),
            P("fl", None),
            P("fl"),
            P("fl"),
            P("fl", None),
            P("fl"),
            P("fl"),
        ),
        out_specs=P("sp", "fl", None, None, None),
        check_vma=False,
    )
```

```python
import functools

import jax
import jax.numpy as jnp
import numpy as np
from jax import lax
from jax.experimental import pallas as pl
from jax.experimental.pallas import tpu as pltpu
from jax.sharding import PartitionSpec as P

F32 = jnp.float32
BF16 = jnp.bfloat16
LANES = 128
ROW_BLOCKS = 8
SUB = 8
TAPS = 27
RIM_TAPS = tuple(9 * a + e for a in range(3) for e in range(3))
GROUP = 16
VMEM_LIMIT = 56 * 2**20


def even_odd(width):
    half = width // 2
    place = np.zeros((width, width), np.float32)
    place[np.arange(0, width, 2), np.arange(half)] = 1
    place[np.arange(1, width, 2), half + np.arange(half)] = 1
    return jnp.asarray(place, BF16)


def activate(total, gain, shift):
    return jnp.maximum(total * gain + shift, 0.0)


def shifted(odd):
    lane = lax.broadcasted_iota(jnp.int32, odd.shape, 1)
    return jnp.where(lane == 0, 0.0, pltpu.roll(odd, 1, 1))


def spread(sides, place):
    quarter = place.shape[0] // 2
    split = [jnp.dot(side, place, preferred_element_type=F32) for side in sides]
    even = jnp.concatenate([part[:, :quarter] for part in split], 1)
    odd = jnp.concatenate([part[:, quarter:] for part in split], 1)
    return shifted(odd), even, odd


def separate(x_ref, plane, place_ref, split_refs, store):
    chans, rows, width = x_ref.shape[1], x_ref.shape[3], x_ref.shape[4]
    half = width // 2
    quarter = half // 2
    for index, first in enumerate(range(0, chans, GROUP)):
        split_ref = split_refs[index % len(split_refs)]
        x = x_ref[0, pl.ds(first, GROUP), plane]
        x = x.astype(F32).reshape(GROUP * rows, width).astype(BF16)
        for side in range(2):
            parts = jnp.dot(
                x[:, side * half : (side + 1) * half], place_ref[...], preferred_element_type=F32
            )
            for block in range(half // LANES):
                odd, at = divmod(block, quarter // LANES)
                split_ref[odd, side * (quarter // LANES) + at] = parts[:, block * LANES : (block + 1) * LANES]
        for row in range(rows):
            even, odd = (
                jnp.concatenate(
                    [split_ref[odd, at, pl.ds(row, GROUP, stride=rows), :] for at in range(half // LANES)], 1
                )
                for odd in range(2)
            )
            for tap, value in enumerate((shifted(odd), even, odd)):
                store(tap, row, first, value.astype(BF16))
        yield


def whole(own, other, core):
    first = jnp.where(core == 0, own, other)
    second = jnp.where(core == 0, other, own)
    return jnp.concatenate([first, second], 0)


def turn(kernel, turned_ref):
    columns = kernel.shape[1]
    for at in range(0, columns, LANES):
        size = min(LANES, columns - at)
        turned_ref[at : at + size, :] = kernel[:, at : at + size].T


def tap_major(turned_ref, taps, w_ref, first):
    chans = turned_ref.shape[0] // TAPS
    at = 0
    for index in range(0, len(taps), LANES // chans):
        parts = [turned_ref[pl.ds(tap, chans, stride=TAPS), :] for tap in taps[index : index + LANES // chans]]
        block = jnp.concatenate(parts, 0).T.astype(BF16)
        w_ref[first : first + LANES, at : at + block.shape[1]] = block
        at += block.shape[1]


def four_weights_kernel(core_ref, own_ref, other_ref, w_ref, *turned_refs):
    core = core_ref[0]
    for index, turned_ref in enumerate(turned_refs):
        turn(jnp.where(core == index, own_ref[...].astype(F32), other_ref[...].astype(F32)), turned_ref)
        tap_major(turned_ref, range(TAPS), w_ref, index * LANES)


def four_weights(own, other, core):
    outs, columns = own.shape
    return pl.pallas_call(
        four_weights_kernel,
        out_shape=jax.ShapeDtypeStruct((2 * outs, columns), BF16),
        in_specs=[
            pl.BlockSpec(memory_space=pltpu.SMEM),
            pl.BlockSpec(memory_space=pltpu.VMEM),
            pl.BlockSpec(memory_space=pltpu.VMEM),
        ],
        scratch_shapes=[pltpu.VMEM((columns, LANES), F32)] * 2,
        compiler_params=pltpu.CompilerParams(vmem_limit_bytes=VMEM_LIMIT),
        cost_estimate=pl.CostEstimate(flops=10**6, bytes_accessed=4 * 10**6, transcendentals=0),
        name="four_weights",
    )(core, own, other)


def three_edges_kernel(
    core_ref, last_ref, rim_ref, own_ref, other_ref, own_scales_ref, other_scales_ref, place_ref,
    message_ref, w_ref, gain_ref, shift_ref, scales_ref,
    *scratch,
):
    *split_refs, turned_ref, pick_ref, data_ref, rims_ref, rim_w_ref = scratch
    core, step, last = core_ref[0], pl.program_id(0), pl.num_programs(0) - 1
    chans, rows, width = last_ref.shape[1], last_ref.shape[3], last_ref.shape[4]
    block, planes = rim_ref.shape[2], rims_ref.shape[0]
    half = width // 2
    out_rows = rows // 2
    taps = 3 * chans
    rim = (rows - 1) % SUB

    @pl.when(step == 0)
    def _():
        turn(whole(own_ref[...].astype(F32), other_ref[...].astype(F32), core), turned_ref)
        tap_major(turned_ref, range(TAPS), w_ref, 0)
        tap_major(turned_ref, RIM_TAPS, rim_w_ref, 0)
        own_scales, other_scales = own_scales_ref[...], other_scales_ref[...]
        lines = own_scales.shape[0]
        scales = jnp.concatenate(
            [own_scales, other_scales, jnp.zeros((LANES - 2 * lines, LANES), F32)], 0
        ).T
        scales_ref[...] = scales
        share = own_ref.shape[0]
        for ref, at in ((gain_ref, 0), (shift_ref, share)):
            ref[...] = whole(scales[at : at + share, 0:1], scales[at : at + share, lines : lines + 1], core)

    def picked(spots):
        values, held = [], None
        for plane, row in spots:
            if plane != held:
                x = rim_ref[0, :, plane, :SUB].astype(F32).reshape(chans * SUB, width)
                for at in range(width // LANES):
                    pick_ref[plane % 2, at] = x[:, at * LANES : (at + 1) * LANES]
                held = plane
            values.append(
                jnp.concatenate(
                    [pick_ref[plane % 2, at, pl.ds(row, chans, stride=SUB), :] for at in range(width // LANES)], 1
                ).astype(BF16)
            )
        values = jnp.concatenate(values, 0)
        parts = [part.astype(BF16) for part in spread((values[:, :half], values[:, half:]), place_ref[...])]
        return [
            jnp.concatenate([part[at * chans : (at + 1) * chans] for part in parts], 0) for at in range(len(spots))
        ]

    @pl.when(core == 0)
    def _():
        for plane, data in enumerate(picked([(plane, rim) for plane in range(block)])):
            rims_ref[step * block + plane] = data

    @pl.when((core == 0) & (step == last))
    def _():
        none = jnp.zeros((taps, half), BF16)
        for index in range(planes // 2 + 1):
            pieces = [
                rims_ref[plane] if 0 <= plane < planes else none for plane in range(2 * index - 1, 2 * index + 2)
            ]
            total = jnp.dot(rim_w_ref[...], jnp.concatenate(pieces, 0), preferred_element_type=F32)
            message_ref[index] = total.astype(BF16)
        spots = [(plane, row) for plane in range(block - 3, block) for row in range(rim - 2, rim + 1)]
        total = jnp.dot(w_ref[...], jnp.concatenate(picked(spots), 0), preferred_element_type=F32)
        message_ref[planes // 2 + 1] = activate(total, gain_ref[...], shift_ref[...]).astype(BF16)
        for index in range(planes // 2 + 2, message_ref.shape[0]):
            message_ref[index] = jnp.zeros_like(message_ref[index])

    @pl.when((core == 1) & (step == 0))
    def _():
        def store(tap, row, first, value):
            data_ref[row + 1, tap * chans + first : tap * chans + first + GROUP, :] = value

        data_ref[0] = jnp.zeros_like(data_ref[0])
        for _ in separate(last_ref, 0, place_ref, split_refs, store):
            pass
        for row in range(out_rows):
            total = jnp.dot(
                w_ref[:, : 3 * taps],
                data_ref[2 * row : 2 * row + 3].reshape(3 * taps, half),
                preferred_element_type=F32,
            )
            message_ref[row] = total.astype(BF16)


def three_edges(volume, own, other, own_scales, other_scales, core):
    _, chans, planes, rows, width = volume.shape
    outs, columns = 2 * own.shape[0], own.shape[1]
    half = width // 2
    block, steps, out_rows = 4, planes // 4, rows // 2
    full = lambda *shape: pl.BlockSpec(shape, lambda i, core: (0,) * len(shape))
    shapes = [
        ((out_rows, outs, half), BF16),
        ((outs, columns), BF16),
        ((outs, 1), F32),
        ((outs, 1), F32),
        ((LANES, LANES), F32),
    ]
    return pl.pallas_call(
        three_edges_kernel,
        grid_spec=pltpu.PrefetchScalarGridSpec(
            num_scalar_prefetch=1,
            grid=(steps,),
            in_specs=[
                pl.BlockSpec((1, chans, 1, rows, width), lambda i, core: (0, 0, planes - 1, 0, 0)),
                pl.BlockSpec(
                    (1, chans, block, 2 * SUB, width),
                    lambda i, core: (0, 0, i + core[0] * (steps - 1 - i), (rows - 1) // (2 * SUB), 0),
                ),
                full(*own.shape),
                full(*other.shape),
                full(*own_scales.shape),
                full(*other_scales.shape),
                full(half, half),
            ],
            out_specs=[full(*shape) for shape, _ in shapes],
            scratch_shapes=[pltpu.VMEM((2, half // LANES, GROUP * rows, LANES), F32)] * 4
            + [
                pltpu.VMEM((columns, LANES), F32),
                pltpu.VMEM((2, width // LANES, chans * SUB, LANES), F32),
                pltpu.VMEM((rows + 1, 3 * chans, half), BF16),
                pltpu.VMEM((planes, 3 * chans, half), BF16),
                pltpu.VMEM((outs, columns // 3), BF16),
            ],
        ),
        out_shape=[jax.ShapeDtypeStruct(*shape) for shape in shapes],
        compiler_params=pltpu.CompilerParams(vmem_limit_bytes=VMEM_LIMIT),
        cost_estimate=pl.CostEstimate(flops=2 * 10**9, bytes_accessed=8 * 10**6, transcendentals=0),
        name="three_edges",
    )(core, volume, volume, own, other, own_scales, other_scales, even_odd(half))


def three_kernel(
    core_ref, x_ref, before_ref, w_ref, place_ref, gain_ref, shift_ref,
    third_ref, plane_ref, row_ref, last_row_ref, local_ref,
    *scratch,
):
    *split_refs, prior_ref, first_ref, second_ref, total_ref = scratch
    core, step, steps = core_ref[0], pl.program_id(0), pl.num_programs(0) - 1
    chans, rows, width = x_ref.shape[1], x_ref.shape[3], x_ref.shape[4]
    half = width // 2
    out_rows = rows // 2
    taps = 3 * chans

    def splitting(pair_ref):
        for plane in range(2):

            def store(tap, row, first, value, plane=plane):
                pair_ref[plane, row + 1, tap * chans + first : tap * chans + first + GROUP, :] = value

            yield from separate(x_ref, plane, place_ref, split_refs, store)

    def summing(pair_ref):
        gain, shift = gain_ref[...], shift_ref[...]
        for row in range(out_rows):
            parts = [
                ref[2 * row : 2 * row + 3].reshape(3 * taps, half)
                for ref in (prior_ref, pair_ref.at[0], pair_ref.at[1])
            ]
            total = jnp.dot(w_ref[...], jnp.concatenate(parts, 0), preferred_element_type=F32)
            third_ref[0, row] = activate(total, gain, shift).astype(BF16)
            total_ref[row] = total
            yield
        row_ref[0] = total_ref[0]
        prior_ref[...] = pair_ref[1]
        yield

    @pl.when(step == 0)
    def _():
        prior_ref[...] = jnp.zeros_like(prior_ref)

        @pl.when(core == 1)
        def _():
            def store(tap, row, first, value):
                prior_ref[row + 1, tap * chans + first : tap * chans + first + GROUP, :] = value

            for _ in separate(before_ref, 0, place_ref, split_refs, store):
                pass

        for ref in (first_ref, second_ref):
            ref[:, 0] = jnp.zeros_like(ref[:, 0])
        for _ in splitting(first_ref):
            pass

    def both(new_ref, old_ref):
        new, old = splitting(new_ref), summing(old_ref)
        for turn in range(2 * chans // GROUP):
            next(new, None)
            for _ in range(out_rows * (turn + 1) // (2 * chans // GROUP) - out_rows * turn // (2 * chans // GROUP)):
                next(old, None)
        for _ in new:
            pass
        for _ in old:
            pass

    for odd, (new_ref, old_ref) in enumerate(((first_ref, second_ref), (second_ref, first_ref))):

        @pl.when((step > 0) & (step < steps) & (step % 2 == odd))
        def _(new_ref=new_ref, old_ref=old_ref):
            both(new_ref, old_ref)

        @pl.when((step == steps) & (step % 2 == odd))
        def _(old_ref=old_ref):
            for _ in summing(old_ref):
                pass

    @pl.when(step == 1)
    def _():
        plane_ref[...] = total_ref[...]

    @pl.when((step > 0) & (core == 1))
    def _():
        local_ref[step - 1] = third_ref[0, out_rows - 1]

    @pl.when((step == steps) & (core == 0))
    def _():
        local_ref[...] = third_ref[0]
        last_row_ref[...] = total_ref[0]


def layer_three(volume, weights, gain, shift, core):
    _, chans, planes, rows, width = volume.shape
    outs = weights.shape[0]
    half = width // 2
    steps, out_rows = planes // 4, rows // 2
    full = lambda *shape: pl.BlockSpec(shape, lambda i, core: (0,) * len(shape))
    return pl.pallas_call(
        three_kernel,
        grid_spec=pltpu.PrefetchScalarGridSpec(
            num_scalar_prefetch=1,
            grid=(steps + 1,),
            in_specs=[
                pl.BlockSpec((1, chans, 2, rows, width), lambda i, core: (0, 0, core[0] * steps + jnp.minimum(i, steps - 1), 0, 0)),
                pl.BlockSpec(
                    (1, chans, 1, rows, width),
                    lambda i, core: (0, 0, jnp.maximum(core[0] * 2 * steps - 1, 0), 0, 0),
                ),
                full(*weights.shape),
                full(half, half),
                full(outs, 1),
                full(outs, 1),
            ],
            out_specs=[
                pl.BlockSpec((1, out_rows, outs, half), lambda i, core: (jnp.maximum(i - 1, 0), 0, 0, 0)),
                full(out_rows, outs, half),
                pl.BlockSpec((1, outs, half), lambda i, core: (jnp.maximum(i - 1, 0), 0, 0)),
                full(outs, half),
                full(out_rows, outs, half),
            ],
            scratch_shapes=[pltpu.VMEM((2, half // LANES, GROUP * rows, LANES), F32)] * 4
            + [
                pltpu.VMEM((rows + 1, 3 * chans, half), BF16),
                pltpu.VMEM((2, rows + 1, 3 * chans, half), BF16),
                pltpu.VMEM((2, rows + 1, 3 * chans, half), BF16),
                pltpu.VMEM((out_rows, outs, half), F32),
            ],
        ),
        out_shape=[
            jax.ShapeDtypeStruct((steps, out_rows, outs, half), BF16),
            jax.ShapeDtypeStruct((out_rows, outs, half), F32),
            jax.ShapeDtypeStruct((steps, outs, half), F32),
            jax.ShapeDtypeStruct((outs, half), F32),
            jax.ShapeDtypeStruct((out_rows, outs, half), BF16),
        ],
        compiler_params=pltpu.CompilerParams(vmem_limit_bytes=VMEM_LIMIT),
        cost_estimate=pl.CostEstimate(flops=10**10, bytes_accessed=2 * 10**7, transcendentals=0),
        name="layer_three",
    )(core, volume, volume, weights, even_odd(half), gain, shift)


def corner_total(core, refs):
    _, plane_ref, _, halo_ref, rows_ref, _, _ = refs
    planes = rows_ref.shape[0]
    first = jnp.where(core == 0, rows_ref[0].astype(F32), halo_ref[planes].astype(F32))
    return plane_ref[0] + jnp.where(core == 0, halo_ref[0].astype(F32), 0.0) + first


def third_value(core, refs, plane, row):
    third_ref, plane_ref, row_ref, halo_ref, rows_ref, gain_ref, shift_ref = refs
    planes = rows_ref.shape[0]
    if plane and row:
        return third_ref[plane, row]
    if plane:
        share = jnp.where(core == 0, rows_ref[plane].astype(F32), halo_ref[planes + plane].astype(F32))
        total = row_ref[plane] + share
    elif row:
        total = plane_ref[row] + jnp.where(core == 0, halo_ref[row].astype(F32), 0.0)
    else:
        total = corner_total(core, refs)
    value = activate(total, gain_ref[...], shift_ref[...])
    if not plane and not row:
        value = jnp.where(core == 0, 0.0, value)
    return value.astype(BF16)


def four_edges_kernel(core_ref, *refs):
    *thirds, local_ref, w_ref, place_ref, message_ref, mid_ref = refs
    core = core_ref[0]
    planes, rows, chans, width = thirds[0].shape
    half = width // 2
    out_rows = rows // 2
    taps = 3 * chans
    mid_ref[...] = w_ref[:, 4 * taps : 5 * taps]

    def data(values):
        parts = [part.astype(BF16) for part in spread((jnp.concatenate(values, 0),), place_ref[...])]
        return [
            jnp.concatenate([part[at * chans : (at + 1) * chans] for part in parts], 0) for at in range(len(values))
        ]

    @pl.when(core == 0)
    def _():
        none = jnp.zeros((taps, half), BF16)
        rim = [none] + data(
            [third_value(core, thirds, plane, rows - 1) for plane in range(planes)]
            + [local_ref[plane] for plane in range(planes)]
        )
        pieces = [jnp.concatenate([rim[2 * m + slot] for m in range(planes)], 1) for slot in range(3)]
        weights = jnp.concatenate([w_ref[:, 3 * slot * taps : (3 * slot + 1) * taps] for slot in range(3)], 1)
        total = jnp.dot(weights, jnp.concatenate(pieces, 0), preferred_element_type=F32).astype(BF16)
        for m in range(planes):
            message_ref[m] = total[:, m * half : (m + 1) * half]
        for index in range(planes, message_ref.shape[0]):
            message_ref[index] = jnp.zeros_like(message_ref[index])

    @pl.when(core == 1)
    def _():
        halo_ref = thirds[3]
        last = data(
            [halo_ref[2 * planes + 1]] + [third_value(core, thirds, planes - 1, row) for row in range(rows)]
        )
        for row in range(0, out_rows, 2):
            pieces = [jnp.concatenate([last[2 * row + at], last[2 * row + 2 + at]], 1) for at in range(3)]
            both = jnp.dot(w_ref[:, : 3 * taps], jnp.concatenate(pieces, 0), preferred_element_type=F32)
            both = both.astype(BF16)
            message_ref[row] = both[:, :half]
            message_ref[row + 1] = both[:, half:]
        corner = halo_ref[2 * planes]
        message_ref[out_rows, :chans] = corner[:, :half]
        message_ref[out_rows, chans:] = corner[:, half:]


def inputs(count):
    return [pl.BlockSpec(memory_space=pltpu.SMEM)] + [pl.BlockSpec(memory_space=pltpu.VMEM)] * count


def four_edges(core, thirds, local, weights):
    planes, rows, chans, width = thirds[0].shape
    outs = weights.shape[0]
    half = width // 2
    return pl.pallas_call(
        four_edges_kernel,
        out_shape=[
            jax.ShapeDtypeStruct((rows // 2 + 1, outs, half), BF16),
            jax.ShapeDtypeStruct((outs, 3 * chans), BF16),
        ],
        in_specs=inputs(len(thirds) + 3),
        compiler_params=pltpu.CompilerParams(vmem_limit_bytes=VMEM_LIMIT),
        cost_estimate=pl.CostEstimate(flops=2 * 10**9, bytes_accessed=8 * 10**6, transcendentals=0),
        name="four_edges",
    )(core, *thirds, local, weights, even_odd(width))


def four_kernel(core_ref, *refs):
    *thirds, local_ref, last_row_ref, w_ref, place_ref, sums_ref, data_ref = refs
    core = core_ref[0]
    planes, rows, chans, width = thirds[0].shape
    halo_ref, gain_ref, shift_ref = thirds[3], thirds[5], thirds[6]
    half = width // 2
    out_rows, count = rows // 2, planes // 2
    taps = 3 * chans
    batch = 4
    data_ref[:, 0] = jnp.zeros_like(data_ref[:, 0])

    def put(values, first, spots):
        for tap, part in enumerate(spread((jnp.concatenate(values, 0),), place_ref[...])):
            part = part.astype(BF16)
            for at in range(len(values)):
                for slot, lanes in spots:
                    data_ref[
                        slot, first + at + 1, tap * chans : (tap + 1) * chans, lanes * half : (lanes + 1) * half
                    ] = part[at * chans : (at + 1) * chans]

    @pl.when(core == 0)
    def _():
        data_ref[0, :, :, :half] = jnp.zeros_like(data_ref[0, :, :, :half])

    @pl.when(core == 1)
    def _():
        total = last_row_ref[...] + halo_ref[planes - 1].astype(F32)
        prior = [activate(total, gain_ref[...], shift_ref[...]).astype(BF16)]
        prior += [local_ref[row] for row in range(1, rows)]
        for first in range(0, rows, batch):
            put(prior[first : first + batch], first, [(0, 0)])

    for plane in range(planes):
        spots = [(1 + plane % 2, plane // 2)]
        if plane % 2 and plane // 2 + 1 < count:
            spots.append((0, plane // 2 + 1))
        for first in range(0, rows, batch):
            put([third_value(core, thirds, plane, row) for row in range(first, first + batch)], first, spots)
    for row in range(out_rows):
        parts = [data_ref[slot, 2 * row : 2 * row + 3].reshape(3 * taps, count * half) for slot in range(3)]
        sums_ref[row] = jnp.dot(w_ref[...], jnp.concatenate(parts, 0), preferred_element_type=F32)


def layer_four(core, thirds, local, last_row, weights):
    planes, rows, chans, width = thirds[0].shape
    outs = weights.shape[0]
    half = width // 2
    out_rows, count = rows // 2, planes // 2
    return pl.pallas_call(
        four_kernel,
        out_shape=jax.ShapeDtypeStruct((out_rows, outs, count * half), F32),
        in_specs=inputs(len(thirds) + 4),
        scratch_shapes=[pltpu.VMEM((3, rows + 1, 3 * chans, count * half), BF16)],
        compiler_params=pltpu.CompilerParams(vmem_limit_bytes=VMEM_LIMIT),
        cost_estimate=pl.CostEstimate(flops=8 * 10**9, bytes_accessed=10**7, transcendentals=0),
        name="layer_four",
    )(core, *thirds, local, last_row, weights, even_odd(width))


def theirs_kernel(
    core_ref, sums_ref, halo_ref, mid_ref, place_ref,
    third_ref, plane_ref, row_ref, three_halo_ref, rows_ref, gain_ref, shift_ref,
    theirs_ref, fix_ref,
):
    core = core_ref[0]
    thirds = third_ref, plane_ref, row_ref, three_halo_ref, rows_ref, gain_ref, shift_ref
    rows, width = halo_ref.shape[0] - 1, halo_ref.shape[2]

    @pl.when(core == 0)
    def _():
        corner = halo_ref[rows].astype(F32)
        total = corner_total(core, thirds) + jnp.concatenate([corner[:LANES], corner[LANES:]], 1)
        value = activate(total, gain_ref[...], shift_ref[...]).astype(BF16)
        data = jnp.concatenate([part.astype(BF16) for part in spread((value,), place_ref[...])], 0)
        fix = jnp.dot(mid_ref[...], data, preferred_element_type=F32)
        fix_ref[...] = fix[:LANES]
        for row in range(rows):
            total = sums_ref[row, LANES:]
            edge = halo_ref[row, LANES:].astype(F32)
            if not row:
                edge = edge + fix[LANES:]
            theirs_ref[row] = jnp.concatenate([total[:, :width] + edge, total[:, width:]], 1)
        theirs_ref[rows] = jnp.zeros_like(theirs_ref[rows])

    @pl.when(core == 1)
    def _():
        count = sums_ref.shape[2] // width
        fix_ref[...] = jnp.zeros_like(fix_ref)
        for row in range(rows):
            total = sums_ref[row, :LANES]
            if not row:
                total = total + jnp.concatenate([halo_ref[count + m, :LANES].astype(F32) for m in range(count)], 1)
            theirs_ref[row] = total
        theirs_ref[rows] = jnp.concatenate([halo_ref[m, :LANES].astype(F32) for m in range(count)], 1)


def assemble_kernel(core_ref, sums_ref, halo_ref, fix_ref, scales_ref, got_ref, out_ref, lines_ref):
    core = core_ref[0]
    gain, shift = scales_ref[:, 1:2], scales_ref[:, 2:3]
    rows, width = halo_ref.shape[0] - 1, halo_ref.shape[2]
    count = sums_ref.shape[2] // width

    def put(row, parts):
        for at, total in enumerate(parts):
            value = activate(total, gain, shift)
            for m in range(count):
                place = row * 2 * count + at * count + m
                lines_ref[pl.ds(place, LANES, stride=rows * 2 * count), :] = value[:, m * width : (m + 1) * width]

    @pl.when(core == 0)
    def _():
        for row in range(rows):
            total = sums_ref[row, :LANES]
            edge = halo_ref[row, :LANES].astype(F32)
            if not row:
                edge = edge + fix_ref[...]
            total = jnp.concatenate([total[:, :width] + edge, total[:, width:]], 1)
            if not row:
                total = total + got_ref[rows]
            put(row, (total, got_ref[row]))

    @pl.when(core == 1)
    def _():
        for row in range(rows):
            total, got = sums_ref[row, LANES:], got_ref[row]
            if not row:
                first = [halo_ref[m, LANES:].astype(F32) for m in range(2 * count)]
                total = total + jnp.concatenate(first[count:], 1)
                got = got + jnp.concatenate(first[:count], 1)
            put(row, (got, total))

    out_ref[...] = lines_ref[...].astype(BF16)


def last_stage(core, sums, halo, mid, thirds, scales):
    rows, outs, lanes = sums.shape
    params = pltpu.CompilerParams(vmem_limit_bytes=VMEM_LIMIT)
    theirs, fix = pl.pallas_call(
        theirs_kernel,
        out_shape=[
            jax.ShapeDtypeStruct((rows + 1, outs // 2, lanes), F32),
            jax.ShapeDtypeStruct((outs // 2, halo.shape[2]), F32),
        ],
        in_specs=inputs(4) + [pl.BlockSpec(memory_space=pl.ANY)] + inputs(6)[1:],
        compiler_params=params,
        name="theirs",
    )(core, sums, halo, mid, even_odd(lanes), *thirds)
    lines = (outs // 2 * rows * lanes * 2 // LANES, LANES)
    return pl.pallas_call(
        assemble_kernel,
        out_shape=jax.ShapeDtypeStruct(lines, BF16),
        in_specs=inputs(5),
        scratch_shapes=[pltpu.VMEM(lines, F32)],
        compiler_params=params,
        name="assemble",
    )(core, sums, halo, fix, scales, swapped(theirs))


def handed_on(message):
    count = lax.axis_size("sp")
    pairs = [(2 * b, 2 * (b + 1) + 1) for b in range(count) if b % ROW_BLOCKS != ROW_BLOCKS - 1]
    pairs += [(2 * b + 1, 2 * (b + ROW_BLOCKS)) for b in range(count - ROW_BLOCKS)]
    return lax.ppermute(message, ("sp", "fl"), pairs)


def swapped(value):
    return lax.ppermute(value, "fl", [(0, 1), (1, 0)])


def shards(volume, kernel_three, gain_three, shift_three, kernel_four, gain_four, shift_four):
    core = lax.axis_index("fl").reshape(1)
    own_scales = jnp.concatenate([gain_three, shift_three, gain_four, shift_four]).reshape(-1, LANES)
    message, weights_three, gain, shift, scales = three_edges(
        volume, kernel_three, swapped(kernel_three), own_scales, swapped(own_scales), core
    )
    halo = handed_on(message)
    *thirds, last_row, local = layer_three(volume, weights_three, gain, shift, core)
    rows = lax.ppermute(halo[: thirds[0].shape[0]], "fl", [(1, 0)])
    thirds = (*thirds, halo, rows, gain, shift)
    local, last_row = swapped(local), lax.ppermute(last_row, "fl", [(0, 1)])
    weights_four = four_weights(kernel_four, swapped(kernel_four), core)
    message, mid = four_edges(core, thirds, local, weights_four)
    halo = handed_on(message)
    sums = layer_four(core, thirds, local, last_row, weights_four)
    lines = last_stage(core, sums, halo, mid, thirds, scales)
    out_rows, outs, lanes = sums.shape
    fourth = lines.reshape(outs // 2, out_rows, 2 * lanes // LANES, LANES)
    return jnp.transpose(fourth, (0, 2, 1, 3))[None]


def solution(mesh):
    return jax.shard_map(
        shards,
        mesh=mesh,
        in_specs=(
            P("sp", None, None, None, None),
            P("fl", None),
            P("fl"),
            P("fl"),
            P("fl", None),
            P("fl"),
            P("fl"),
        ),
        out_specs=P("sp", "fl", None, None, None),
        check_vma=False,
    )
```

```python
import functools

import jax
import jax.numpy as jnp
import numpy as np
from jax import lax
from jax.experimental import pallas as pl
from jax.experimental.pallas import tpu as pltpu
from jax.sharding import PartitionSpec as P

F32 = jnp.float32
BF16 = jnp.bfloat16
LANES = 128
ROW_BLOCKS = 8
SUB = 8
TAPS = 27
RIM_TAPS = tuple(9 * a + e for a in range(3) for e in range(3))
GROUP = 16
MIB = 2**20


def even_odd(width):
    half = width // 2
    place = np.zeros((width, width), np.float32)
    place[np.arange(0, width, 2), np.arange(half)] = 1
    place[np.arange(1, width, 2), half + np.arange(half)] = 1
    return jnp.asarray(place, BF16)


def activate(total, gain, shift):
    return jnp.maximum(total * gain + shift, 0.0)


def shifted(odd):
    lane = lax.broadcasted_iota(jnp.int32, odd.shape, 1)
    return jnp.where(lane == 0, 0.0, pltpu.roll(odd, 1, 1))


def spread(sides, place):
    quarter = place.shape[0] // 2
    split = [jnp.dot(side, place, preferred_element_type=F32) for side in sides]
    even = jnp.concatenate([part[:, :quarter] for part in split], 1)
    odd = jnp.concatenate([part[:, quarter:] for part in split], 1)
    return shifted(odd), even, odd


def separate(x_ref, plane, place_ref, split_refs, store):
    chans, rows, width = x_ref.shape[1], x_ref.shape[3], x_ref.shape[4]
    half = width // 2
    quarter = half // 2
    for index, first in enumerate(range(0, chans, GROUP)):
        split_ref = split_refs[index % len(split_refs)]
        x = x_ref[0, pl.ds(first, GROUP), plane]
        x = x.astype(F32).reshape(GROUP * rows, width).astype(BF16)
        for side in range(2):
            parts = jnp.dot(
                x[:, side * half : (side + 1) * half], place_ref[...], preferred_element_type=F32
            )
            for block in range(half // LANES):
                odd, at = divmod(block, quarter // LANES)
                split_ref[odd, side * (quarter // LANES) + at] = parts[:, block * LANES : (block + 1) * LANES]
        for row in range(rows):
            even, odd = (
                jnp.concatenate(
                    [split_ref[odd, at, pl.ds(row, GROUP, stride=rows), :] for at in range(half // LANES)], 1
                )
                for odd in range(2)
            )
            for tap, value in enumerate((shifted(odd), even, odd)):
                store(tap, row, first, value.astype(BF16))
        yield


def whole(own, other, core):
    first = jnp.where(core == 0, own, other)
    second = jnp.where(core == 0, other, own)
    return jnp.concatenate([first, second], 0)


def turn(kernel, turned_ref):
    columns = kernel.shape[1]
    for at in range(0, columns, LANES):
        size = min(LANES, columns - at)
        turned_ref[at : at + size, :] = kernel[:, at : at + size].T


def tap_major(turned_ref, taps, w_ref, first):
    chans = turned_ref.shape[0] // TAPS
    at = 0
    for index in range(0, len(taps), LANES // chans):
        parts = [turned_ref[pl.ds(tap, chans, stride=TAPS), :] for tap in taps[index : index + LANES // chans]]
        block = jnp.concatenate(parts, 0).T.astype(BF16)
        w_ref[first : first + LANES, at : at + block.shape[1]] = block
        at += block.shape[1]


def four_weights_kernel(core_ref, own_ref, other_ref, w_ref, *turned_refs):
    core = core_ref[0]
    for index, turned_ref in enumerate(turned_refs):
        turn(jnp.where(core == index, own_ref[...].astype(F32), other_ref[...].astype(F32)), turned_ref)
        tap_major(turned_ref, range(TAPS), w_ref, index * LANES)


def four_weights(own, other, core):
    outs, columns = own.shape
    return pl.pallas_call(
        four_weights_kernel,
        out_shape=jax.ShapeDtypeStruct((2 * outs, columns), BF16),
        in_specs=[
            pl.BlockSpec(memory_space=pltpu.SMEM),
            pl.BlockSpec(memory_space=pltpu.VMEM),
            pl.BlockSpec(memory_space=pltpu.VMEM),
        ],
        scratch_shapes=[pltpu.VMEM((columns, LANES), F32)] * 2,
        compiler_params=pltpu.CompilerParams(vmem_limit_bytes=16 * MIB),
        cost_estimate=pl.CostEstimate(flops=10**6, bytes_accessed=4 * 10**6, transcendentals=0),
        name="four_weights",
    )(core, own, other)


def three_edges_kernel(
    core_ref, last_ref, rim_ref, own_ref, other_ref, own_scales_ref, other_scales_ref, place_ref,
    message_ref, w_ref, gain_ref, shift_ref, scales_ref,
    *scratch,
):
    *split_refs, turned_ref, pick_ref, data_ref, rims_ref, rim_w_ref = scratch
    core, step, last = core_ref[0], pl.program_id(0), pl.num_programs(0) - 1
    chans, rows, width = rim_ref.shape[1], last_ref.shape[3], last_ref.shape[4]
    block, planes = rim_ref.shape[2], rims_ref.shape[0]
    half = width // 2
    out_rows = rows // 2
    taps = 3 * chans
    rim = (rows - 1) % SUB

    @pl.when(step == 0)
    def _():
        turn(whole(own_ref[...].astype(F32), other_ref[...].astype(F32), core), turned_ref)
        tap_major(turned_ref, range(TAPS), w_ref, 0)
        tap_major(turned_ref, RIM_TAPS, rim_w_ref, 0)
        own_scales, other_scales = own_scales_ref[...], other_scales_ref[...]
        lines = own_scales.shape[0]
        scales = jnp.concatenate(
            [own_scales, other_scales, jnp.zeros((LANES - 2 * lines, LANES), F32)], 0
        ).T
        scales_ref[...] = scales
        share = own_ref.shape[0]
        for ref, at in ((gain_ref, 0), (shift_ref, share)):
            ref[...] = whole(scales[at : at + share, 0:1], scales[at : at + share, lines : lines + 1], core)

    def picked(spots):
        values, held = [], None
        for plane, row in spots:
            if plane != held:
                x = rim_ref[0, :, plane, :SUB].astype(F32).reshape(chans * SUB, width)
                for at in range(width // LANES):
                    pick_ref[plane % 2, at] = x[:, at * LANES : (at + 1) * LANES]
                held = plane
            values.append(
                jnp.concatenate(
                    [pick_ref[plane % 2, at, pl.ds(row, chans, stride=SUB), :] for at in range(width // LANES)], 1
                ).astype(BF16)
            )
        values = jnp.concatenate(values, 0)
        parts = [part.astype(BF16) for part in spread((values[:, :half], values[:, half:]), place_ref[...])]
        return [
            jnp.concatenate([part[at * chans : (at + 1) * chans] for part in parts], 0) for at in range(len(spots))
        ]

    @pl.when(core == 0)
    def _():
        for plane, data in enumerate(picked([(plane, rim) for plane in range(block)])):
            rims_ref[step * block + plane] = data

    @pl.when((core == 0) & (step == last))
    def _():
        none = jnp.zeros((taps, half), BF16)
        for index in range(planes // 2 + 1):
            pieces = [
                rims_ref[plane] if 0 <= plane < planes else none for plane in range(2 * index - 1, 2 * index + 2)
            ]
            total = jnp.dot(rim_w_ref[...], jnp.concatenate(pieces, 0), preferred_element_type=F32)
            message_ref[index] = total.astype(BF16)
        spots = [(plane, row) for plane in range(block - 3, block) for row in range(rim - 2, rim + 1)]
        total = jnp.dot(w_ref[...], jnp.concatenate(picked(spots), 0), preferred_element_type=F32)
        message_ref[planes // 2 + 1] = activate(total, gain_ref[...], shift_ref[...]).astype(BF16)
        for index in range(planes // 2 + 2, message_ref.shape[0]):
            message_ref[index] = jnp.zeros_like(message_ref[index])

    @pl.when(core == 1)
    def _():
        part = last_ref.shape[1]

        def store(tap, row, first, value):
            at = pl.multiple_of(tap * chans + step * part + first, GROUP)
            data_ref[row + 1, pl.ds(at, GROUP), :] = value

        for _ in separate(last_ref, 0, place_ref, split_refs, store):
            pass

    @pl.when((core == 1) & (step == last))
    def _():
        data_ref[0] = jnp.zeros_like(data_ref[0])
        for row in range(out_rows):
            total = jnp.dot(
                w_ref[:, : 3 * taps],
                data_ref[2 * row : 2 * row + 3].reshape(3 * taps, half),
                preferred_element_type=F32,
            )
            message_ref[row] = total.astype(BF16)


def three_edges(volume, own, other, own_scales, other_scales, core):
    _, chans, planes, rows, width = volume.shape
    outs, columns = 2 * own.shape[0], own.shape[1]
    half = width // 2
    block, steps, out_rows = 4, planes // 4, rows // 2
    full = lambda *shape: pl.BlockSpec(shape, lambda i, core: (0,) * len(shape))
    shapes = [
        ((out_rows, outs, half), BF16),
        ((outs, columns), BF16),
        ((outs, 1), F32),
        ((outs, 1), F32),
        ((LANES, LANES), F32),
    ]
    return pl.pallas_call(
        three_edges_kernel,
        grid_spec=pltpu.PrefetchScalarGridSpec(
            num_scalar_prefetch=1,
            grid=(steps,),
            in_specs=[
                pl.BlockSpec((1, chans // steps, 1, rows, width), lambda i, core: (0, i * core[0], planes - 1, 0, 0)),
                pl.BlockSpec(
                    (1, chans, block, 2 * SUB, width),
                    lambda i, core: (0, 0, i + core[0] * (steps - 1 - i), (rows - 1) // (2 * SUB), 0),
                ),
                full(*own.shape),
                full(*other.shape),
                full(*own_scales.shape),
                full(*other_scales.shape),
                full(half, half),
            ],
            out_specs=[full(*shape) for shape, _ in shapes],
            scratch_shapes=[pltpu.VMEM((2, half // LANES, GROUP * rows, LANES), F32)] * 4
            + [
                pltpu.VMEM((columns, LANES), F32),
                pltpu.VMEM((2, width // LANES, chans * SUB, LANES), F32),
                pltpu.VMEM((rows + 1, 3 * chans, half), BF16),
                pltpu.VMEM((planes, 3 * chans, half), BF16),
                pltpu.VMEM((outs, columns // 3), BF16),
            ],
        ),
        out_shape=[jax.ShapeDtypeStruct(*shape) for shape in shapes],
        compiler_params=pltpu.CompilerParams(vmem_limit_bytes=36 * MIB),
        cost_estimate=pl.CostEstimate(flops=2 * 10**9, bytes_accessed=8 * 10**6, transcendentals=0),
        name="three_edges",
    )(core, volume, volume, own, other, own_scales, other_scales, even_odd(half))


def three_kernel(
    core_ref, x_ref, before_ref, w_ref, place_ref, gain_ref, shift_ref,
    third_ref, plane_ref, row_ref, local_ref,
    *scratch,
):
    *split_refs, prior_ref, first_ref, second_ref, total_ref = scratch
    core, step, steps = core_ref[0], pl.program_id(0), pl.num_programs(0) - 1
    chans, rows, width = x_ref.shape[1], x_ref.shape[3], x_ref.shape[4]
    half = width // 2
    out_rows = rows // 2
    taps = 3 * chans

    def splitting(pair_ref):
        for plane in range(2):

            def store(tap, row, first, value, plane=plane):
                pair_ref[plane, row + 1, tap * chans + first : tap * chans + first + GROUP, :] = value

            yield from separate(x_ref, plane, place_ref, split_refs, store)

    def summing(pair_ref):
        gain, shift = gain_ref[...], shift_ref[...]
        for row in range(out_rows):
            parts = [
                ref[2 * row : 2 * row + 3].reshape(3 * taps, half)
                for ref in (prior_ref, pair_ref.at[0], pair_ref.at[1])
            ]
            total = jnp.dot(w_ref[...], jnp.concatenate(parts, 0), preferred_element_type=F32)
            third_ref[0, row] = activate(total, gain, shift).astype(BF16)
            total_ref[row] = total
            yield
        row_ref[0] = total_ref[0]
        prior_ref[...] = pair_ref[1]
        yield

    @pl.when(step == 0)
    def _():
        prior_ref[...] = jnp.zeros_like(prior_ref)

        @pl.when(core == 1)
        def _():
            def store(tap, row, first, value):
                prior_ref[row + 1, tap * chans + first : tap * chans + first + GROUP, :] = value

            for _ in separate(before_ref, 0, place_ref, split_refs, store):
                pass

        for ref in (first_ref, second_ref):
            ref[:, 0] = jnp.zeros_like(ref[:, 0])
        for _ in splitting(first_ref):
            pass

    def both(new_ref, old_ref):
        new, old = splitting(new_ref), summing(old_ref)
        for turn in range(2 * chans // GROUP):
            next(new, None)
            for _ in range(out_rows * (turn + 1) // (2 * chans // GROUP) - out_rows * turn // (2 * chans // GROUP)):
                next(old, None)
        for _ in new:
            pass
        for _ in old:
            pass

    for odd, (new_ref, old_ref) in enumerate(((first_ref, second_ref), (second_ref, first_ref))):

        @pl.when((step > 0) & (step < steps) & (step % 2 == odd))
        def _(new_ref=new_ref, old_ref=old_ref):
            both(new_ref, old_ref)

        @pl.when((step == steps) & (step % 2 == odd))
        def _(old_ref=old_ref):
            for _ in summing(old_ref):
                pass

    @pl.when(step == 1)
    def _():
        plane_ref[...] = total_ref[...]

    @pl.when((step > 0) & (core == 1))
    def _():
        local_ref[step - 1] = third_ref[0, out_rows - 1]

    @pl.when((step == steps) & (core == 0))
    def _():
        local_ref[...] = third_ref[0]
        local_ref[0] = total_ref[0].astype(BF16)


def layer_three(volume, weights, gain, shift, core):
    _, chans, planes, rows, width = volume.shape
    outs = weights.shape[0]
    half = width // 2
    steps, out_rows = planes // 4, rows // 2
    full = lambda *shape: pl.BlockSpec(shape, lambda i, core: (0,) * len(shape))
    return pl.pallas_call(
        three_kernel,
        grid_spec=pltpu.PrefetchScalarGridSpec(
            num_scalar_prefetch=1,
            grid=(steps + 1,),
            in_specs=[
                pl.BlockSpec((1, chans, 2, rows, width), lambda i, core: (0, 0, core[0] * steps + jnp.minimum(i, steps - 1), 0, 0)),
                pl.BlockSpec(
                    (1, chans, 1, rows, width),
                    lambda i, core: (0, 0, jnp.maximum(core[0] * 2 * steps - 1, 0), 0, 0),
                ),
                full(*weights.shape),
                full(half, half),
                full(outs, 1),
                full(outs, 1),
            ],
            out_specs=[
                pl.BlockSpec((1, out_rows, outs, half), lambda i, core: (jnp.maximum(i - 1, 0), 0, 0, 0)),
                full(out_rows, outs, half),
                pl.BlockSpec((1, outs, half), lambda i, core: (jnp.maximum(i - 1, 0), 0, 0)),
                full(out_rows, outs, half),
            ],
            scratch_shapes=[pltpu.VMEM((2, half // LANES, GROUP * rows, LANES), F32)] * 4
            + [
                pltpu.VMEM((rows + 1, 3 * chans, half), BF16),
                pltpu.VMEM((2, rows + 1, 3 * chans, half), BF16),
                pltpu.VMEM((2, rows + 1, 3 * chans, half), BF16),
                pltpu.VMEM((out_rows, outs, half), F32),
            ],
        ),
        out_shape=[
            jax.ShapeDtypeStruct((steps, out_rows, outs, half), BF16),
            jax.ShapeDtypeStruct((out_rows, outs, half), F32),
            jax.ShapeDtypeStruct((steps, outs, half), F32),
            jax.ShapeDtypeStruct((out_rows, outs, half), BF16),
        ],
        compiler_params=pltpu.CompilerParams(vmem_limit_bytes=46 * MIB),
        cost_estimate=pl.CostEstimate(flops=10**10, bytes_accessed=2 * 10**7, transcendentals=0),
        name="layer_three",
    )(core, volume, volume, weights, even_odd(half), gain, shift)


def corner_total(core, refs):
    _, plane_ref, _, halo_ref, rows_ref, _, _ = refs
    planes = rows_ref.shape[0]
    first = jnp.where(core == 0, rows_ref[0].astype(F32), halo_ref[planes].astype(F32))
    return plane_ref[0] + jnp.where(core == 0, halo_ref[0].astype(F32), 0.0) + first


def third_value(core, refs, plane, row):
    third_ref, plane_ref, row_ref, halo_ref, rows_ref, gain_ref, shift_ref = refs
    planes = rows_ref.shape[0]
    if plane and row:
        return third_ref[plane, row]
    if plane:
        share = jnp.where(core == 0, rows_ref[plane].astype(F32), halo_ref[planes + plane].astype(F32))
        total = row_ref[plane] + share
    elif row:
        total = plane_ref[row] + jnp.where(core == 0, halo_ref[row].astype(F32), 0.0)
    else:
        total = corner_total(core, refs)
    value = activate(total, gain_ref[...], shift_ref[...])
    if not plane and not row:
        value = jnp.where(core == 0, 0.0, value)
    return value.astype(BF16)


def four_edges_kernel(core_ref, *refs):
    *thirds, local_ref, w_ref, place_ref, message_ref, mid_ref = refs
    core = core_ref[0]
    planes, rows, chans, width = thirds[0].shape
    half = width // 2
    out_rows = rows // 2
    taps = 3 * chans
    mid_ref[...] = w_ref[:, 4 * taps : 5 * taps]

    def data(values):
        parts = [part.astype(BF16) for part in spread((jnp.concatenate(values, 0),), place_ref[...])]
        return [
            jnp.concatenate([part[at * chans : (at + 1) * chans] for part in parts], 0) for at in range(len(values))
        ]

    @pl.when(core == 0)
    def _():
        none = jnp.zeros((taps, half), BF16)
        rim = [none] + data(
            [third_value(core, thirds, plane, rows - 1) for plane in range(planes)]
            + [local_ref[plane] for plane in range(planes)]
        )
        pieces = [jnp.concatenate([rim[2 * m + slot] for m in range(planes)], 1) for slot in range(3)]
        weights = jnp.concatenate([w_ref[:, 3 * slot * taps : (3 * slot + 1) * taps] for slot in range(3)], 1)
        total = jnp.dot(weights, jnp.concatenate(pieces, 0), preferred_element_type=F32).astype(BF16)
        for m in range(planes):
            message_ref[m] = total[:, m * half : (m + 1) * half]
        for index in range(planes, message_ref.shape[0]):
            message_ref[index] = jnp.zeros_like(message_ref[index])

    @pl.when(core == 1)
    def _():
        halo_ref = thirds[3]
        last = data(
            [halo_ref[2 * planes + 1]] + [third_value(core, thirds, planes - 1, row) for row in range(rows)]
        )
        for row in range(0, out_rows, 2):
            pieces = [jnp.concatenate([last[2 * row + at], last[2 * row + 2 + at]], 1) for at in range(3)]
            both = jnp.dot(w_ref[:, : 3 * taps], jnp.concatenate(pieces, 0), preferred_element_type=F32)
            both = both.astype(BF16)
            message_ref[row] = both[:, :half]
            message_ref[row + 1] = both[:, half:]
        corner = halo_ref[2 * planes]
        message_ref[out_rows, :chans] = corner[:, :half]
        message_ref[out_rows, chans:] = corner[:, half:]


def inputs(count):
    return [pl.BlockSpec(memory_space=pltpu.SMEM)] + [pl.BlockSpec(memory_space=pltpu.VMEM)] * count


def four_edges(core, thirds, local, weights):
    planes, rows, chans, width = thirds[0].shape
    outs = weights.shape[0]
    half = width // 2
    return pl.pallas_call(
        four_edges_kernel,
        out_shape=[
            jax.ShapeDtypeStruct((rows // 2 + 1, outs, half), BF16),
            jax.ShapeDtypeStruct((outs, 3 * chans), BF16),
        ],
        in_specs=inputs(len(thirds) + 3),
        compiler_params=pltpu.CompilerParams(vmem_limit_bytes=24 * MIB),
        cost_estimate=pl.CostEstimate(flops=2 * 10**9, bytes_accessed=8 * 10**6, transcendentals=0),
        name="four_edges",
    )(core, *thirds, local, weights, even_odd(width))


def four_kernel(core_ref, *refs):
    *thirds, local_ref, w_ref, place_ref, sums_ref, corner_ref, data_ref = refs
    core = core_ref[0]
    planes, rows, chans, width = thirds[0].shape
    halo_ref, gain_ref, shift_ref = thirds[3], thirds[5], thirds[6]
    half = width // 2
    out_rows, count = rows // 2, planes // 2
    taps = 3 * chans
    batch = 4
    data_ref[:, 0] = jnp.zeros_like(data_ref[:, 0])
    corner_ref[...] = corner_total(core, thirds)

    def put(values, first, spots):
        for tap, part in enumerate(spread((jnp.concatenate(values, 0),), place_ref[...])):
            part = part.astype(BF16)
            for at in range(len(values)):
                for slot, lanes in spots:
                    data_ref[
                        slot, first + at + 1, tap * chans : (tap + 1) * chans, lanes * half : (lanes + 1) * half
                    ] = part[at * chans : (at + 1) * chans]

    @pl.when(core == 0)
    def _():
        data_ref[0, :, :, :half] = jnp.zeros_like(data_ref[0, :, :, :half])

    @pl.when(core == 1)
    def _():
        total = local_ref[0].astype(F32) + halo_ref[planes - 1].astype(F32)
        prior = [activate(total, gain_ref[...], shift_ref[...]).astype(BF16)]
        prior += [local_ref[row] for row in range(1, rows)]
        for first in range(0, rows, batch):
            put(prior[first : first + batch], first, [(0, 0)])

    for plane in range(planes):
        spots = [(1 + plane % 2, plane // 2)]
        if plane % 2 and plane // 2 + 1 < count:
            spots.append((0, plane // 2 + 1))
        for first in range(0, rows, batch):
            put([third_value(core, thirds, plane, row) for row in range(first, first + batch)], first, spots)
    for row in range(out_rows):
        parts = [data_ref[slot, 2 * row : 2 * row + 3].reshape(3 * taps, count * half) for slot in range(3)]
        sums_ref[row] = jnp.dot(w_ref[...], jnp.concatenate(parts, 0), preferred_element_type=F32)


def layer_four(core, thirds, local, weights):
    planes, rows, chans, width = thirds[0].shape
    outs = weights.shape[0]
    half = width // 2
    out_rows, count = rows // 2, planes // 2
    return pl.pallas_call(
        four_kernel,
        out_shape=[
            jax.ShapeDtypeStruct((out_rows, outs, count * half), F32),
            jax.ShapeDtypeStruct((chans, width), F32),
        ],
        in_specs=inputs(len(thirds) + 3),
        scratch_shapes=[pltpu.VMEM((3, rows + 1, 3 * chans, count * half), BF16)],
        compiler_params=pltpu.CompilerParams(vmem_limit_bytes=32 * MIB),
        cost_estimate=pl.CostEstimate(flops=8 * 10**9, bytes_accessed=10**7, transcendentals=0),
        name="layer_four",
    )(core, *thirds, local, weights, even_odd(width))


def theirs_kernel(
    core_ref, sums_ref, corner_ref, halo_ref, mid_ref, place_ref, gain_ref, shift_ref, theirs_ref, fix_ref
):
    core = core_ref[0]
    rows, width = halo_ref.shape[0] - 1, halo_ref.shape[2]

    @pl.when(core == 0)
    def _():
        corner = halo_ref[rows].astype(F32)
        total = corner_ref[...] + jnp.concatenate([corner[:LANES], corner[LANES:]], 1)
        value = activate(total, gain_ref[...], shift_ref[...]).astype(BF16)
        data = jnp.concatenate([part.astype(BF16) for part in spread((value,), place_ref[...])], 0)
        fix = jnp.dot(mid_ref[...], data, preferred_element_type=F32)
        fix_ref[...] = fix[:LANES]
        for row in range(rows):
            total = sums_ref[row, LANES:]
            edge = halo_ref[row, LANES:].astype(F32)
            if not row:
                edge = edge + fix[LANES:]
            theirs_ref[row] = jnp.concatenate([total[:, :width] + edge, total[:, width:]], 1)
        theirs_ref[rows] = jnp.zeros_like(theirs_ref[rows])

    @pl.when(core == 1)
    def _():
        count = sums_ref.shape[2] // width
        fix_ref[...] = jnp.zeros_like(fix_ref)
        for row in range(rows):
            total = sums_ref[row, :LANES]
            if not row:
                total = total + jnp.concatenate([halo_ref[count + m, :LANES].astype(F32) for m in range(count)], 1)
            theirs_ref[row] = total
        theirs_ref[rows] = jnp.concatenate([halo_ref[m, :LANES].astype(F32) for m in range(count)], 1)


def assemble_kernel(core_ref, sums_ref, halo_ref, fix_ref, scales_ref, got_ref, out_ref, lines_ref):
    core = core_ref[0]
    gain, shift = scales_ref[:, 1:2], scales_ref[:, 2:3]
    rows, width = halo_ref.shape[0] - 1, halo_ref.shape[2]
    count = sums_ref.shape[2] // width

    def put(row, parts):
        for at, total in enumerate(parts):
            value = activate(total, gain, shift)
            for m in range(count):
                place = row * 2 * count + at * count + m
                lines_ref[pl.ds(place, LANES, stride=rows * 2 * count), :] = value[:, m * width : (m + 1) * width]

    @pl.when(core == 0)
    def _():
        for row in range(rows):
            total = sums_ref[row, :LANES]
            edge = halo_ref[row, :LANES].astype(F32)
            if not row:
                edge = edge + fix_ref[...]
            total = jnp.concatenate([total[:, :width] + edge, total[:, width:]], 1)
            if not row:
                total = total + got_ref[rows]
            put(row, (total, got_ref[row]))

    @pl.when(core == 1)
    def _():
        for row in range(rows):
            total, got = sums_ref[row, LANES:], got_ref[row]
            if not row:
                first = [halo_ref[m, LANES:].astype(F32) for m in range(2 * count)]
                total = total + jnp.concatenate(first[count:], 1)
                got = got + jnp.concatenate(first[:count], 1)
            put(row, (got, total))

    out_ref[...] = lines_ref[...].astype(BF16)


def last_stage(core, sums, corner, halo, mid, gain, shift, scales):
    rows, outs, lanes = sums.shape
    params = pltpu.CompilerParams(vmem_limit_bytes=16 * MIB)
    theirs, fix = pl.pallas_call(
        theirs_kernel,
        out_shape=[
            jax.ShapeDtypeStruct((rows + 1, outs // 2, lanes), F32),
            jax.ShapeDtypeStruct((outs // 2, halo.shape[2]), F32),
        ],
        in_specs=inputs(7),
        compiler_params=params,
        name="theirs",
    )(core, sums, corner, halo, mid, even_odd(lanes), gain, shift)
    lines = (outs // 2 * rows * lanes * 2 // LANES, LANES)
    return pl.pallas_call(
        assemble_kernel,
        out_shape=jax.ShapeDtypeStruct(lines, BF16),
        in_specs=inputs(5),
        scratch_shapes=[pltpu.VMEM(lines, F32)],
        compiler_params=params,
        name="assemble",
    )(core, sums, halo, fix, scales, swapped(theirs))


def handed_on(message):
    count = lax.axis_size("sp")
    pairs = [(2 * b, 2 * (b + 1) + 1) for b in range(count) if b % ROW_BLOCKS != ROW_BLOCKS - 1]
    pairs += [(2 * b + 1, 2 * (b + ROW_BLOCKS)) for b in range(count - ROW_BLOCKS)]
    return lax.ppermute(message, ("sp", "fl"), pairs)


def swapped(value):
    return lax.ppermute(value, "fl", [(0, 1), (1, 0)])


def shards(volume, kernel_three, gain_three, shift_three, kernel_four, gain_four, shift_four):
    core = lax.axis_index("fl").reshape(1)
    own_scales = jnp.concatenate([gain_three, shift_three, gain_four, shift_four]).reshape(-1, LANES)
    message, weights_three, gain, shift, scales = three_edges(
        volume, kernel_three, swapped(kernel_three), own_scales, swapped(own_scales), core
    )
    halo = handed_on(message)
    *thirds, local = layer_three(volume, weights_three, gain, shift, core)
    rows = lax.ppermute(halo[: thirds[0].shape[0]], "fl", [(1, 0)])
    thirds = (*thirds, halo, rows, gain, shift)
    local = swapped(local)
    weights_four = four_weights(kernel_four, swapped(kernel_four), core)
    message, mid = four_edges(core, thirds, local, weights_four)
    halo = handed_on(message)
    sums, corner = layer_four(core, thirds, local, weights_four)
    lines = last_stage(core, sums, corner, halo, mid, gain, shift, scales)
    out_rows, outs, lanes = sums.shape
    fourth = lines.reshape(outs // 2, out_rows, 2 * lanes // LANES, LANES)
    return jnp.transpose(fourth, (0, 2, 1, 3))[None]


def solution(mesh):
    return jax.shard_map(
        shards,
        mesh=mesh,
        in_specs=(
            P("sp", None, None, None, None),
            P("fl", None),
            P("fl"),
            P("fl"),
            P("fl", None),
            P("fl"),
            P("fl"),
        ),
        out_specs=P("sp", "fl", None, None, None),
        check_vma=False,
    )
```

```python
import functools

import jax
import jax.numpy as jnp
import numpy as np
from jax import lax
from jax.experimental import pallas as pl
from jax.experimental.pallas import tpu as pltpu
from jax.sharding import PartitionSpec as P

F32 = jnp.float32
BF16 = jnp.bfloat16
LANES = 128
ROW_BLOCKS = 8
SUB = 8
TAPS = 27
RIM_TAPS = tuple(9 * a + e for a in range(3) for e in range(3))
GROUP = 16
MIB = 2**20


def even_odd(width):
    half = width // 2
    place = np.zeros((width, width), np.float32)
    place[np.arange(0, width, 2), np.arange(half)] = 1
    place[np.arange(1, width, 2), half + np.arange(half)] = 1
    return jnp.asarray(place, BF16)


def activate(total, gain, shift):
    return jnp.maximum(total * gain + shift, 0.0)


def shifted(odd):
    lane = lax.broadcasted_iota(jnp.int32, odd.shape, 1)
    return jnp.where(lane == 0, 0.0, pltpu.roll(odd, 1, 1))


def spread(sides, place):
    quarter = place.shape[0] // 2
    split = [jnp.dot(side, place, preferred_element_type=F32) for side in sides]
    even = jnp.concatenate([part[:, :quarter] for part in split], 1)
    odd = jnp.concatenate([part[:, quarter:] for part in split], 1)
    return shifted(odd), even, odd


def separate(x_ref, plane, place_ref, split_refs, store):
    chans, rows, width = x_ref.shape[1], x_ref.shape[3], x_ref.shape[4]
    half = width // 2
    quarter = half // 2
    for index, first in enumerate(range(0, chans, GROUP)):
        split_ref = split_refs[index % len(split_refs)]
        x = x_ref[0, pl.ds(first, GROUP), plane]
        x = x.astype(F32).reshape(GROUP * rows, width).astype(BF16)
        for side in range(2):
            parts = jnp.dot(
                x[:, side * half : (side + 1) * half], place_ref[...], preferred_element_type=F32
            )
            for block in range(half // LANES):
                odd, at = divmod(block, quarter // LANES)
                split_ref[odd, side * (quarter // LANES) + at] = parts[:, block * LANES : (block + 1) * LANES]
        for row in range(rows):
            even, odd = (
                jnp.concatenate(
                    [split_ref[odd, at, pl.ds(row, GROUP, stride=rows), :] for at in range(half // LANES)], 1
                )
                for odd in range(2)
            )
            for tap, value in enumerate((shifted(odd), even, odd)):
                store(tap, row, first, value.astype(BF16))
        yield


def inputs(count):
    return [pl.BlockSpec(memory_space=pltpu.SMEM)] + [pl.BlockSpec(memory_space=pltpu.VMEM)] * count


def whole(own, other, core):
    first = jnp.where(core == 0, own, other)
    second = jnp.where(core == 0, other, own)
    return jnp.concatenate([first, second], 0)


def turn(kernel, turned_ref):
    columns = kernel.shape[1]
    for at in range(0, columns, LANES):
        size = min(LANES, columns - at)
        turned_ref[at : at + size, :] = kernel[:, at : at + size].T


def tap_major(turned_ref, taps, w_ref, first):
    chans = turned_ref.shape[0] // TAPS
    at = 0
    for index in range(0, len(taps), LANES // chans):
        parts = [turned_ref[pl.ds(tap, chans, stride=TAPS), :] for tap in taps[index : index + LANES // chans]]
        block = jnp.concatenate(parts, 0).T.astype(BF16)
        w_ref[first : first + LANES, at : at + block.shape[1]] = block
        at += block.shape[1]


def four_weights_kernel(core_ref, own_ref, other_ref, w_ref, *turned_refs):
    core = core_ref[0]
    for index, turned_ref in enumerate(turned_refs):
        turn(jnp.where(core == index, own_ref[...].astype(F32), other_ref[...].astype(F32)), turned_ref)
        tap_major(turned_ref, range(TAPS), w_ref, index * LANES)


def four_weights(own, other, core):
    outs, columns = own.shape
    return pl.pallas_call(
        four_weights_kernel,
        out_shape=jax.ShapeDtypeStruct((2 * outs, columns), BF16),
        in_specs=[
            pl.BlockSpec(memory_space=pltpu.SMEM),
            pl.BlockSpec(memory_space=pltpu.VMEM),
            pl.BlockSpec(memory_space=pltpu.VMEM),
        ],
        scratch_shapes=[pltpu.VMEM((columns, LANES), F32)] * 2,
        compiler_params=pltpu.CompilerParams(vmem_limit_bytes=16 * MIB),
        cost_estimate=pl.CostEstimate(flops=10**6, bytes_accessed=4 * 10**6, transcendentals=0),
        name="four_weights",
    )(core, own, other)


def three_picks_kernel(core_ref, last_ref, before_ref, rim_ref, place_ref, picked_ref, prior_ref, *scratch):
    *split_refs, pick_ref = scratch
    core, step, last = core_ref[0], pl.program_id(0), pl.num_programs(0) - 1
    chans, block, width = rim_ref.shape[1], rim_ref.shape[2], rim_ref.shape[4]
    rows, part = last_ref.shape[3], last_ref.shape[1]
    planes = block * 4
    half = width // 2
    rim = (rows - 1) % SUB

    def picked(spots):
        values, held = [], None
        for plane, row in spots:
            if plane != held:
                x = rim_ref[0, :, plane, :SUB].astype(F32).reshape(chans * SUB, width)
                for at in range(width // LANES):
                    pick_ref[plane % 2, at] = x[:, at * LANES : (at + 1) * LANES]
                held = plane
            values.append(
                jnp.concatenate(
                    [pick_ref[plane % 2, at, pl.ds(row, chans, stride=SUB), :] for at in range(width // LANES)], 1
                ).astype(BF16)
            )
        values = jnp.concatenate(values, 0)
        parts = [part.astype(BF16) for part in spread((values[:, :half], values[:, half:]), place_ref[...])]
        return [
            jnp.concatenate([part[at * chans : (at + 1) * chans] for part in parts], 0) for at in range(len(spots))
        ]

    @pl.when(core == 0)
    def _():
        for plane, data in enumerate(picked([(plane, rim) for plane in range(block)])):
            picked_ref[step * block + plane] = data

    @pl.when((core == 0) & (step == last))
    def _():
        spots = [(plane, row) for plane in range(block - 3, block) for row in range(rim - 2, rim + 1)]
        for index, data in enumerate(picked(spots)):
            picked_ref[planes + index] = data
        prior_ref[...] = jnp.zeros_like(prior_ref)

    @pl.when(core == 1)
    def _():
        for source_ref, to_ref in ((last_ref, picked_ref), (before_ref, prior_ref)):

            def store(tap, row, first, value):
                at = pl.multiple_of(tap * chans + step * part + first, GROUP)
                to_ref[row + 1, pl.ds(at, GROUP), :] = value

            for _ in separate(source_ref, 0, place_ref, split_refs, store):
                pass

    @pl.when((core == 1) & (step == last))
    def _():
        for ref in (picked_ref, prior_ref):
            ref[0] = jnp.zeros_like(ref[0])


def three_picks(volume, core):
    _, chans, planes, rows, width = volume.shape
    half = width // 2
    block, steps = planes // 4, 4
    shape = (rows + 1, 3 * chans, half)
    full = lambda *shape: pl.BlockSpec(shape, lambda i, core: (0,) * len(shape))
    return pl.pallas_call(
        three_picks_kernel,
        grid_spec=pltpu.PrefetchScalarGridSpec(
            num_scalar_prefetch=1,
            grid=(steps,),
            in_specs=[
                pl.BlockSpec((1, chans // steps, 1, rows, width), lambda i, core: (0, i * core[0], planes - 1, 0, 0)),
                pl.BlockSpec(
                    (1, chans // steps, 1, rows, width), lambda i, core: (0, i * core[0], planes // 2 - 1, 0, 0)
                ),
                pl.BlockSpec(
                    (1, chans, block, 2 * SUB, width),
                    lambda i, core: (0, 0, i + core[0] * (steps - 1 - i), (rows - 1) // (2 * SUB), 0),
                ),
                full(half, half),
            ],
            out_specs=[full(*shape), full(*shape)],
            scratch_shapes=[pltpu.VMEM((2, half // LANES, GROUP * rows, LANES), F32)] * 2
            + [pltpu.VMEM((2, width // LANES, chans * SUB, LANES), F32)],
        ),
        out_shape=[jax.ShapeDtypeStruct(shape, BF16)] * 2,
        compiler_params=pltpu.CompilerParams(vmem_limit_bytes=36 * MIB),
        cost_estimate=pl.CostEstimate(flops=10**9, bytes_accessed=10**7, transcendentals=0),
        name="three_picks",
    )(core, volume, volume, volume, even_odd(half))


def three_edges_kernel(
    core_ref, picked_ref, own_ref, other_ref, own_scales_ref, other_scales_ref,
    message_ref, w_ref, gain_ref, shift_ref, scales_ref,
    turned_ref, rim_w_ref,
):
    core = core_ref[0]
    count, taps, half = picked_ref.shape
    out_rows = message_ref.shape[0]
    planes = count - 9
    turn(whole(own_ref[...].astype(F32), other_ref[...].astype(F32), core), turned_ref)
    tap_major(turned_ref, range(TAPS), w_ref, 0)
    own_scales, other_scales = own_scales_ref[...], other_scales_ref[...]
    lines = own_scales.shape[0]
    scales = jnp.concatenate([own_scales, other_scales, jnp.zeros((LANES - 2 * lines, LANES), F32)], 0).T
    scales_ref[...] = scales
    share = own_ref.shape[0]
    for ref, at in ((gain_ref, 0), (shift_ref, share)):
        ref[...] = whole(scales[at : at + share, 0:1], scales[at : at + share, lines : lines + 1], core)

    @pl.when(core == 0)
    def _():
        tap_major(turned_ref, RIM_TAPS, rim_w_ref, 0)
        none = jnp.zeros((taps, half), BF16)
        for index in range(planes // 2 + 1):
            pieces = [
                picked_ref[plane] if 0 <= plane < planes else none for plane in range(2 * index - 1, 2 * index + 2)
            ]
            total = jnp.dot(rim_w_ref[...], jnp.concatenate(pieces, 0), preferred_element_type=F32)
            message_ref[index] = total.astype(BF16)
        data = picked_ref[planes:].reshape(9 * taps, half)
        total = jnp.dot(w_ref[...], data, preferred_element_type=F32)
        message_ref[planes // 2 + 1] = activate(total, gain_ref[...], shift_ref[...]).astype(BF16)
        for index in range(planes // 2 + 2, out_rows):
            message_ref[index] = jnp.zeros_like(message_ref[index])

    @pl.when(core == 1)
    def _():
        for row in range(out_rows):
            total = jnp.dot(
                w_ref[:, : 3 * taps],
                picked_ref[2 * row : 2 * row + 3].reshape(3 * taps, half),
                preferred_element_type=F32,
            )
            message_ref[row] = total.astype(BF16)


def three_edges(picked, own, other, own_scales, other_scales, core):
    outs, columns = 2 * own.shape[0], own.shape[1]
    out_rows, half = picked.shape[0] // 2, picked.shape[2]
    shapes = [
        ((out_rows, outs, half), BF16),
        ((outs, columns), BF16),
        ((outs, 1), F32),
        ((outs, 1), F32),
        ((LANES, LANES), F32),
    ]
    return pl.pallas_call(
        three_edges_kernel,
        in_specs=inputs(5),
        out_shape=[jax.ShapeDtypeStruct(*shape) for shape in shapes],
        scratch_shapes=[pltpu.VMEM((columns, LANES), F32), pltpu.VMEM((outs, columns // 3), BF16)],
        compiler_params=pltpu.CompilerParams(vmem_limit_bytes=16 * MIB),
        cost_estimate=pl.CostEstimate(flops=10**9, bytes_accessed=10**6, transcendentals=0),
        name="three_edges",
    )(core, picked, own, other, own_scales, other_scales)


def three_kernel(
    core_ref, x_ref, before_ref, w_ref, place_ref, gain_ref, shift_ref,
    third_ref, plane_ref, row_ref, local_ref,
    *scratch,
):
    *split_refs, prior_ref, first_ref, second_ref, total_ref = scratch
    core, step, steps = core_ref[0], pl.program_id(0), pl.num_programs(0) - 1
    chans, rows, width = x_ref.shape[1], x_ref.shape[3], x_ref.shape[4]
    half = width // 2
    out_rows = rows // 2
    taps = 3 * chans

    def splitting(pair_ref):
        for plane in range(2):

            def store(tap, row, first, value, plane=plane):
                pair_ref[plane, row + 1, tap * chans + first : tap * chans + first + GROUP, :] = value

            yield from separate(x_ref, plane, place_ref, split_refs, store)

    def summing(pair_ref):
        gain, shift = gain_ref[...], shift_ref[...]
        for row in range(out_rows):
            parts = [
                ref[2 * row : 2 * row + 3].reshape(3 * taps, half)
                for ref in (prior_ref, pair_ref.at[0], pair_ref.at[1])
            ]
            total = jnp.dot(w_ref[...], jnp.concatenate(parts, 0), preferred_element_type=F32)
            third_ref[0, row] = activate(total, gain, shift).astype(BF16)
            total_ref[row] = total
            yield
        row_ref[0] = total_ref[0]
        prior_ref[...] = pair_ref[1]
        yield

    @pl.when(step == 0)
    def _():
        prior_ref[...] = before_ref[...]
        for ref in (first_ref, second_ref):
            ref[:, 0] = jnp.zeros_like(ref[:, 0])
        for _ in splitting(first_ref):
            pass

    def both(new_ref, old_ref):
        new, old = splitting(new_ref), summing(old_ref)
        for turn in range(2 * chans // GROUP):
            next(new, None)
            for _ in range(out_rows * (turn + 1) // (2 * chans // GROUP) - out_rows * turn // (2 * chans // GROUP)):
                next(old, None)
        for _ in new:
            pass
        for _ in old:
            pass

    for odd, (new_ref, old_ref) in enumerate(((first_ref, second_ref), (second_ref, first_ref))):

        @pl.when((step > 0) & (step < steps) & (step % 2 == odd))
        def _(new_ref=new_ref, old_ref=old_ref):
            both(new_ref, old_ref)

        @pl.when((step == steps) & (step % 2 == odd))
        def _(old_ref=old_ref):
            for _ in summing(old_ref):
                pass

    @pl.when(step == 1)
    def _():
        plane_ref[...] = total_ref[...]

    @pl.when((step > 0) & (core == 1))
    def _():
        local_ref[step - 1] = third_ref[0, out_rows - 1]

    @pl.when((step == steps) & (core == 0))
    def _():
        local_ref[...] = third_ref[0]
        local_ref[0] = total_ref[0].astype(BF16)


def layer_three(volume, prior, weights, gain, shift, core):
    _, chans, planes, rows, width = volume.shape
    outs = weights.shape[0]
    half = width // 2
    steps, out_rows = planes // 4, rows // 2
    full = lambda *shape: pl.BlockSpec(shape, lambda i, core: (0,) * len(shape))
    return pl.pallas_call(
        three_kernel,
        grid_spec=pltpu.PrefetchScalarGridSpec(
            num_scalar_prefetch=1,
            grid=(steps + 1,),
            in_specs=[
                pl.BlockSpec((1, chans, 2, rows, width), lambda i, core: (0, 0, core[0] * steps + jnp.minimum(i, steps - 1), 0, 0)),
                pl.BlockSpec(prior.shape, lambda i, core: (0, 0, 0), pipeline_mode=pl.Buffered(1)),
                full(*weights.shape),
                full(half, half),
                full(outs, 1),
                full(outs, 1),
            ],
            out_specs=[
                pl.BlockSpec((1, out_rows, outs, half), lambda i, core: (jnp.maximum(i - 1, 0), 0, 0, 0)),
                full(out_rows, outs, half),
                pl.BlockSpec((1, outs, half), lambda i, core: (jnp.maximum(i - 1, 0), 0, 0)),
                full(out_rows, outs, half),
            ],
            scratch_shapes=[pltpu.VMEM((2, half // LANES, GROUP * rows, LANES), F32)] * 4
            + [
                pltpu.VMEM((rows + 1, 3 * chans, half), BF16),
                pltpu.VMEM((2, rows + 1, 3 * chans, half), BF16),
                pltpu.VMEM((2, rows + 1, 3 * chans, half), BF16),
                pltpu.VMEM((out_rows, outs, half), F32),
            ],
        ),
        out_shape=[
            jax.ShapeDtypeStruct((steps, out_rows, outs, half), BF16),
            jax.ShapeDtypeStruct((out_rows, outs, half), F32),
            jax.ShapeDtypeStruct((steps, outs, half), F32),
            jax.ShapeDtypeStruct((out_rows, outs, half), BF16),
        ],
        compiler_params=pltpu.CompilerParams(vmem_limit_bytes=46 * MIB),
        cost_estimate=pl.CostEstimate(flops=2 * 10**9, bytes_accessed=2 * 10**6, transcendentals=0),
        name="layer_three",
    )(core, volume, prior, weights, even_odd(half), gain, shift)


def corner_total(core, refs):
    _, plane_ref, _, halo_ref, rows_ref, _, _ = refs
    planes = rows_ref.shape[0]
    first = jnp.where(core == 0, rows_ref[0].astype(F32), halo_ref[planes].astype(F32))
    return plane_ref[0] + jnp.where(core == 0, halo_ref[0].astype(F32), 0.0) + first


def third_value(core, refs, plane, row):
    third_ref, plane_ref, row_ref, halo_ref, rows_ref, gain_ref, shift_ref = refs
    planes = rows_ref.shape[0]
    if plane and row:
        return third_ref[plane, row]
    if plane:
        share = jnp.where(core == 0, rows_ref[plane].astype(F32), halo_ref[planes + plane].astype(F32))
        total = row_ref[plane] + share
    elif row:
        total = plane_ref[row] + jnp.where(core == 0, halo_ref[row].astype(F32), 0.0)
    else:
        total = corner_total(core, refs)
    value = activate(total, gain_ref[...], shift_ref[...])
    if not plane and not row:
        value = jnp.where(core == 0, 0.0, value)
    return value.astype(BF16)


def four_edges_kernel(core_ref, *refs):
    *thirds, local_ref, w_ref, place_ref, message_ref, mid_ref = refs
    core = core_ref[0]
    planes, rows, chans, width = thirds[0].shape
    half = width // 2
    out_rows = rows // 2
    taps = 3 * chans
    mid_ref[...] = w_ref[:, 4 * taps : 5 * taps]

    def data(values):
        parts = [part.astype(BF16) for part in spread((jnp.concatenate(values, 0),), place_ref[...])]
        return [
            jnp.concatenate([part[at * chans : (at + 1) * chans] for part in parts], 0) for at in range(len(values))
        ]

    @pl.when(core == 0)
    def _():
        none = jnp.zeros((taps, half), BF16)
        rim = [none] + data(
            [third_value(core, thirds, plane, rows - 1) for plane in range(planes)]
            + [local_ref[plane] for plane in range(planes)]
        )
        pieces = [jnp.concatenate([rim[2 * m + slot] for m in range(planes)], 1) for slot in range(3)]
        weights = jnp.concatenate([w_ref[:, 3 * slot * taps : (3 * slot + 1) * taps] for slot in range(3)], 1)
        total = jnp.dot(weights, jnp.concatenate(pieces, 0), preferred_element_type=F32).astype(BF16)
        for m in range(planes):
            message_ref[m] = total[:, m * half : (m + 1) * half]
        for index in range(planes, message_ref.shape[0]):
            message_ref[index] = jnp.zeros_like(message_ref[index])

    @pl.when(core == 1)
    def _():
        halo_ref = thirds[3]
        last = data(
            [halo_ref[2 * planes + 1]] + [third_value(core, thirds, planes - 1, row) for row in range(rows)]
        )
        for row in range(0, out_rows, 2):
            pieces = [jnp.concatenate([last[2 * row + at], last[2 * row + 2 + at]], 1) for at in range(3)]
            both = jnp.dot(w_ref[:, : 3 * taps], jnp.concatenate(pieces, 0), preferred_element_type=F32)
            both = both.astype(BF16)
            message_ref[row] = both[:, :half]
            message_ref[row + 1] = both[:, half:]
        corner = halo_ref[2 * planes]
        message_ref[out_rows, :chans] = corner[:, :half]
        message_ref[out_rows, chans:] = corner[:, half:]


def four_edges(core, thirds, local, weights):
    planes, rows, chans, width = thirds[0].shape
    outs = weights.shape[0]
    half = width // 2
    return pl.pallas_call(
        four_edges_kernel,
        out_shape=[
            jax.ShapeDtypeStruct((rows // 2 + 1, outs, half), BF16),
            jax.ShapeDtypeStruct((outs, 3 * chans), BF16),
        ],
        in_specs=inputs(len(thirds) + 3),
        compiler_params=pltpu.CompilerParams(vmem_limit_bytes=24 * MIB),
        cost_estimate=pl.CostEstimate(flops=10**9, bytes_accessed=10**6, transcendentals=0),
        name="four_edges",
    )(core, *thirds, local, weights, even_odd(width))


def four_kernel(core_ref, *refs):
    *thirds, local_ref, w_ref, place_ref, own_ref, theirs_ref, corner_ref, data_ref = refs
    core = core_ref[0]
    planes, rows, chans, width = thirds[0].shape
    halo_ref, gain_ref, shift_ref = thirds[3], thirds[5], thirds[6]
    half = width // 2
    out_rows, count = rows // 2, planes // 2
    taps = 3 * chans
    batch = 4
    data_ref[:, 0] = jnp.zeros_like(data_ref[:, 0])
    corner_ref[...] = corner_total(core, thirds)

    def put(values, first, spots):
        for tap, part in enumerate(spread((jnp.concatenate(values, 0),), place_ref[...])):
            part = part.astype(BF16)
            for at in range(len(values)):
                for slot, lanes in spots:
                    data_ref[
                        slot, first + at + 1, tap * chans : (tap + 1) * chans, lanes * half : (lanes + 1) * half
                    ] = part[at * chans : (at + 1) * chans]

    @pl.when(core == 0)
    def _():
        data_ref[0, :, :, :half] = jnp.zeros_like(data_ref[0, :, :, :half])

    @pl.when(core == 1)
    def _():
        total = local_ref[0].astype(F32) + halo_ref[planes - 1].astype(F32)
        prior = [activate(total, gain_ref[...], shift_ref[...]).astype(BF16)]
        prior += [local_ref[row] for row in range(1, rows)]
        for first in range(0, rows, batch):
            put(prior[first : first + batch], first, [(0, 0)])

    for plane in range(planes):
        spots = [(1 + plane % 2, plane // 2)]
        if plane % 2 and plane // 2 + 1 < count:
            spots.append((0, plane // 2 + 1))
        for first in range(0, rows, batch):
            put([third_value(core, thirds, plane, row) for row in range(first, first + batch)], first, spots)
    for row in range(out_rows):
        parts = [data_ref[slot, 2 * row : 2 * row + 3].reshape(3 * taps, count * half) for slot in range(3)]
        total = jnp.dot(w_ref[...], jnp.concatenate(parts, 0), preferred_element_type=F32)
        own_ref[row] = jnp.where(core == 0, total[:LANES], total[LANES:])
        theirs_ref[row] = jnp.where(core == 0, total[LANES:], total[:LANES])


def layer_four(core, thirds, local, weights):
    planes, rows, chans, width = thirds[0].shape
    outs = weights.shape[0]
    half = width // 2
    out_rows, count = rows // 2, planes // 2
    return pl.pallas_call(
        four_kernel,
        out_shape=[
            jax.ShapeDtypeStruct((out_rows, outs // 2, count * half), F32),
            jax.ShapeDtypeStruct((out_rows, outs // 2, count * half), F32),
            jax.ShapeDtypeStruct((chans, width), F32),
        ],
        in_specs=inputs(len(thirds) + 3),
        scratch_shapes=[pltpu.VMEM((3, rows + 1, 3 * chans, count * half), BF16)],
        compiler_params=pltpu.CompilerParams(vmem_limit_bytes=32 * MIB),
        cost_estimate=pl.CostEstimate(flops=2 * 10**9, bytes_accessed=10**6, transcendentals=0),
        name="layer_four",
    )(core, *thirds, local, weights, even_odd(width))


def shares_kernel(core_ref, corner_ref, halo_ref, mid_ref, place_ref, gain_ref, shift_ref, shares_ref, fix_ref):
    core = core_ref[0]
    rows = halo_ref.shape[0] - 1

    @pl.when(core == 0)
    def _():
        corner = halo_ref[rows].astype(F32)
        total = corner_ref[...] + jnp.concatenate([corner[:LANES], corner[LANES:]], 1)
        value = activate(total, gain_ref[...], shift_ref[...]).astype(BF16)
        data = jnp.concatenate([part.astype(BF16) for part in spread((value,), place_ref[...])], 0)
        fix = jnp.dot(mid_ref[...], data, preferred_element_type=F32)
        fix_ref[...] = fix[:LANES]
        shares_ref[...] = halo_ref[:rows, LANES:].astype(F32)
        shares_ref[0] += fix[LANES:]

    @pl.when(core == 1)
    def _():
        fix_ref[...] = jnp.zeros_like(fix_ref)
        shares_ref[...] = halo_ref[:rows, :LANES].astype(F32)


def assemble_kernel(
    core_ref, own_ref, got_ref, halo_ref, fix_ref, scales_ref, shares_ref, out_ref, lines_ref
):
    core = core_ref[0]
    gain, shift = scales_ref[:, 1:2], scales_ref[:, 2:3]
    rows, width = halo_ref.shape[0] - 1, halo_ref.shape[2]
    count = own_ref.shape[2] // width

    def put(row, parts):
        for at, total in enumerate(parts):
            value = activate(total, gain, shift)
            for m in range(count):
                place = row * 2 * count + at * count + m
                lines_ref[pl.ds(place, LANES, stride=rows * 2 * count), :] = value[:, m * width : (m + 1) * width]

    def with_edge(total, edge):
        return jnp.concatenate([total[:, :width] + edge, total[:, width:]], 1)

    @pl.when(core == 0)
    def _():
        for row in range(rows):
            edge = halo_ref[row, :LANES].astype(F32)
            if not row:
                edge = edge + fix_ref[...]
            total, got = with_edge(own_ref[row], edge), got_ref[row]
            if not row:
                first = [shares_ref[m] for m in range(2 * count)]
                total = total + jnp.concatenate(first[:count], 1)
                got = got + jnp.concatenate(first[count:], 1)
            put(row, (total, got))

    @pl.when(core == 1)
    def _():
        for row in range(rows):
            total, got = own_ref[row], with_edge(got_ref[row], shares_ref[row])
            if not row:
                first = [halo_ref[m, LANES:].astype(F32) for m in range(2 * count)]
                total = total + jnp.concatenate(first[count:], 1)
                got = got + jnp.concatenate(first[:count], 1)
            put(row, (got, total))

    out_ref[...] = lines_ref[...].astype(BF16)


def last_stage(core, own, theirs, corner, halo, mid, gain, shift, scales):
    rows, outs, lanes = own.shape
    got = swapped(theirs)
    shares, fix = pl.pallas_call(
        shares_kernel,
        out_shape=[
            jax.ShapeDtypeStruct((rows, outs, halo.shape[2]), F32),
            jax.ShapeDtypeStruct((outs, halo.shape[2]), F32),
        ],
        in_specs=inputs(6),
        compiler_params=pltpu.CompilerParams(vmem_limit_bytes=16 * MIB),
        cost_estimate=pl.CostEstimate(flops=10**8, bytes_accessed=10**6, transcendentals=0),
        name="shares",
    )(core, corner, halo, mid, even_odd(lanes), gain, shift)
    lines = (outs * rows * lanes * 2 // LANES, LANES)
    return pl.pallas_call(
        assemble_kernel,
        out_shape=jax.ShapeDtypeStruct(lines, BF16),
        in_specs=inputs(6),
        scratch_shapes=[pltpu.VMEM(lines, F32)],
        compiler_params=pltpu.CompilerParams(vmem_limit_bytes=16 * MIB),
        name="assemble",
    )(core, own, got, halo, fix, scales, swapped(shares))


def handed_on(message):
    count = lax.axis_size("sp")
    pairs = [(2 * b, 2 * (b + 1) + 1) for b in range(count) if b % ROW_BLOCKS != ROW_BLOCKS - 1]
    pairs += [(2 * b + 1, 2 * (b + ROW_BLOCKS)) for b in range(count - ROW_BLOCKS)]
    return lax.ppermute(message, ("sp", "fl"), pairs)


def swapped(value):
    return lax.ppermute(value, "fl", [(0, 1), (1, 0)])


def shards(volume, kernel_three, gain_three, shift_three, kernel_four, gain_four, shift_four):
    core = lax.axis_index("fl").reshape(1)
    own_scales = jnp.concatenate([gain_three, shift_three, gain_four, shift_four]).reshape(-1, LANES)
    picked, prior = three_picks(volume, core)
    message, weights_three, gain, shift, scales = three_edges(
        picked, kernel_three, swapped(kernel_three), own_scales, swapped(own_scales), core
    )
    halo = handed_on(message)
    *thirds, local = layer_three(volume, prior, weights_three, gain, shift, core)
    rows = lax.ppermute(halo[: thirds[0].shape[0]], "fl", [(1, 0)])
    thirds = (*thirds, halo, rows, gain, shift)
    local = swapped(local)
    weights_four = four_weights(kernel_four, swapped(kernel_four), core)
    message, mid = four_edges(core, thirds, local, weights_four)
    halo = handed_on(message)
    own, theirs, corner = layer_four(core, thirds, local, weights_four)
    lines = last_stage(core, own, theirs, corner, halo, mid, gain, shift, scales)
    out_rows, outs, lanes = own.shape
    fourth = lines.reshape(outs, out_rows, 2 * lanes // LANES, LANES)
    return jnp.transpose(fourth, (0, 2, 1, 3))[None]


def solution(mesh):
    return jax.shard_map(
        shards,
        mesh=mesh,
        in_specs=(
            P("sp", None, None, None, None),
            P("fl", None),
            P("fl"),
            P("fl"),
            P("fl", None),
            P("fl"),
            P("fl"),
        ),
        out_specs=P("sp", "fl", None, None, None),
        check_vma=False,
    )
```

```python
import functools

import jax
import jax.numpy as jnp
import numpy as np
from jax import lax
from jax.experimental import pallas as pl
from jax.experimental.pallas import tpu as pltpu
from jax.sharding import PartitionSpec as P

F32 = jnp.float32
BF16 = jnp.bfloat16
LANES = 128
ROW_BLOCKS = 8
SUB = 8
TAPS = 27
RIM_TAPS = tuple(9 * a + e for a in range(3) for e in range(3))
GROUP = 16
MIB = 2**20


def even_odd(width):
    half = width // 2
    place = np.zeros((width, width), np.float32)
    place[np.arange(0, width, 2), np.arange(half)] = 1
    place[np.arange(1, width, 2), half + np.arange(half)] = 1
    return jnp.asarray(place, BF16)


def activate(total, gain, shift):
    return jnp.maximum(total * gain + shift, 0.0)


def shifted(odd):
    lane = lax.broadcasted_iota(jnp.int32, odd.shape, 1)
    return jnp.where(lane == 0, 0.0, pltpu.roll(odd, 1, 1))


def spread(sides, place):
    quarter = place.shape[0] // 2
    split = [jnp.dot(side, place, preferred_element_type=F32) for side in sides]
    even = jnp.concatenate([part[:, :quarter] for part in split], 1)
    odd = jnp.concatenate([part[:, quarter:] for part in split], 1)
    return shifted(odd), even, odd


def separate(x_ref, plane, place_ref, split_refs, store):
    chans, rows, width = x_ref.shape[1], x_ref.shape[3], x_ref.shape[4]
    half = width // 2
    quarter = half // 2
    for index, first in enumerate(range(0, chans, GROUP)):
        split_ref = split_refs[index % len(split_refs)]
        x = x_ref[0, pl.ds(first, GROUP), plane]
        x = x.astype(F32).reshape(GROUP * rows, width).astype(BF16)
        for side in range(2):
            parts = jnp.dot(
                x[:, side * half : (side + 1) * half], place_ref[...], preferred_element_type=F32
            )
            for block in range(half // LANES):
                odd, at = divmod(block, quarter // LANES)
                split_ref[odd, side * (quarter // LANES) + at] = parts[:, block * LANES : (block + 1) * LANES]
        for row in range(rows):
            even, odd = (
                jnp.concatenate(
                    [split_ref[odd, at, pl.ds(row, GROUP, stride=rows), :] for at in range(half // LANES)], 1
                )
                for odd in range(2)
            )
            for tap, value in enumerate((shifted(odd), even, odd)):
                store(tap, row, first, value.astype(BF16))
        yield


def inputs(count):
    return [pl.BlockSpec(memory_space=pltpu.SMEM)] + [pl.BlockSpec(memory_space=pltpu.VMEM)] * count


def whole(own, other, core):
    first = jnp.where(core == 0, own, other)
    second = jnp.where(core == 0, other, own)
    return jnp.concatenate([first, second], 0)


def turn(kernel, turned_ref):
    columns = kernel.shape[1]
    for at in range(0, columns, LANES):
        size = min(LANES, columns - at)
        turned_ref[at : at + size, :] = kernel[:, at : at + size].T


def tap_major(turned_ref, taps, w_ref, first):
    chans = turned_ref.shape[0] // TAPS
    at = 0
    for index in range(0, len(taps), LANES // chans):
        parts = [turned_ref[pl.ds(tap, chans, stride=TAPS), :] for tap in taps[index : index + LANES // chans]]
        block = jnp.concatenate(parts, 0).T.astype(BF16)
        w_ref[first : first + LANES, at : at + block.shape[1]] = block
        at += block.shape[1]


def four_weights_kernel(core_ref, own_ref, other_ref, w_ref, *turned_refs):
    core = core_ref[0]
    for index, turned_ref in enumerate(turned_refs):
        turn(jnp.where(core == index, own_ref[...].astype(F32), other_ref[...].astype(F32)), turned_ref)
        tap_major(turned_ref, range(TAPS), w_ref, index * LANES)


def four_weights(own, other, core):
    outs, columns = own.shape
    return pl.pallas_call(
        four_weights_kernel,
        out_shape=jax.ShapeDtypeStruct((2 * outs, columns), BF16),
        in_specs=[
            pl.BlockSpec(memory_space=pltpu.SMEM),
            pl.BlockSpec(memory_space=pltpu.VMEM),
            pl.BlockSpec(memory_space=pltpu.VMEM),
        ],
        scratch_shapes=[pltpu.VMEM((columns, LANES), F32)] * 2,
        compiler_params=pltpu.CompilerParams(vmem_limit_bytes=16 * MIB),
        cost_estimate=pl.CostEstimate(flops=10**3, bytes_accessed=10**3, transcendentals=0),
        name="four_weights",
    )(core, own, other)


def three_picks_kernel(core_ref, last_ref, before_ref, rim_ref, place_ref, picked_ref, prior_ref, *scratch):
    *split_refs, pick_ref = scratch
    core, step, last = core_ref[0], pl.program_id(0), pl.num_programs(0) - 1
    chans, block, width = rim_ref.shape[1], rim_ref.shape[2], rim_ref.shape[4]
    rows, part = last_ref.shape[3], last_ref.shape[1]
    planes = block * 4
    half = width // 2
    rim = (rows - 1) % SUB

    def picked(spots):
        values, held = [], None
        for plane, row in spots:
            if plane != held:
                x = rim_ref[0, :, plane, :SUB].astype(F32).reshape(chans * SUB, width)
                for at in range(width // LANES):
                    pick_ref[plane % 2, at] = x[:, at * LANES : (at + 1) * LANES]
                held = plane
            values.append(
                jnp.concatenate(
                    [pick_ref[plane % 2, at, pl.ds(row, chans, stride=SUB), :] for at in range(width // LANES)], 1
                ).astype(BF16)
            )
        values = jnp.concatenate(values, 0)
        parts = [part.astype(BF16) for part in spread((values[:, :half], values[:, half:]), place_ref[...])]
        return [
            jnp.concatenate([part[at * chans : (at + 1) * chans] for part in parts], 0) for at in range(len(spots))
        ]

    @pl.when(core == 0)
    def _():
        for plane, data in enumerate(picked([(plane, rim) for plane in range(block)])):
            picked_ref[step * block + plane] = data

    @pl.when((core == 0) & (step == last))
    def _():
        spots = [(plane, row) for plane in range(block - 3, block) for row in range(rim - 2, rim + 1)]
        for index, data in enumerate(picked(spots)):
            picked_ref[planes + index] = data
        prior_ref[...] = jnp.zeros_like(prior_ref)

    @pl.when(core == 1)
    def _():
        for source_ref, to_ref in ((last_ref, picked_ref), (before_ref, prior_ref)):

            def store(tap, row, first, value):
                at = pl.multiple_of(tap * chans + step * part + first, GROUP)
                to_ref[row + 1, pl.ds(at, GROUP), :] = value

            for _ in separate(source_ref, 0, place_ref, split_refs, store):
                pass

    @pl.when((core == 1) & (step == last))
    def _():
        for ref in (picked_ref, prior_ref):
            ref[0] = jnp.zeros_like(ref[0])


def three_picks(volume, core):
    _, chans, planes, rows, width = volume.shape
    half = width // 2
    block, steps = planes // 4, 4
    shape = (rows + 1, 3 * chans, half)
    full = lambda *shape: pl.BlockSpec(shape, lambda i, core: (0,) * len(shape))
    return pl.pallas_call(
        three_picks_kernel,
        grid_spec=pltpu.PrefetchScalarGridSpec(
            num_scalar_prefetch=1,
            grid=(steps,),
            in_specs=[
                pl.BlockSpec((1, chans // steps, 1, rows, width), lambda i, core: (0, i * core[0], planes - 1, 0, 0)),
                pl.BlockSpec(
                    (1, chans // steps, 1, rows, width), lambda i, core: (0, i * core[0], planes // 2 - 1, 0, 0)
                ),
                pl.BlockSpec(
                    (1, chans, block, 2 * SUB, width),
                    lambda i, core: (0, 0, i + core[0] * (steps - 1 - i), (rows - 1) // (2 * SUB), 0),
                ),
                full(half, half),
            ],
            out_specs=[full(*shape), full(*shape)],
            scratch_shapes=[pltpu.VMEM((2, half // LANES, GROUP * rows, LANES), F32)] * 2
            + [pltpu.VMEM((2, width // LANES, chans * SUB, LANES), F32)],
        ),
        out_shape=[jax.ShapeDtypeStruct(shape, BF16)] * 2,
        compiler_params=pltpu.CompilerParams(vmem_limit_bytes=36 * MIB),
        cost_estimate=pl.CostEstimate(flops=10**9, bytes_accessed=10**7, transcendentals=0),
        name="three_picks",
    )(core, volume, volume, volume, even_odd(half))


def three_edges_kernel(
    core_ref, picked_ref, own_ref, other_ref, own_scales_ref, other_scales_ref,
    message_ref, w_ref, gain_ref, shift_ref, scales_ref,
    turned_ref, rim_w_ref,
):
    core = core_ref[0]
    count, taps, half = picked_ref.shape
    out_rows = message_ref.shape[0]
    planes = count - 9
    turn(whole(own_ref[...].astype(F32), other_ref[...].astype(F32), core), turned_ref)
    tap_major(turned_ref, range(TAPS), w_ref, 0)
    own_scales, other_scales = own_scales_ref[...], other_scales_ref[...]
    lines = own_scales.shape[0]
    scales = jnp.concatenate([own_scales, other_scales, jnp.zeros((LANES - 2 * lines, LANES), F32)], 0).T
    scales_ref[...] = scales
    share = own_ref.shape[0]
    for ref, at in ((gain_ref, 0), (shift_ref, share)):
        ref[...] = whole(scales[at : at + share, 0:1], scales[at : at + share, lines : lines + 1], core)

    @pl.when(core == 0)
    def _():
        tap_major(turned_ref, RIM_TAPS, rim_w_ref, 0)
        none = jnp.zeros((taps, half), BF16)
        for index in range(planes // 2 + 1):
            pieces = [
                picked_ref[plane] if 0 <= plane < planes else none for plane in range(2 * index - 1, 2 * index + 2)
            ]
            total = jnp.dot(rim_w_ref[...], jnp.concatenate(pieces, 0), preferred_element_type=F32)
            message_ref[index] = total.astype(BF16)
        data = picked_ref[planes:].reshape(9 * taps, half)
        total = jnp.dot(w_ref[...], data, preferred_element_type=F32)
        message_ref[planes // 2 + 1] = activate(total, gain_ref[...], shift_ref[...]).astype(BF16)
        for index in range(planes // 2 + 2, out_rows):
            message_ref[index] = jnp.zeros_like(message_ref[index])

    @pl.when(core == 1)
    def _():
        for row in range(out_rows):
            total = jnp.dot(
                w_ref[:, : 3 * taps],
                picked_ref[2 * row : 2 * row + 3].reshape(3 * taps, half),
                preferred_element_type=F32,
            )
            message_ref[row] = total.astype(BF16)


def three_edges(picked, own, other, own_scales, other_scales, core):
    outs, columns = 2 * own.shape[0], own.shape[1]
    out_rows, half = picked.shape[0] // 2, picked.shape[2]
    shapes = [
        ((out_rows, outs, half), BF16),
        ((outs, columns), BF16),
        ((outs, 1), F32),
        ((outs, 1), F32),
        ((LANES, LANES), F32),
    ]
    return pl.pallas_call(
        three_edges_kernel,
        in_specs=inputs(5),
        out_shape=[jax.ShapeDtypeStruct(*shape) for shape in shapes],
        scratch_shapes=[pltpu.VMEM((columns, LANES), F32), pltpu.VMEM((outs, columns // 3), BF16)],
        compiler_params=pltpu.CompilerParams(vmem_limit_bytes=16 * MIB),
        cost_estimate=pl.CostEstimate(flops=10**9, bytes_accessed=10**6, transcendentals=0),
        name="three_edges",
    )(core, picked, own, other, own_scales, other_scales)


def three_kernel(
    core_ref, x_ref, before_ref, w_ref, place_ref, gain_ref, shift_ref,
    third_ref, plane_ref, row_ref, local_ref,
    *scratch,
):
    *split_refs, prior_ref, first_ref, second_ref, total_ref = scratch
    core, step, steps = core_ref[0], pl.program_id(0), pl.num_programs(0) - 1
    chans, rows, width = x_ref.shape[1], x_ref.shape[3], x_ref.shape[4]
    half = width // 2
    out_rows = rows // 2
    taps = 3 * chans

    def splitting(pair_ref):
        for plane in range(2):

            def store(tap, row, first, value, plane=plane):
                pair_ref[plane, row + 1, tap * chans + first : tap * chans + first + GROUP, :] = value

            yield from separate(x_ref, plane, place_ref, split_refs, store)

    def summing(pair_ref):
        gain, shift = gain_ref[...], shift_ref[...]
        for row in range(out_rows):
            parts = [
                ref[2 * row : 2 * row + 3].reshape(3 * taps, half)
                for ref in (prior_ref, pair_ref.at[0], pair_ref.at[1])
            ]
            total = jnp.dot(w_ref[...], jnp.concatenate(parts, 0), preferred_element_type=F32)
            third_ref[0, row] = activate(total, gain, shift).astype(BF16)
            total_ref[row] = total
            yield
        row_ref[0] = total_ref[0]
        prior_ref[...] = pair_ref[1]
        yield

    @pl.when(step == 0)
    def _():
        prior_ref[...] = before_ref[...]
        for ref in (first_ref, second_ref):
            ref[:, 0] = jnp.zeros_like(ref[:, 0])
        for _ in splitting(first_ref):
            pass

    def both(new_ref, old_ref):
        new, old = splitting(new_ref), summing(old_ref)
        for turn in range(2 * chans // GROUP):
            next(new, None)
            for _ in range(out_rows * (turn + 1) // (2 * chans // GROUP) - out_rows * turn // (2 * chans // GROUP)):
                next(old, None)
        for _ in new:
            pass
        for _ in old:
            pass

    for odd, (new_ref, old_ref) in enumerate(((first_ref, second_ref), (second_ref, first_ref))):

        @pl.when((step > 0) & (step < steps) & (step % 2 == odd))
        def _(new_ref=new_ref, old_ref=old_ref):
            both(new_ref, old_ref)

        @pl.when((step == steps) & (step % 2 == odd))
        def _(old_ref=old_ref):
            for _ in summing(old_ref):
                pass

    @pl.when(step == 1)
    def _():
        plane_ref[...] = total_ref[...]

    @pl.when((step > 0) & (core == 1))
    def _():
        local_ref[step - 1] = third_ref[0, out_rows - 1]

    @pl.when((step == steps) & (core == 0))
    def _():
        local_ref[...] = third_ref[0]
        local_ref[0] = total_ref[0].astype(BF16)


def layer_three(volume, prior, weights, gain, shift, core):
    _, chans, planes, rows, width = volume.shape
    outs = weights.shape[0]
    half = width // 2
    steps, out_rows = planes // 4, rows // 2
    full = lambda *shape: pl.BlockSpec(shape, lambda i, core: (0,) * len(shape))
    return pl.pallas_call(
        three_kernel,
        grid_spec=pltpu.PrefetchScalarGridSpec(
            num_scalar_prefetch=1,
            grid=(steps + 1,),
            in_specs=[
                pl.BlockSpec((1, chans, 2, rows, width), lambda i, core: (0, 0, core[0] * steps + jnp.minimum(i, steps - 1), 0, 0)),
                pl.BlockSpec(prior.shape, lambda i, core: (0, 0, 0), pipeline_mode=pl.Buffered(1)),
                full(*weights.shape),
                full(half, half),
                full(outs, 1),
                full(outs, 1),
            ],
            out_specs=[
                pl.BlockSpec((1, out_rows, outs, half), lambda i, core: (jnp.maximum(i - 1, 0), 0, 0, 0)),
                full(out_rows, outs, half),
                pl.BlockSpec((1, outs, half), lambda i, core: (jnp.maximum(i - 1, 0), 0, 0)),
                full(out_rows, outs, half),
            ],
            scratch_shapes=[pltpu.VMEM((2, half // LANES, GROUP * rows, LANES), F32)] * 4
            + [
                pltpu.VMEM((rows + 1, 3 * chans, half), BF16),
                pltpu.VMEM((2, rows + 1, 3 * chans, half), BF16),
                pltpu.VMEM((2, rows + 1, 3 * chans, half), BF16),
                pltpu.VMEM((out_rows, outs, half), F32),
            ],
        ),
        out_shape=[
            jax.ShapeDtypeStruct((steps, out_rows, outs, half), BF16),
            jax.ShapeDtypeStruct((out_rows, outs, half), F32),
            jax.ShapeDtypeStruct((steps, outs, half), F32),
            jax.ShapeDtypeStruct((out_rows, outs, half), BF16),
        ],
        compiler_params=pltpu.CompilerParams(vmem_limit_bytes=46 * MIB),
        cost_estimate=pl.CostEstimate(flops=10**10, bytes_accessed=2 * 10**7, transcendentals=0),
        name="layer_three",
    )(core, volume, prior, weights, even_odd(half), gain, shift)


def corner_total(core, refs, rows_ref):
    third_ref, plane_ref, _, halo_ref, _, _ = refs
    planes = third_ref.shape[0]
    first = jnp.where(core == 0, rows_ref[0].astype(F32), halo_ref[planes].astype(F32))
    return plane_ref[0] + jnp.where(core == 0, halo_ref[0].astype(F32), 0.0) + first


def third_value(core, refs, plane, row, rows_ref=None):
    third_ref, plane_ref, row_ref, halo_ref, gain_ref, shift_ref = refs
    planes = third_ref.shape[0]
    if plane and row:
        return third_ref[plane, row]
    if plane:
        share = halo_ref[planes + plane].astype(F32)
        if rows_ref is not None:
            share = jnp.where(core == 0, rows_ref[plane].astype(F32), share)
        total = row_ref[plane] + share
    elif row:
        total = plane_ref[row] + jnp.where(core == 0, halo_ref[row].astype(F32), 0.0)
    else:
        total = corner_total(core, refs, rows_ref)
    value = activate(total, gain_ref[...], shift_ref[...])
    if not plane and not row:
        value = jnp.where(core == 0, 0.0, value)
    return value.astype(BF16)


def four_edges_kernel(core_ref, *refs):
    *thirds, local_ref, w_ref, place_ref, message_ref, mid_ref, rows_ref = refs
    core = core_ref[0]
    planes, rows, chans, width = thirds[0].shape
    rows_ref[...] = thirds[3][:planes]
    half = width // 2
    out_rows = rows // 2
    taps = 3 * chans
    mid_ref[...] = w_ref[:, 4 * taps : 5 * taps]

    def data(values):
        parts = [part.astype(BF16) for part in spread((jnp.concatenate(values, 0),), place_ref[...])]
        return [
            jnp.concatenate([part[at * chans : (at + 1) * chans] for part in parts], 0) for at in range(len(values))
        ]

    @pl.when(core == 0)
    def _():
        none = jnp.zeros((taps, half), BF16)
        rim = [none] + data(
            [third_value(core, thirds, plane, rows - 1) for plane in range(planes)]
            + [local_ref[plane] for plane in range(planes)]
        )
        pieces = [jnp.concatenate([rim[2 * m + slot] for m in range(planes)], 1) for slot in range(3)]
        weights = jnp.concatenate([w_ref[:, 3 * slot * taps : (3 * slot + 1) * taps] for slot in range(3)], 1)
        total = jnp.dot(weights, jnp.concatenate(pieces, 0), preferred_element_type=F32).astype(BF16)
        for m in range(planes):
            message_ref[m] = total[:, m * half : (m + 1) * half]
        for index in range(planes, message_ref.shape[0]):
            message_ref[index] = jnp.zeros_like(message_ref[index])

    @pl.when(core == 1)
    def _():
        halo_ref = thirds[3]
        last = data(
            [halo_ref[2 * planes + 1]] + [third_value(core, thirds, planes - 1, row) for row in range(rows)]
        )
        for row in range(0, out_rows, 2):
            pieces = [jnp.concatenate([last[2 * row + at], last[2 * row + 2 + at]], 1) for at in range(3)]
            both = jnp.dot(w_ref[:, : 3 * taps], jnp.concatenate(pieces, 0), preferred_element_type=F32)
            both = both.astype(BF16)
            message_ref[row] = both[:, :half]
            message_ref[row + 1] = both[:, half:]
        corner = halo_ref[2 * planes]
        message_ref[out_rows, :chans] = corner[:, :half]
        message_ref[out_rows, chans:] = corner[:, half:]


def four_edges(core, thirds, local, weights):
    planes, rows, chans, width = thirds[0].shape
    outs = weights.shape[0]
    half = width // 2
    return pl.pallas_call(
        four_edges_kernel,
        out_shape=[
            jax.ShapeDtypeStruct((rows // 2 + 1, outs, half), BF16),
            jax.ShapeDtypeStruct((outs, 3 * chans), BF16),
            jax.ShapeDtypeStruct((planes, chans, width), BF16),
        ],
        in_specs=inputs(len(thirds) + 3),
        compiler_params=pltpu.CompilerParams(vmem_limit_bytes=24 * MIB),
        cost_estimate=pl.CostEstimate(flops=10**9, bytes_accessed=10**6, transcendentals=0),
        name="four_edges",
    )(core, *thirds, local, weights, even_odd(width))


def four_kernel(core_ref, *refs):
    *thirds, rows_ref, local_ref, w_ref, place_ref, own_ref, theirs_ref, corner_ref, data_ref = refs
    core = core_ref[0]
    planes, rows, chans, width = thirds[0].shape
    halo_ref, gain_ref, shift_ref = thirds[3:]
    half = width // 2
    out_rows, count = rows // 2, planes // 2
    taps = 3 * chans
    batch = 4
    data_ref[:, 0] = jnp.zeros_like(data_ref[:, 0])
    corner_ref[...] = corner_total(core, thirds, rows_ref)

    def put(values, first, spots):
        for tap, part in enumerate(spread((jnp.concatenate(values, 0),), place_ref[...])):
            part = part.astype(BF16)
            for at in range(len(values)):
                for slot, lanes in spots:
                    data_ref[
                        slot, first + at + 1, tap * chans : (tap + 1) * chans, lanes * half : (lanes + 1) * half
                    ] = part[at * chans : (at + 1) * chans]

    @pl.when(core == 0)
    def _():
        data_ref[0, :, :, :half] = jnp.zeros_like(data_ref[0, :, :, :half])

    @pl.when(core == 1)
    def _():
        total = local_ref[0].astype(F32) + halo_ref[planes - 1].astype(F32)
        prior = [activate(total, gain_ref[...], shift_ref[...]).astype(BF16)]
        prior += [local_ref[row] for row in range(1, rows)]
        for first in range(0, rows, batch):
            put(prior[first : first + batch], first, [(0, 0)])

    for plane in range(planes):
        spots = [(1 + plane % 2, plane // 2)]
        if plane % 2 and plane // 2 + 1 < count:
            spots.append((0, plane // 2 + 1))
        for first in range(0, rows, batch):
            put([third_value(core, thirds, plane, row, rows_ref) for row in range(first, first + batch)], first, spots)
    for row in range(out_rows):
        parts = [data_ref[slot, 2 * row : 2 * row + 3].reshape(3 * taps, count * half) for slot in range(3)]
        total = jnp.dot(w_ref[...], jnp.concatenate(parts, 0), preferred_element_type=F32)
        own_ref[row] = jnp.where(core == 0, total[:LANES], total[LANES:])
        theirs_ref[row] = jnp.where(core == 0, total[LANES:], total[:LANES])


def layer_four(core, thirds, rows_before, local, weights):
    planes, rows, chans, width = thirds[0].shape
    outs = weights.shape[0]
    half = width // 2
    out_rows, count = rows // 2, planes // 2
    return pl.pallas_call(
        four_kernel,
        out_shape=[
            jax.ShapeDtypeStruct((out_rows, outs // 2, count * half), F32),
            jax.ShapeDtypeStruct((out_rows, outs // 2, count * half), F32),
            jax.ShapeDtypeStruct((chans, width), F32),
        ],
        in_specs=inputs(len(thirds) + 4),
        scratch_shapes=[pltpu.VMEM((3, rows + 1, 3 * chans, count * half), BF16)],
        compiler_params=pltpu.CompilerParams(vmem_limit_bytes=32 * MIB),
        cost_estimate=pl.CostEstimate(flops=4 * 10**9, bytes_accessed=4 * 10**6, transcendentals=0),
        name="layer_four",
    )(core, *thirds, rows_before, local, weights, even_odd(width))


def shares_kernel(core_ref, corner_ref, halo_ref, mid_ref, place_ref, gain_ref, shift_ref, shares_ref, fix_ref):
    core = core_ref[0]
    rows = halo_ref.shape[0] - 1

    @pl.when(core == 0)
    def _():
        corner = halo_ref[rows].astype(F32)
        total = corner_ref[...] + jnp.concatenate([corner[:LANES], corner[LANES:]], 1)
        value = activate(total, gain_ref[...], shift_ref[...]).astype(BF16)
        data = jnp.concatenate([part.astype(BF16) for part in spread((value,), place_ref[...])], 0)
        fix = jnp.dot(mid_ref[...], data, preferred_element_type=F32)
        fix_ref[...] = fix[:LANES]
        shares_ref[...] = halo_ref[:rows, LANES:].astype(F32)
        shares_ref[0] += fix[LANES:]

    @pl.when(core == 1)
    def _():
        fix_ref[...] = jnp.zeros_like(fix_ref)
        shares_ref[...] = halo_ref[:rows, :LANES].astype(F32)


def assemble_kernel(
    core_ref, own_ref, got_ref, halo_ref, fix_ref, scales_ref, shares_ref, out_ref, lines_ref
):
    core = core_ref[0]
    gain, shift = scales_ref[:, 1:2], scales_ref[:, 2:3]
    rows, width = halo_ref.shape[0] - 1, halo_ref.shape[2]
    count = own_ref.shape[2] // width

    def put(row, parts):
        for at, total in enumerate(parts):
            value = activate(total, gain, shift)
            for m in range(count):
                place = row * 2 * count + at * count + m
                lines_ref[pl.ds(place, LANES, stride=rows * 2 * count), :] = value[:, m * width : (m + 1) * width]

    def with_edge(total, edge):
        return jnp.concatenate([total[:, :width] + edge, total[:, width:]], 1)

    @pl.when(core == 0)
    def _():
        for row in range(rows):
            edge = halo_ref[row, :LANES].astype(F32)
            if not row:
                edge = edge + fix_ref[...]
            total, got = with_edge(own_ref[row], edge), got_ref[row]
            if not row:
                first = [shares_ref[m] for m in range(2 * count)]
                total = total + jnp.concatenate(first[:count], 1)
                got = got + jnp.concatenate(first[count:], 1)
            put(row, (total, got))

    @pl.when(core == 1)
    def _():
        for row in range(rows):
            total, got = own_ref[row], with_edge(got_ref[row], shares_ref[row])
            if not row:
                first = [halo_ref[m, LANES:].astype(F32) for m in range(2 * count)]
                total = total + jnp.concatenate(first[count:], 1)
                got = got + jnp.concatenate(first[:count], 1)
            put(row, (got, total))

    out_ref[...] = lines_ref[...].astype(BF16)


def last_stage(core, own, theirs, corner, halo, mid, gain, shift, scales):
    rows, outs, lanes = own.shape
    got = swapped(theirs)
    shares, fix = pl.pallas_call(
        shares_kernel,
        out_shape=[
            jax.ShapeDtypeStruct((rows, outs, halo.shape[2]), F32),
            jax.ShapeDtypeStruct((outs, halo.shape[2]), F32),
        ],
        in_specs=inputs(6),
        compiler_params=pltpu.CompilerParams(vmem_limit_bytes=16 * MIB),
        cost_estimate=pl.CostEstimate(flops=10**8, bytes_accessed=10**6, transcendentals=0),
        name="shares",
    )(core, corner, halo, mid, even_odd(lanes), gain, shift)
    lines = (outs * rows * lanes * 2 // LANES, LANES)
    return pl.pallas_call(
        assemble_kernel,
        out_shape=jax.ShapeDtypeStruct(lines, BF16),
        in_specs=inputs(6),
        scratch_shapes=[pltpu.VMEM(lines, F32)],
        compiler_params=pltpu.CompilerParams(vmem_limit_bytes=16 * MIB),
        name="assemble",
    )(core, own, got, halo, fix, scales, swapped(shares))


def handed_on(message):
    count = lax.axis_size("sp")
    pairs = [(2 * b, 2 * (b + 1) + 1) for b in range(count) if b % ROW_BLOCKS != ROW_BLOCKS - 1]
    pairs += [(2 * b + 1, 2 * (b + ROW_BLOCKS)) for b in range(count - ROW_BLOCKS)]
    return lax.ppermute(message, ("sp", "fl"), pairs)


def swapped(value):
    return lax.ppermute(value, "fl", [(0, 1), (1, 0)])


def shards(volume, kernel_three, gain_three, shift_three, kernel_four, gain_four, shift_four):
    core = lax.axis_index("fl").reshape(1)
    own_scales = jnp.concatenate([gain_three, shift_three, gain_four, shift_four]).reshape(-1, LANES)
    picked, prior = three_picks(volume, core)
    others = lax.optimization_barrier((swapped(kernel_three), swapped(own_scales), swapped(kernel_four)))
    message, weights_three, gain, shift, scales = three_edges(
        picked, kernel_three, others[0], own_scales, others[1], core
    )
    halo = handed_on(message)
    *thirds, local = layer_three(volume, prior, weights_three, gain, shift, core)
    halo, local = lax.optimization_barrier((halo, local))
    thirds = (*thirds, halo, gain, shift)
    local = swapped(local)
    weights_four = four_weights(kernel_four, others[2], core)
    message, mid, rows = four_edges(core, thirds, local, weights_four)
    halo = handed_on(message)
    rows = lax.ppermute(rows, "fl", [(1, 0)])
    own, theirs, corner = layer_four(core, thirds, rows, local, weights_four)
    lines = last_stage(core, own, theirs, corner, halo, mid, gain, shift, scales)
    out_rows, outs, lanes = own.shape
    fourth = lines.reshape(outs, out_rows, 2 * lanes // LANES, LANES)
    return jnp.transpose(fourth, (0, 2, 1, 3))[None]


def solution(mesh):
    return jax.shard_map(
        shards,
        mesh=mesh,
        in_specs=(
            P("sp", None, None, None, None),
            P("fl", None),
            P("fl"),
            P("fl"),
            P("fl", None),
            P("fl"),
            P("fl"),
        ),
        out_specs=P("sp", "fl", None, None, None),
        check_vma=False,
    )
```

```python
import functools

import jax
import jax.numpy as jnp
import numpy as np
from jax import lax
from jax.experimental import pallas as pl
from jax.experimental.pallas import tpu as pltpu
from jax.sharding import PartitionSpec as P

F32 = jnp.float32
BF16 = jnp.bfloat16
LANES = 128
ROW_BLOCKS = 8
SUB = 8
TAPS = 27
RIM_TAPS = tuple(9 * a + e for a in range(3) for e in range(3))
GROUP = 16
MIB = 2**20


def even_odd(width):
    half = width // 2
    place = np.zeros((width, width), np.float32)
    place[np.arange(0, width, 2), np.arange(half)] = 1
    place[np.arange(1, width, 2), half + np.arange(half)] = 1
    return jnp.asarray(place, BF16)


def activate(total, gain, shift):
    return jnp.maximum(total * gain + shift, 0.0)


def shifted(odd):
    lane = lax.broadcasted_iota(jnp.int32, odd.shape, 1)
    return jnp.where(lane == 0, 0.0, pltpu.roll(odd, 1, 1))


def spread(sides, place):
    quarter = place.shape[0] // 2
    split = [jnp.dot(side, place, preferred_element_type=F32) for side in sides]
    even = jnp.concatenate([part[:, :quarter] for part in split], 1)
    odd = jnp.concatenate([part[:, quarter:] for part in split], 1)
    return shifted(odd), even, odd


def separate(x_ref, plane, place_ref, split_refs, store):
    chans, rows, width = x_ref.shape[1], x_ref.shape[3], x_ref.shape[4]
    half = width // 2
    quarter = half // 2
    for index, first in enumerate(range(0, chans, GROUP)):
        split_ref = split_refs[index % len(split_refs)]
        x = x_ref[0, pl.ds(first, GROUP), plane]
        x = x.astype(F32).reshape(GROUP * rows, width).astype(BF16)
        for side in range(2):
            parts = jnp.dot(
                x[:, side * half : (side + 1) * half], place_ref[...], preferred_element_type=F32
            )
            for block in range(half // LANES):
                odd, at = divmod(block, quarter // LANES)
                split_ref[odd, side * (quarter // LANES) + at] = parts[:, block * LANES : (block + 1) * LANES]
        for row in range(rows):
            even, odd = (
                jnp.concatenate(
                    [split_ref[odd, at, pl.ds(row, GROUP, stride=rows), :] for at in range(half // LANES)], 1
                )
                for odd in range(2)
            )
            for tap, value in enumerate((shifted(odd), even, odd)):
                store(tap, row, first, value.astype(BF16))
        yield


def inputs(count):
    return [pl.BlockSpec(memory_space=pltpu.SMEM)] + [pl.BlockSpec(memory_space=pltpu.VMEM)] * count


def whole(own, other, core):
    first = jnp.where(core == 0, own, other)
    second = jnp.where(core == 0, other, own)
    return jnp.concatenate([first, second], 0)


def turn(kernel, turned_ref):
    columns = kernel.shape[1]
    for at in range(0, columns, LANES):
        size = min(LANES, columns - at)
        turned_ref[at : at + size, :] = kernel[:, at : at + size].T


def tap_major(turned_ref, taps, w_ref, first):
    chans = turned_ref.shape[0] // TAPS
    at = 0
    for index in range(0, len(taps), LANES // chans):
        parts = [turned_ref[pl.ds(tap, chans, stride=TAPS), :] for tap in taps[index : index + LANES // chans]]
        block = jnp.concatenate(parts, 0).T.astype(BF16)
        w_ref[first : first + LANES, at : at + block.shape[1]] = block
        at += block.shape[1]


def four_weights_kernel(core_ref, own_ref, other_ref, w_ref, *turned_refs):
    core = core_ref[0]
    for index, turned_ref in enumerate(turned_refs):
        turn(jnp.where(core == index, own_ref[...].astype(F32), other_ref[...].astype(F32)), turned_ref)
        tap_major(turned_ref, range(TAPS), w_ref, index * LANES)


def four_weights(own, other, core):
    outs, columns = own.shape
    return pl.pallas_call(
        four_weights_kernel,
        out_shape=jax.ShapeDtypeStruct((2 * outs, columns), BF16),
        in_specs=[
            pl.BlockSpec(memory_space=pltpu.SMEM),
            pl.BlockSpec(memory_space=pltpu.VMEM),
            pl.BlockSpec(memory_space=pltpu.VMEM),
        ],
        scratch_shapes=[pltpu.VMEM((columns, LANES), F32)] * 2,
        compiler_params=pltpu.CompilerParams(vmem_limit_bytes=16 * MIB),
        cost_estimate=pl.CostEstimate(flops=10**3, bytes_accessed=10**3, transcendentals=0),
        name="four_weights",
    )(core, own, other)


def three_picks_kernel(core_ref, last_ref, before_ref, rim_ref, place_ref, picked_ref, prior_ref, *scratch):
    *split_refs, pick_ref = scratch
    core, step, last = core_ref[0], pl.program_id(0), pl.num_programs(0) - 1
    chans, block, width = rim_ref.shape[1], rim_ref.shape[2], rim_ref.shape[4]
    rows, part = last_ref.shape[3], last_ref.shape[1]
    planes = block * 4
    half = width // 2
    rim = (rows - 1) % SUB

    def picked(spots):
        values, held = [], None
        for plane, row in spots:
            if plane != held:
                x = rim_ref[0, :, plane, :SUB].astype(F32).reshape(chans * SUB, width)
                for at in range(width // LANES):
                    pick_ref[plane % 2, at] = x[:, at * LANES : (at + 1) * LANES]
                held = plane
            values.append(
                jnp.concatenate(
                    [pick_ref[plane % 2, at, pl.ds(row, chans, stride=SUB), :] for at in range(width // LANES)], 1
                ).astype(BF16)
            )
        values = jnp.concatenate(values, 0)
        parts = [part.astype(BF16) for part in spread((values[:, :half], values[:, half:]), place_ref[...])]
        return [
            jnp.concatenate([part[at * chans : (at + 1) * chans] for part in parts], 0) for at in range(len(spots))
        ]

    @pl.when(core == 0)
    def _():
        for plane, data in enumerate(picked([(plane, rim) for plane in range(block)])):
            picked_ref[step * block + plane] = data

    @pl.when((core == 0) & (step == last))
    def _():
        spots = [(plane, row) for plane in range(block - 3, block) for row in range(rim - 2, rim + 1)]
        for index, data in enumerate(picked(spots)):
            picked_ref[planes + index] = data
        prior_ref[...] = jnp.zeros_like(prior_ref)

    @pl.when(core == 1)
    def _():
        for source_ref, to_ref in ((last_ref, picked_ref), (before_ref, prior_ref)):

            def store(tap, row, first, value):
                at = pl.multiple_of(tap * chans + step * part + first, GROUP)
                to_ref[row + 1, pl.ds(at, GROUP), :] = value

            for _ in separate(source_ref, 0, place_ref, split_refs, store):
                pass

    @pl.when((core == 1) & (step == last))
    def _():
        for ref in (picked_ref, prior_ref):
            ref[0] = jnp.zeros_like(ref[0])


def three_picks(volume, core):
    _, chans, planes, rows, width = volume.shape
    half = width // 2
    block, steps = planes // 4, 4
    shape = (rows + 1, 3 * chans, half)
    full = lambda *shape: pl.BlockSpec(shape, lambda i, core: (0,) * len(shape))
    return pl.pallas_call(
        three_picks_kernel,
        grid_spec=pltpu.PrefetchScalarGridSpec(
            num_scalar_prefetch=1,
            grid=(steps,),
            in_specs=[
                pl.BlockSpec((1, chans // steps, 1, rows, width), lambda i, core: (0, i * core[0], planes - 1, 0, 0)),
                pl.BlockSpec(
                    (1, chans // steps, 1, rows, width), lambda i, core: (0, i * core[0], planes // 2 - 1, 0, 0)
                ),
                pl.BlockSpec(
                    (1, chans, block, 2 * SUB, width),
                    lambda i, core: (0, 0, i + core[0] * (steps - 1 - i), (rows - 1) // (2 * SUB), 0),
                ),
                full(half, half),
            ],
            out_specs=[full(*shape), full(*shape)],
            scratch_shapes=[pltpu.VMEM((2, half // LANES, GROUP * rows, LANES), F32)] * 2
            + [pltpu.VMEM((2, width // LANES, chans * SUB, LANES), F32)],
        ),
        out_shape=[jax.ShapeDtypeStruct(shape, BF16)] * 2,
        compiler_params=pltpu.CompilerParams(vmem_limit_bytes=36 * MIB),
        cost_estimate=pl.CostEstimate(flops=10**9, bytes_accessed=10**7, transcendentals=0),
        name="three_picks",
    )(core, volume, volume, volume, even_odd(half))


def three_edges_kernel(
    core_ref, picked_ref, own_ref, other_ref, own_scales_ref, other_scales_ref,
    message_ref, w_ref, gain_ref, shift_ref, scales_ref,
    turned_ref, rim_w_ref,
):
    core = core_ref[0]
    count, taps, half = picked_ref.shape
    out_rows = message_ref.shape[0]
    planes = count - 9
    turn(whole(own_ref[...].astype(F32), other_ref[...].astype(F32), core), turned_ref)
    tap_major(turned_ref, range(TAPS), w_ref, 0)
    own_scales, other_scales = own_scales_ref[...], other_scales_ref[...]
    lines = own_scales.shape[0]
    scales = jnp.concatenate([own_scales, other_scales, jnp.zeros((LANES - 2 * lines, LANES), F32)], 0).T
    scales_ref[...] = scales
    share = own_ref.shape[0]
    for ref, at in ((gain_ref, 0), (shift_ref, share)):
        ref[...] = whole(scales[at : at + share, 0:1], scales[at : at + share, lines : lines + 1], core)

    @pl.when(core == 0)
    def _():
        tap_major(turned_ref, RIM_TAPS, rim_w_ref, 0)
        none = jnp.zeros((taps, half), BF16)
        for index in range(planes // 2 + 1):
            pieces = [
                picked_ref[plane] if 0 <= plane < planes else none for plane in range(2 * index - 1, 2 * index + 2)
            ]
            total = jnp.dot(rim_w_ref[...], jnp.concatenate(pieces, 0), preferred_element_type=F32)
            message_ref[index] = total.astype(BF16)
        data = picked_ref[planes:].reshape(9 * taps, half)
        total = jnp.dot(w_ref[...], data, preferred_element_type=F32)
        message_ref[planes // 2 + 1] = activate(total, gain_ref[...], shift_ref[...]).astype(BF16)
        for index in range(planes // 2 + 2, out_rows):
            message_ref[index] = jnp.zeros_like(message_ref[index])

    @pl.when(core == 1)
    def _():
        for row in range(out_rows):
            total = jnp.dot(
                w_ref[:, : 3 * taps],
                picked_ref[2 * row : 2 * row + 3].reshape(3 * taps, half),
                preferred_element_type=F32,
            )
            message_ref[row] = total.astype(BF16)


def three_edges(picked, own, other, own_scales, other_scales, core):
    outs, columns = 2 * own.shape[0], own.shape[1]
    out_rows, half = picked.shape[0] // 2, picked.shape[2]
    shapes = [
        ((out_rows, outs, half), BF16),
        ((outs, columns), BF16),
        ((outs, 1), F32),
        ((outs, 1), F32),
        ((LANES, LANES), F32),
    ]
    return pl.pallas_call(
        three_edges_kernel,
        in_specs=inputs(5),
        out_shape=[jax.ShapeDtypeStruct(*shape) for shape in shapes],
        scratch_shapes=[pltpu.VMEM((columns, LANES), F32), pltpu.VMEM((outs, columns // 3), BF16)],
        compiler_params=pltpu.CompilerParams(vmem_limit_bytes=16 * MIB),
        cost_estimate=pl.CostEstimate(flops=10**9, bytes_accessed=10**6, transcendentals=0),
        name="three_edges",
    )(core, picked, own, other, own_scales, other_scales)


def three_kernel(
    core_ref, x_ref, before_ref, w_ref, place_ref, gain_ref, shift_ref,
    third_ref, plane_ref, row_ref, local_ref,
    *scratch,
):
    *split_refs, prior_ref, first_ref, second_ref, total_ref = scratch
    core, step, steps = core_ref[0], pl.program_id(0), pl.num_programs(0) - 1
    chans, rows, width = x_ref.shape[1], x_ref.shape[3], x_ref.shape[4]
    half = width // 2
    out_rows = rows // 2
    taps = 3 * chans

    def splitting(pair_ref):
        for plane in range(2):

            def store(tap, row, first, value, plane=plane):
                pair_ref[plane, row + 1, tap * chans + first : tap * chans + first + GROUP, :] = value

            yield from separate(x_ref, plane, place_ref, split_refs, store)

    def summing(pair_ref):
        gain, shift = gain_ref[...], shift_ref[...]
        for row in range(out_rows):
            parts = [
                ref[2 * row : 2 * row + 3].reshape(3 * taps, half)
                for ref in (prior_ref, pair_ref.at[0], pair_ref.at[1])
            ]
            total = jnp.dot(w_ref[...], jnp.concatenate(parts, 0), preferred_element_type=F32)
            third_ref[0, row] = activate(total, gain, shift).astype(BF16)
            total_ref[row] = total
            yield
        row_ref[0] = total_ref[0]
        prior_ref[...] = pair_ref[1]
        yield

    @pl.when(step == 0)
    def _():
        prior_ref[...] = before_ref[...]
        for ref in (first_ref, second_ref):
            ref[:, 0] = jnp.zeros_like(ref[:, 0])
        for _ in splitting(first_ref):
            pass

    def both(new_ref, old_ref):
        new, old = splitting(new_ref), summing(old_ref)
        for turn in range(2 * chans // GROUP):
            next(new, None)
            for _ in range(out_rows * (turn + 1) // (2 * chans // GROUP) - out_rows * turn // (2 * chans // GROUP)):
                next(old, None)
        for _ in new:
            pass
        for _ in old:
            pass

    for odd, (new_ref, old_ref) in enumerate(((first_ref, second_ref), (second_ref, first_ref))):

        @pl.when((step > 0) & (step < steps) & (step % 2 == odd))
        def _(new_ref=new_ref, old_ref=old_ref):
            both(new_ref, old_ref)

        @pl.when((step == steps) & (step % 2 == odd))
        def _(old_ref=old_ref):
            for _ in summing(old_ref):
                pass

    @pl.when(step == 1)
    def _():
        plane_ref[...] = total_ref[...]

    @pl.when((step > 0) & (core == 1))
    def _():
        local_ref[step - 1] = third_ref[0, out_rows - 1]

    @pl.when((step == steps) & (core == 0))
    def _():
        local_ref[...] = third_ref[0]
        local_ref[0] = total_ref[0].astype(BF16)


def layer_three(volume, prior, weights, gain, shift, core):
    _, chans, planes, rows, width = volume.shape
    outs = weights.shape[0]
    half = width // 2
    steps, out_rows = planes // 4, rows // 2
    full = lambda *shape: pl.BlockSpec(shape, lambda i, core: (0,) * len(shape))
    return pl.pallas_call(
        three_kernel,
        grid_spec=pltpu.PrefetchScalarGridSpec(
            num_scalar_prefetch=1,
            grid=(steps + 1,),
            in_specs=[
                pl.BlockSpec((1, chans, 2, rows, width), lambda i, core: (0, 0, core[0] * steps + jnp.minimum(i, steps - 1), 0, 0)),
                pl.BlockSpec(prior.shape, lambda i, core: (0, 0, 0), pipeline_mode=pl.Buffered(1)),
                full(*weights.shape),
                full(half, half),
                full(outs, 1),
                full(outs, 1),
            ],
            out_specs=[
                pl.BlockSpec((1, out_rows, outs, half), lambda i, core: (jnp.maximum(i - 1, 0), 0, 0, 0)),
                full(out_rows, outs, half),
                pl.BlockSpec((1, outs, half), lambda i, core: (jnp.maximum(i - 1, 0), 0, 0)),
                full(out_rows, outs, half),
            ],
            scratch_shapes=[pltpu.VMEM((2, half // LANES, GROUP * rows, LANES), F32)] * 4
            + [
                pltpu.VMEM((rows + 1, 3 * chans, half), BF16),
                pltpu.VMEM((2, rows + 1, 3 * chans, half), BF16),
                pltpu.VMEM((2, rows + 1, 3 * chans, half), BF16),
                pltpu.VMEM((out_rows, outs, half), F32),
            ],
        ),
        out_shape=[
            jax.ShapeDtypeStruct((steps, out_rows, outs, half), BF16),
            jax.ShapeDtypeStruct((out_rows, outs, half), F32),
            jax.ShapeDtypeStruct((steps, outs, half), F32),
            jax.ShapeDtypeStruct((out_rows, outs, half), BF16),
        ],
        compiler_params=pltpu.CompilerParams(vmem_limit_bytes=46 * MIB),
        cost_estimate=pl.CostEstimate(flops=10**10, bytes_accessed=2 * 10**7, transcendentals=0),
        name="layer_three",
    )(core, volume, prior, weights, even_odd(half), gain, shift)


def corner_total(core, refs, rows_ref):
    third_ref, plane_ref, _, halo_ref, _, _ = refs
    planes = third_ref.shape[0]
    first = jnp.where(core == 0, rows_ref[0].astype(F32), halo_ref[planes].astype(F32))
    return plane_ref[0] + jnp.where(core == 0, halo_ref[0].astype(F32), 0.0) + first


def third_value(core, refs, plane, row, rows_ref=None):
    third_ref, plane_ref, row_ref, halo_ref, gain_ref, shift_ref = refs
    planes = third_ref.shape[0]
    if plane and row:
        return third_ref[plane, row]
    if plane:
        share = halo_ref[planes + plane].astype(F32)
        if rows_ref is not None:
            share = jnp.where(core == 0, rows_ref[plane].astype(F32), share)
        total = row_ref[plane] + share
    elif row:
        total = plane_ref[row] + jnp.where(core == 0, halo_ref[row].astype(F32), 0.0)
    else:
        total = corner_total(core, refs, rows_ref)
    value = activate(total, gain_ref[...], shift_ref[...])
    if not plane and not row:
        value = jnp.where(core == 0, 0.0, value)
    return value.astype(BF16)


def four_edges_kernel(core_ref, *refs):
    *thirds, local_ref, w_ref, place_ref, message_ref, mid_ref = refs
    core = core_ref[0]
    planes, rows, chans, width = thirds[0].shape
    half = width // 2
    out_rows = rows // 2
    taps = 3 * chans
    mid_ref[...] = w_ref[:, 4 * taps : 5 * taps]

    def data(values):
        parts = [part.astype(BF16) for part in spread((jnp.concatenate(values, 0),), place_ref[...])]
        return [
            jnp.concatenate([part[at * chans : (at + 1) * chans] for part in parts], 0) for at in range(len(values))
        ]

    @pl.when(core == 0)
    def _():
        none = jnp.zeros((taps, half), BF16)
        rim = [none] + data(
            [third_value(core, thirds, plane, rows - 1) for plane in range(planes)]
            + [local_ref[plane] for plane in range(planes)]
        )
        pieces = [jnp.concatenate([rim[2 * m + slot] for m in range(planes)], 1) for slot in range(3)]
        weights = jnp.concatenate([w_ref[:, 3 * slot * taps : (3 * slot + 1) * taps] for slot in range(3)], 1)
        total = jnp.dot(weights, jnp.concatenate(pieces, 0), preferred_element_type=F32).astype(BF16)
        for m in range(planes):
            message_ref[m] = total[:, m * half : (m + 1) * half]
        for index in range(planes, message_ref.shape[0]):
            message_ref[index] = jnp.zeros_like(message_ref[index])

    @pl.when(core == 1)
    def _():
        halo_ref = thirds[3]
        last = data(
            [halo_ref[2 * planes + 1]] + [third_value(core, thirds, planes - 1, row) for row in range(rows)]
        )
        for row in range(0, out_rows, 2):
            pieces = [jnp.concatenate([last[2 * row + at], last[2 * row + 2 + at]], 1) for at in range(3)]
            both = jnp.dot(w_ref[:, : 3 * taps], jnp.concatenate(pieces, 0), preferred_element_type=F32)
            both = both.astype(BF16)
            message_ref[row] = both[:, :half]
            message_ref[row + 1] = both[:, half:]
        corner = halo_ref[2 * planes]
        message_ref[out_rows, :chans] = corner[:, :half]
        message_ref[out_rows, chans:] = corner[:, half:]


def four_edges(core, thirds, local, weights):
    planes, rows, chans, width = thirds[0].shape
    outs = weights.shape[0]
    half = width // 2
    return pl.pallas_call(
        four_edges_kernel,
        out_shape=[
            jax.ShapeDtypeStruct((rows // 2 + 1, outs, half), BF16),
            jax.ShapeDtypeStruct((outs, 3 * chans), BF16),
        ],
        in_specs=inputs(len(thirds) + 3),
        compiler_params=pltpu.CompilerParams(vmem_limit_bytes=24 * MIB),
        cost_estimate=pl.CostEstimate(flops=10**9, bytes_accessed=10**6, transcendentals=0),
        name="four_edges",
    )(core, *thirds, local, weights, even_odd(width))


def four_kernel(core_ref, *refs):
    *thirds, local_ref, w_ref, place_ref, own_ref, theirs_ref, corner_ref, data_ref = refs
    core = core_ref[0]
    planes, rows, chans, width = thirds[0].shape
    halo_ref, gain_ref, shift_ref = thirds[3:]
    rows_ref = local_ref.at[planes : 2 * planes]
    half = width // 2
    out_rows, count = rows // 2, planes // 2
    taps = 3 * chans
    batch = 4
    data_ref[:, 0] = jnp.zeros_like(data_ref[:, 0])
    corner_ref[...] = corner_total(core, thirds, rows_ref)

    def put(values, first, spots):
        for tap, part in enumerate(spread((jnp.concatenate(values, 0),), place_ref[...])):
            part = part.astype(BF16)
            for at in range(len(values)):
                for slot, lanes in spots:
                    data_ref[
                        slot, first + at + 1, tap * chans : (tap + 1) * chans, lanes * half : (lanes + 1) * half
                    ] = part[at * chans : (at + 1) * chans]

    @pl.when(core == 0)
    def _():
        data_ref[0, :, :, :half] = jnp.zeros_like(data_ref[0, :, :, :half])

    @pl.when(core == 1)
    def _():
        total = local_ref[0].astype(F32) + halo_ref[planes - 1].astype(F32)
        prior = [activate(total, gain_ref[...], shift_ref[...]).astype(BF16)]
        prior += [local_ref[row] for row in range(1, rows)]
        for first in range(0, rows, batch):
            put(prior[first : first + batch], first, [(0, 0)])

    for plane in range(planes):
        spots = [(1 + plane % 2, plane // 2)]
        if plane % 2 and plane // 2 + 1 < count:
            spots.append((0, plane // 2 + 1))
        for first in range(0, rows, batch):
            put([third_value(core, thirds, plane, row, rows_ref) for row in range(first, first + batch)], first, spots)
    for row in range(out_rows):
        parts = [data_ref[slot, 2 * row : 2 * row + 3].reshape(3 * taps, count * half) for slot in range(3)]
        total = jnp.dot(w_ref[...], jnp.concatenate(parts, 0), preferred_element_type=F32)
        own_ref[row] = jnp.where(core == 0, total[:LANES], total[LANES:])
        theirs_ref[row] = jnp.where(core == 0, total[LANES:], total[:LANES])


def layer_four(core, thirds, local, weights):
    planes, rows, chans, width = thirds[0].shape
    outs = weights.shape[0]
    half = width // 2
    out_rows, count = rows // 2, planes // 2
    return pl.pallas_call(
        four_kernel,
        out_shape=[
            jax.ShapeDtypeStruct((out_rows, outs // 2, count * half), F32),
            jax.ShapeDtypeStruct((out_rows, outs // 2, count * half), F32),
            jax.ShapeDtypeStruct((chans, width), F32),
        ],
        in_specs=inputs(len(thirds) + 3),
        scratch_shapes=[pltpu.VMEM((3, rows + 1, 3 * chans, count * half), BF16)],
        compiler_params=pltpu.CompilerParams(vmem_limit_bytes=32 * MIB),
        cost_estimate=pl.CostEstimate(flops=4 * 10**9, bytes_accessed=4 * 10**6, transcendentals=0),
        name="layer_four",
    )(core, *thirds, local, weights, even_odd(width))


def shares_kernel(core_ref, corner_ref, halo_ref, mid_ref, place_ref, gain_ref, shift_ref, shares_ref, fix_ref):
    core = core_ref[0]
    rows = halo_ref.shape[0] - 1

    @pl.when(core == 0)
    def _():
        corner = halo_ref[rows].astype(F32)
        total = corner_ref[...] + jnp.concatenate([corner[:LANES], corner[LANES:]], 1)
        value = activate(total, gain_ref[...], shift_ref[...]).astype(BF16)
        data = jnp.concatenate([part.astype(BF16) for part in spread((value,), place_ref[...])], 0)
        fix = jnp.dot(mid_ref[...], data, preferred_element_type=F32)
        fix_ref[...] = fix[:LANES]
        shares_ref[...] = halo_ref[:rows, LANES:].astype(F32)
        shares_ref[0] += fix[LANES:]

    @pl.when(core == 1)
    def _():
        fix_ref[...] = jnp.zeros_like(fix_ref)
        shares_ref[...] = halo_ref[:rows, :LANES].astype(F32)


def assemble_kernel(
    core_ref, own_ref, got_ref, halo_ref, fix_ref, scales_ref, shares_ref, out_ref, lines_ref
):
    core = core_ref[0]
    gain, shift = scales_ref[:, 1:2], scales_ref[:, 2:3]
    rows, width = halo_ref.shape[0] - 1, halo_ref.shape[2]
    count = own_ref.shape[2] // width

    def put(row, parts):
        for at, total in enumerate(parts):
            value = activate(total, gain, shift)
            for m in range(count):
                place = row * 2 * count + at * count + m
                lines_ref[pl.ds(place, LANES, stride=rows * 2 * count), :] = value[:, m * width : (m + 1) * width]

    def with_edge(total, edge):
        return jnp.concatenate([total[:, :width] + edge, total[:, width:]], 1)

    @pl.when(core == 0)
    def _():
        for row in range(rows):
            edge = halo_ref[row, :LANES].astype(F32)
            if not row:
                edge = edge + fix_ref[...]
            total, got = with_edge(own_ref[row], edge), got_ref[row]
            if not row:
                first = [shares_ref[m] for m in range(2 * count)]
                total = total + jnp.concatenate(first[:count], 1)
                got = got + jnp.concatenate(first[count:], 1)
            put(row, (total, got))

    @pl.when(core == 1)
    def _():
        for row in range(rows):
            total, got = own_ref[row], with_edge(got_ref[row], shares_ref[row])
            if not row:
                first = [halo_ref[m, LANES:].astype(F32) for m in range(2 * count)]
                total = total + jnp.concatenate(first[count:], 1)
                got = got + jnp.concatenate(first[:count], 1)
            put(row, (got, total))

    out_ref[...] = lines_ref[...].astype(BF16)


def last_stage(core, own, theirs, corner, halo, mid, gain, shift, scales):
    rows, outs, lanes = own.shape
    got = swapped(theirs)
    shares, fix = pl.pallas_call(
        shares_kernel,
        out_shape=[
            jax.ShapeDtypeStruct((rows, outs, halo.shape[2]), F32),
            jax.ShapeDtypeStruct((outs, halo.shape[2]), F32),
        ],
        in_specs=inputs(6),
        compiler_params=pltpu.CompilerParams(vmem_limit_bytes=16 * MIB),
        cost_estimate=pl.CostEstimate(flops=10**8, bytes_accessed=10**6, transcendentals=0),
        name="shares",
    )(core, corner, halo, mid, even_odd(lanes), gain, shift)
    lines = (outs * rows * lanes * 2 // LANES, LANES)
    return pl.pallas_call(
        assemble_kernel,
        out_shape=jax.ShapeDtypeStruct(lines, BF16),
        in_specs=inputs(6),
        scratch_shapes=[pltpu.VMEM(lines, F32)],
        compiler_params=pltpu.CompilerParams(vmem_limit_bytes=16 * MIB),
        name="assemble",
    )(core, own, got, halo, fix, scales, swapped(shares))


def handed_on(message):
    count = lax.axis_size("sp")
    pairs = [(2 * b, 2 * (b + 1) + 1) for b in range(count) if b % ROW_BLOCKS != ROW_BLOCKS - 1]
    pairs += [(2 * b + 1, 2 * (b + ROW_BLOCKS)) for b in range(count - ROW_BLOCKS)]
    return lax.ppermute(message, ("sp", "fl"), pairs)


def swapped(value):
    return lax.ppermute(value, "fl", [(0, 1), (1, 0)])


def shards(volume, kernel_three, gain_three, shift_three, kernel_four, gain_four, shift_four):
    core = lax.axis_index("fl").reshape(1)
    own_scales = jnp.concatenate([gain_three, shift_three, gain_four, shift_four]).reshape(-1, LANES)
    picked, prior = three_picks(volume, core)
    others = lax.optimization_barrier((swapped(kernel_three), swapped(own_scales), swapped(kernel_four)))
    message, weights_three, gain, shift, scales = three_edges(
        picked, kernel_three, others[0], own_scales, others[1], core
    )
    weights_three, kernel_four = lax.optimization_barrier((weights_three, kernel_four))
    halo = handed_on(message)
    *thirds, local = layer_three(volume, prior, weights_three, gain, shift, core)
    planes = thirds[0].shape[0]
    passed = jnp.where(core[0] == 1, halo[:planes], local[planes : 2 * planes])
    local = swapped(lax.dynamic_update_slice(local, passed, (planes, 0, 0)))
    thirds = (*thirds, halo, gain, shift)
    weights_four = four_weights(kernel_four, others[2], core)
    message, mid = four_edges(core, thirds, local, weights_four)
    halo = handed_on(message)
    own, theirs, corner = layer_four(core, thirds, local, weights_four)
    lines = last_stage(core, own, theirs, corner, halo, mid, gain, shift, scales)
    out_rows, outs, lanes = own.shape
    fourth = lines.reshape(outs, out_rows, 2 * lanes // LANES, LANES)
    return jnp.transpose(fourth, (0, 2, 1, 3))[None]


def solution(mesh):
    return jax.shard_map(
        shards,
        mesh=mesh,
        in_specs=(
            P("sp", None, None, None, None),
            P("fl", None),
            P("fl"),
            P("fl"),
            P("fl", None),
            P("fl"),
            P("fl"),
        ),
        out_specs=P("sp", "fl", None, None, None),
        check_vma=False,
    )
```

```python
import functools

import jax
import jax.numpy as jnp
import numpy as np
from jax import lax
from jax.experimental import pallas as pl
from jax.experimental.pallas import tpu as pltpu
from jax.sharding import PartitionSpec as P

F32 = jnp.float32
BF16 = jnp.bfloat16
LANES = 128
ROW_BLOCKS = 8
SUB = 8
TAPS = 27
RIM_TAPS = tuple(9 * a + e for a in range(3) for e in range(3))
GROUP = 16
MIB = 2**20


def even_odd(width):
    half = width // 2
    place = np.zeros((width, width), np.float32)
    place[np.arange(0, width, 2), np.arange(half)] = 1
    place[np.arange(1, width, 2), half + np.arange(half)] = 1
    return jnp.asarray(place, BF16)


def activate(total, gain, shift):
    return jnp.maximum(total * gain + shift, 0.0)


def shifted(odd):
    lane = lax.broadcasted_iota(jnp.int32, odd.shape, 1)
    return jnp.where(lane == 0, 0.0, pltpu.roll(odd, 1, 1))


def spread(sides, place):
    quarter = place.shape[0] // 2
    split = [jnp.dot(side, place, preferred_element_type=F32) for side in sides]
    even = jnp.concatenate([part[:, :quarter] for part in split], 1)
    odd = jnp.concatenate([part[:, quarter:] for part in split], 1)
    return shifted(odd), even, odd


def separate(x_ref, plane, place_ref, split_refs, store):
    chans, rows, width = x_ref.shape[1], x_ref.shape[3], x_ref.shape[4]
    half = width // 2
    quarter = half // 2
    for index, first in enumerate(range(0, chans, GROUP)):
        split_ref = split_refs[index % len(split_refs)]
        x = x_ref[0, pl.ds(first, GROUP), plane]
        x = x.astype(F32).reshape(GROUP * rows, width).astype(BF16)
        for side in range(2):
            parts = jnp.dot(
                x[:, side * half : (side + 1) * half], place_ref[...], preferred_element_type=F32
            )
            for block in range(half // LANES):
                odd, at = divmod(block, quarter // LANES)
                split_ref[odd, side * (quarter // LANES) + at] = parts[:, block * LANES : (block + 1) * LANES]
        for row in range(rows):
            even, odd = (
                jnp.concatenate(
                    [split_ref[odd, at, pl.ds(row, GROUP, stride=rows), :] for at in range(half // LANES)], 1
                )
                for odd in range(2)
            )
            for tap, value in enumerate((shifted(odd), even, odd)):
                store(tap, row, first, value.astype(BF16))
        yield


def inputs(count):
    return [pl.BlockSpec(memory_space=pltpu.SMEM)] + [pl.BlockSpec(memory_space=pltpu.VMEM)] * count


def whole(own, other, core):
    first = jnp.where(core == 0, own, other)
    second = jnp.where(core == 0, other, own)
    return jnp.concatenate([first, second], 0)


def turn(kernel, turned_ref):
    columns = kernel.shape[1]
    for at in range(0, columns, LANES):
        size = min(LANES, columns - at)
        turned_ref[at : at + size, :] = kernel[:, at : at + size].T


def tap_major(turned_ref, taps, w_ref, first):
    chans = turned_ref.shape[0] // TAPS
    at = 0
    for index in range(0, len(taps), LANES // chans):
        parts = [turned_ref[pl.ds(tap, chans, stride=TAPS), :] for tap in taps[index : index + LANES // chans]]
        block = jnp.concatenate(parts, 0).T.astype(BF16)
        w_ref[first : first + LANES, at : at + block.shape[1]] = block
        at += block.shape[1]


def four_weights_kernel(core_ref, own_ref, other_ref, w_ref, *turned_refs):
    core = core_ref[0]
    for index, turned_ref in enumerate(turned_refs):
        turn(jnp.where(core == index, own_ref[...].astype(F32), other_ref[...].astype(F32)), turned_ref)
        tap_major(turned_ref, range(TAPS), w_ref, index * LANES)


def four_weights(own, other, core):
    outs, columns = own.shape
    return pl.pallas_call(
        four_weights_kernel,
        out_shape=jax.ShapeDtypeStruct((2 * outs, columns), BF16),
        in_specs=[
            pl.BlockSpec(memory_space=pltpu.SMEM),
            pl.BlockSpec(memory_space=pltpu.VMEM),
            pl.BlockSpec(memory_space=pltpu.VMEM),
        ],
        scratch_shapes=[pltpu.VMEM((columns, LANES), F32)] * 2,
        compiler_params=pltpu.CompilerParams(vmem_limit_bytes=16 * MIB),
        cost_estimate=pl.CostEstimate(flops=10**3, bytes_accessed=10**3, transcendentals=0),
        name="four_weights",
    )(core, own, other)


def three_picks_kernel(core_ref, last_ref, before_ref, rim_ref, picked_ref, prior_ref, *scratch):
    *split_refs, pick_ref, place_ref = scratch
    core, step, last = core_ref[0], pl.program_id(0), pl.num_programs(0) - 1
    chans, block, width = rim_ref.shape[1], rim_ref.shape[2], rim_ref.shape[4]
    rows, part = last_ref.shape[3], last_ref.shape[1]
    planes = block * 4
    half = width // 2
    rim = (rows - 1) % SUB

    @pl.when(step == 0)
    def _():
        source = lax.broadcasted_iota(jnp.int32, place_ref.shape, 0)
        target = lax.broadcasted_iota(jnp.int32, place_ref.shape, 1)
        quarter = half // 2
        wanted = jnp.where(target < quarter, 2 * target, 2 * (target - quarter) + 1)
        place_ref[...] = jnp.where(source == wanted, 1.0, 0.0).astype(BF16)

    def picked(spots):
        values, held = [], None
        for plane, row in spots:
            if plane != held:
                x = rim_ref[0, :, plane, :SUB].astype(F32).reshape(chans * SUB, width)
                for at in range(width // LANES):
                    pick_ref[plane % 2, at] = x[:, at * LANES : (at + 1) * LANES]
                held = plane
            values.append(
                jnp.concatenate(
                    [pick_ref[plane % 2, at, pl.ds(row, chans, stride=SUB), :] for at in range(width // LANES)], 1
                ).astype(BF16)
            )
        values = jnp.concatenate(values, 0)
        parts = [part.astype(BF16) for part in spread((values[:, :half], values[:, half:]), place_ref[...])]
        return [
            jnp.concatenate([part[at * chans : (at + 1) * chans] for part in parts], 0) for at in range(len(spots))
        ]

    @pl.when(core == 0)
    def _():
        for plane, data in enumerate(picked([(plane, rim) for plane in range(block)])):
            picked_ref[step * block + plane] = data

    @pl.when((core == 0) & (step == last))
    def _():
        spots = [(plane, row) for plane in range(block - 3, block) for row in range(rim - 2, rim + 1)]
        for index, data in enumerate(picked(spots)):
            picked_ref[planes + index] = data
        prior_ref[...] = jnp.zeros_like(prior_ref)

    @pl.when(core == 1)
    def _():
        for source_ref, to_ref in ((last_ref, picked_ref), (before_ref, prior_ref)):

            def store(tap, row, first, value):
                at = pl.multiple_of(tap * chans + step * part + first, GROUP)
                to_ref[row + 1, pl.ds(at, GROUP), :] = value

            for _ in separate(source_ref, 0, place_ref, split_refs, store):
                pass

    @pl.when((core == 1) & (step == last))
    def _():
        for ref in (picked_ref, prior_ref):
            ref[0] = jnp.zeros_like(ref[0])


def three_picks(volume, core):
    _, chans, planes, rows, width = volume.shape
    half = width // 2
    block, steps = planes // 4, 4
    shape = (rows + 1, 3 * chans, half)
    full = lambda *shape: pl.BlockSpec(shape, lambda i, core: (0,) * len(shape))
    return pl.pallas_call(
        three_picks_kernel,
        grid_spec=pltpu.PrefetchScalarGridSpec(
            num_scalar_prefetch=1,
            grid=(steps,),
            in_specs=[
                pl.BlockSpec((1, chans // steps, 1, rows, width), lambda i, core: (0, i * core[0], planes - 1, 0, 0)),
                pl.BlockSpec(
                    (1, chans // steps, 1, rows, width), lambda i, core: (0, i * core[0], planes // 2 - 1, 0, 0)
                ),
                pl.BlockSpec(
                    (1, chans, block, 2 * SUB, width),
                    lambda i, core: (0, 0, i + core[0] * (steps - 1 - i), (rows - 1) // (2 * SUB), 0),
                ),
            ],
            out_specs=[full(*shape), full(*shape)],
            scratch_shapes=[pltpu.VMEM((2, half // LANES, GROUP * rows, LANES), F32)] * 2
            + [pltpu.VMEM((2, width // LANES, chans * SUB, LANES), F32), pltpu.VMEM((half, half), BF16)],
        ),
        out_shape=[jax.ShapeDtypeStruct(shape, BF16)] * 2,
        compiler_params=pltpu.CompilerParams(vmem_limit_bytes=28 * MIB),
        cost_estimate=pl.CostEstimate(flops=10**9, bytes_accessed=10**7, transcendentals=0),
        name="three_picks",
    )(core, volume, volume, volume)


def three_edges_kernel(
    core_ref, picked_ref, own_ref, other_ref, own_scales_ref, other_scales_ref,
    message_ref, w_ref, gain_ref, shift_ref, scales_ref,
    turned_ref, rim_w_ref,
):
    core = core_ref[0]
    count, taps, half = picked_ref.shape
    out_rows = message_ref.shape[0]
    planes = count - 9
    turn(whole(own_ref[...].astype(F32), other_ref[...].astype(F32), core), turned_ref)
    tap_major(turned_ref, range(TAPS), w_ref, 0)
    own_scales, other_scales = own_scales_ref[...], other_scales_ref[...]
    lines = own_scales.shape[0]
    scales = jnp.concatenate([own_scales, other_scales, jnp.zeros((LANES - 2 * lines, LANES), F32)], 0).T
    scales_ref[...] = scales
    share = own_ref.shape[0]
    for ref, at in ((gain_ref, 0), (shift_ref, share)):
        ref[...] = whole(scales[at : at + share, 0:1], scales[at : at + share, lines : lines + 1], core)

    @pl.when(core == 0)
    def _():
        tap_major(turned_ref, RIM_TAPS, rim_w_ref, 0)
        none = jnp.zeros((taps, half), BF16)
        for index in range(planes // 2 + 1):
            pieces = [
                picked_ref[plane] if 0 <= plane < planes else none for plane in range(2 * index - 1, 2 * index + 2)
            ]
            total = jnp.dot(rim_w_ref[...], jnp.concatenate(pieces, 0), preferred_element_type=F32)
            message_ref[index] = total.astype(BF16)
        data = picked_ref[planes:].reshape(9 * taps, half)
        total = jnp.dot(w_ref[...], data, preferred_element_type=F32)
        message_ref[planes // 2 + 1] = activate(total, gain_ref[...], shift_ref[...]).astype(BF16)
        for index in range(planes // 2 + 2, out_rows):
            message_ref[index] = jnp.zeros_like(message_ref[index])

    @pl.when(core == 1)
    def _():
        for row in range(out_rows):
            total = jnp.dot(
                w_ref[:, : 3 * taps],
                picked_ref[2 * row : 2 * row + 3].reshape(3 * taps, half),
                preferred_element_type=F32,
            )
            message_ref[row] = total.astype(BF16)


def three_edges(picked, own, other, own_scales, other_scales, core):
    outs, columns = 2 * own.shape[0], own.shape[1]
    out_rows, half = picked.shape[0] // 2, picked.shape[2]
    shapes = [
        ((out_rows, outs, half), BF16),
        ((outs, columns), BF16),
        ((outs, 1), F32),
        ((outs, 1), F32),
        ((LANES, LANES), F32),
    ]
    return pl.pallas_call(
        three_edges_kernel,
        in_specs=inputs(5),
        out_shape=[jax.ShapeDtypeStruct(*shape) for shape in shapes],
        scratch_shapes=[pltpu.VMEM((columns, LANES), F32), pltpu.VMEM((outs, columns // 3), BF16)],
        compiler_params=pltpu.CompilerParams(vmem_limit_bytes=16 * MIB),
        cost_estimate=pl.CostEstimate(flops=10**9, bytes_accessed=10**6, transcendentals=0),
        name="three_edges",
    )(core, picked, own, other, own_scales, other_scales)


def three_kernel(
    core_ref, x_ref, before_ref, w_ref, place_ref, gain_ref, shift_ref,
    third_ref, plane_ref, row_ref, local_ref,
    *scratch,
):
    *split_refs, even_ref, odd_ref = scratch
    core, step, last = core_ref[0], pl.program_id(0), pl.num_programs(0) - 1
    chans, rows, width = x_ref.shape[1], x_ref.shape[3], x_ref.shape[4]
    half = width // 2
    out_rows = rows // 2
    taps = 3 * chans
    prior, new = (step + 1) % 2, step % 2

    @pl.when(step == 0)
    def _():
        odd_ref[1] = before_ref[...]
        even_ref[0] = jnp.zeros_like(even_ref[0])
        odd_ref[0, 0] = jnp.zeros_like(even_ref[0])

    def store_even(tap, row, first, value):
        even_ref[row + 1, tap * chans + first : tap * chans + first + GROUP, :] = value

    def store_odd(tap, row, first, value):
        odd_ref[new, row + 1, tap * chans + first : tap * chans + first + GROUP, :] = value

    for plane, store in enumerate((store_even, store_odd)):
        for _ in separate(x_ref, plane, place_ref, split_refs, store):
            pass

    def summing(keep):
        gain, shift = gain_ref[...], shift_ref[...]
        for row in range(out_rows):
            span = slice(2 * row, 2 * row + 3)
            parts = [odd_ref[prior, span], even_ref[span], odd_ref[new, span]]
            data = jnp.concatenate([part.reshape(3 * taps, half) for part in parts], 0)
            total = jnp.dot(w_ref[...], data, preferred_element_type=F32)
            third_ref[0, row] = activate(total, gain, shift).astype(BF16)
            if keep:
                plane_ref[row] = total
            if not row:
                row_ref[0] = total

    @pl.when(step == 0)
    def _():
        summing(True)

    @pl.when(step > 0)
    def _():
        summing(False)

    @pl.when(core == 1)
    def _():
        local_ref[step] = third_ref[0, out_rows - 1]

    @pl.when((step == last) & (core == 0))
    def _():
        local_ref[...] = third_ref[0]
        local_ref[0] = row_ref[0].astype(BF16)


def layer_three(volume, prior, weights, gain, shift, core):
    _, chans, planes, rows, width = volume.shape
    outs = weights.shape[0]
    half = width // 2
    steps, out_rows = planes // 4, rows // 2
    full = lambda *shape: pl.BlockSpec(shape, lambda i, core: (0,) * len(shape))
    return pl.pallas_call(
        three_kernel,
        grid_spec=pltpu.PrefetchScalarGridSpec(
            num_scalar_prefetch=1,
            grid=(steps,),
            in_specs=[
                pl.BlockSpec((1, chans, 2, rows, width), lambda i, core: (0, 0, core[0] * steps + i, 0, 0)),
                pl.BlockSpec(prior.shape, lambda i, core: (0, 0, 0), pipeline_mode=pl.Buffered(1)),
                full(*weights.shape),
                full(half, half),
                full(outs, 1),
                full(outs, 1),
            ],
            out_specs=[
                pl.BlockSpec((1, out_rows, outs, half), lambda i, core: (i, 0, 0, 0)),
                full(out_rows, outs, half),
                pl.BlockSpec((1, outs, half), lambda i, core: (i, 0, 0)),
                full(out_rows, outs, half),
            ],
            scratch_shapes=[pltpu.VMEM((2, half // LANES, GROUP * rows, LANES), F32)] * 4
            + [
                pltpu.VMEM((rows + 1, 3 * chans, half), BF16),
                pltpu.VMEM((2, rows + 1, 3 * chans, half), BF16),
            ],
        ),
        out_shape=[
            jax.ShapeDtypeStruct((steps, out_rows, outs, half), BF16),
            jax.ShapeDtypeStruct((out_rows, outs, half), F32),
            jax.ShapeDtypeStruct((steps, outs, half), F32),
            jax.ShapeDtypeStruct((out_rows, outs, half), BF16),
        ],
        compiler_params=pltpu.CompilerParams(vmem_limit_bytes=34 * MIB),
        cost_estimate=pl.CostEstimate(flops=10**10, bytes_accessed=2 * 10**7, transcendentals=0),
        name="layer_three",
    )(core, volume, prior, weights, even_odd(half), gain, shift)


def corner_total(core, refs, rows_ref):
    third_ref, plane_ref, _, halo_ref, _, _ = refs
    planes = third_ref.shape[0]
    first = jnp.where(core == 0, rows_ref[0].astype(F32), halo_ref[planes].astype(F32))
    return plane_ref[0] + jnp.where(core == 0, halo_ref[0].astype(F32), 0.0) + first


def third_value(core, refs, plane, row, rows_ref=None):
    third_ref, plane_ref, row_ref, halo_ref, gain_ref, shift_ref = refs
    planes = third_ref.shape[0]
    if plane and row:
        return third_ref[plane, row]
    if plane:
        share = halo_ref[planes + plane].astype(F32)
        if rows_ref is not None:
            share = jnp.where(core == 0, rows_ref[plane].astype(F32), share)
        total = row_ref[plane] + share
    elif row:
        total = plane_ref[row] + jnp.where(core == 0, halo_ref[row].astype(F32), 0.0)
    else:
        total = corner_total(core, refs, rows_ref)
    value = activate(total, gain_ref[...], shift_ref[...])
    if not plane and not row:
        value = jnp.where(core == 0, 0.0, value)
    return value.astype(BF16)


def four_edges_kernel(core_ref, *refs):
    *thirds, local_ref, w_ref, place_ref, message_ref, mid_ref = refs
    core = core_ref[0]
    planes, rows, chans, width = thirds[0].shape
    half = width // 2
    out_rows = rows // 2
    taps = 3 * chans
    mid_ref[...] = w_ref[:, 4 * taps : 5 * taps]

    def data(values):
        parts = [part.astype(BF16) for part in spread((jnp.concatenate(values, 0),), place_ref[...])]
        return [
            jnp.concatenate([part[at * chans : (at + 1) * chans] for part in parts], 0) for at in range(len(values))
        ]

    @pl.when(core == 0)
    def _():
        none = jnp.zeros((taps, half), BF16)
        rim = [none] + data(
            [third_value(core, thirds, plane, rows - 1) for plane in range(planes)]
            + [local_ref[plane] for plane in range(planes)]
        )
        pieces = [jnp.concatenate([rim[2 * m + slot] for m in range(planes)], 1) for slot in range(3)]
        weights = jnp.concatenate([w_ref[:, 3 * slot * taps : (3 * slot + 1) * taps] for slot in range(3)], 1)
        total = jnp.dot(weights, jnp.concatenate(pieces, 0), preferred_element_type=F32).astype(BF16)
        for m in range(planes):
            message_ref[m] = total[:, m * half : (m + 1) * half]
        for index in range(planes, message_ref.shape[0]):
            message_ref[index] = jnp.zeros_like(message_ref[index])

    @pl.when(core == 1)
    def _():
        halo_ref = thirds[3]
        last = data(
            [halo_ref[2 * planes + 1]] + [third_value(core, thirds, planes - 1, row) for row in range(rows)]
        )
        for row in range(0, out_rows, 2):
            pieces = [jnp.concatenate([last[2 * row + at], last[2 * row + 2 + at]], 1) for at in range(3)]
            both = jnp.dot(w_ref[:, : 3 * taps], jnp.concatenate(pieces, 0), preferred_element_type=F32)
            both = both.astype(BF16)
            message_ref[row] = both[:, :half]
            message_ref[row + 1] = both[:, half:]
        corner = halo_ref[2 * planes]
        message_ref[out_rows, :chans] = corner[:, :half]
        message_ref[out_rows, chans:] = corner[:, half:]


def four_edges(core, thirds, local, weights):
    planes, rows, chans, width = thirds[0].shape
    outs = weights.shape[0]
    half = width // 2
    return pl.pallas_call(
        four_edges_kernel,
        out_shape=[
            jax.ShapeDtypeStruct((rows // 2 + 1, outs, half), BF16),
            jax.ShapeDtypeStruct((outs, 3 * chans), BF16),
        ],
        in_specs=inputs(len(thirds) + 3),
        compiler_params=pltpu.CompilerParams(vmem_limit_bytes=24 * MIB),
        cost_estimate=pl.CostEstimate(flops=10**9, bytes_accessed=10**6, transcendentals=0),
        name="four_edges",
    )(core, *thirds, local, weights, even_odd(width))


def four_kernel(core_ref, *refs):
    *thirds, local_ref, w_ref, place_ref, own_ref, theirs_ref, corner_ref, data_ref = refs
    core = core_ref[0]
    planes, rows, chans, width = thirds[0].shape
    halo_ref, gain_ref, shift_ref = thirds[3:]
    rows_ref = local_ref.at[planes : 2 * planes]
    half = width // 2
    out_rows, count = rows // 2, planes // 2
    taps = 3 * chans
    batch = 4
    data_ref[:, 0] = jnp.zeros_like(data_ref[:, 0])
    corner_ref[...] = corner_total(core, thirds, rows_ref)

    def put(values, first, spots):
        for tap, part in enumerate(spread((jnp.concatenate(values, 0),), place_ref[...])):
            part = part.astype(BF16)
            for at in range(len(values)):
                for slot, lanes in spots:
                    data_ref[
                        slot, first + at + 1, tap * chans : (tap + 1) * chans, lanes * half : (lanes + 1) * half
                    ] = part[at * chans : (at + 1) * chans]

    @pl.when(core == 0)
    def _():
        data_ref[0, :, :, :half] = jnp.zeros_like(data_ref[0, :, :, :half])

    @pl.when(core == 1)
    def _():
        total = local_ref[0].astype(F32) + halo_ref[planes - 1].astype(F32)
        prior = [activate(total, gain_ref[...], shift_ref[...]).astype(BF16)]
        prior += [local_ref[row] for row in range(1, rows)]
        for first in range(0, rows, batch):
            put(prior[first : first + batch], first, [(0, 0)])

    for plane in range(planes):
        spots = [(1 + plane % 2, plane // 2)]
        if plane % 2 and plane // 2 + 1 < count:
            spots.append((0, plane // 2 + 1))
        for first in range(0, rows, batch):
            put([third_value(core, thirds, plane, row, rows_ref) for row in range(first, first + batch)], first, spots)
    for row in range(out_rows):
        parts = [data_ref[slot, 2 * row : 2 * row + 3].reshape(3 * taps, count * half) for slot in range(3)]
        total = jnp.dot(w_ref[...], jnp.concatenate(parts, 0), preferred_element_type=F32)
        own_ref[row] = jnp.where(core == 0, total[:LANES], total[LANES:])
        theirs_ref[row] = jnp.where(core == 0, total[LANES:], total[:LANES])


def layer_four(core, thirds, local, weights):
    planes, rows, chans, width = thirds[0].shape
    outs = weights.shape[0]
    half = width // 2
    out_rows, count = rows // 2, planes // 2
    return pl.pallas_call(
        four_kernel,
        out_shape=[
            jax.ShapeDtypeStruct((out_rows, outs // 2, count * half), F32),
            jax.ShapeDtypeStruct((out_rows, outs // 2, count * half), F32),
            jax.ShapeDtypeStruct((chans, width), F32),
        ],
        in_specs=inputs(len(thirds) + 3),
        scratch_shapes=[pltpu.VMEM((3, rows + 1, 3 * chans, count * half), BF16)],
        compiler_params=pltpu.CompilerParams(vmem_limit_bytes=32 * MIB),
        cost_estimate=pl.CostEstimate(flops=4 * 10**9, bytes_accessed=4 * 10**6, transcendentals=0),
        name="layer_four",
    )(core, *thirds, local, weights, even_odd(width))


def shares_kernel(core_ref, corner_ref, halo_ref, mid_ref, place_ref, gain_ref, shift_ref, shares_ref, fix_ref):
    core = core_ref[0]
    rows = halo_ref.shape[0] - 1

    @pl.when(core == 0)
    def _():
        corner = halo_ref[rows].astype(F32)
        total = corner_ref[...] + jnp.concatenate([corner[:LANES], corner[LANES:]], 1)
        value = activate(total, gain_ref[...], shift_ref[...]).astype(BF16)
        data = jnp.concatenate([part.astype(BF16) for part in spread((value,), place_ref[...])], 0)
        fix = jnp.dot(mid_ref[...], data, preferred_element_type=F32)
        fix_ref[...] = fix[:LANES]
        shares_ref[...] = halo_ref[:rows, LANES:].astype(F32)
        shares_ref[0] += fix[LANES:]

    @pl.when(core == 1)
    def _():
        fix_ref[...] = jnp.zeros_like(fix_ref)
        shares_ref[...] = halo_ref[:rows, :LANES].astype(F32)


def assemble_kernel(
    core_ref, own_ref, got_ref, halo_ref, fix_ref, scales_ref, shares_ref, out_ref, lines_ref
):
    core = core_ref[0]
    gain, shift = scales_ref[:, 1:2], scales_ref[:, 2:3]
    rows, width = halo_ref.shape[0] - 1, halo_ref.shape[2]
    count = own_ref.shape[2] // width

    def put(row, parts):
        for at, total in enumerate(parts):
            value = activate(total, gain, shift)
            for m in range(count):
                place = row * 2 * count + at * count + m
                lines_ref[pl.ds(place, LANES, stride=rows * 2 * count), :] = value[:, m * width : (m + 1) * width]

    def with_edge(total, edge):
        return jnp.concatenate([total[:, :width] + edge, total[:, width:]], 1)

    @pl.when(core == 0)
    def _():
        for row in range(rows):
            edge = halo_ref[row, :LANES].astype(F32)
            if not row:
                edge = edge + fix_ref[...]
            total, got = with_edge(own_ref[row], edge), got_ref[row]
            if not row:
                first = [shares_ref[m] for m in range(2 * count)]
                total = total + jnp.concatenate(first[:count], 1)
                got = got + jnp.concatenate(first[count:], 1)
            put(row, (total, got))

    @pl.when(core == 1)
    def _():
        for row in range(rows):
            total, got = own_ref[row], with_edge(got_ref[row], shares_ref[row])
            if not row:
                first = [halo_ref[m, LANES:].astype(F32) for m in range(2 * count)]
                total = total + jnp.concatenate(first[count:], 1)
                got = got + jnp.concatenate(first[:count], 1)
            put(row, (got, total))

    out_ref[...] = lines_ref[...].astype(BF16)


def last_stage(core, own, theirs, corner, halo, mid, gain, shift, scales):
    rows, outs, lanes = own.shape
    got = swapped(theirs)
    shares, fix = pl.pallas_call(
        shares_kernel,
        out_shape=[
            jax.ShapeDtypeStruct((rows, outs, halo.shape[2]), F32),
            jax.ShapeDtypeStruct((outs, halo.shape[2]), F32),
        ],
        in_specs=inputs(6),
        compiler_params=pltpu.CompilerParams(vmem_limit_bytes=16 * MIB),
        cost_estimate=pl.CostEstimate(flops=10**8, bytes_accessed=10**6, transcendentals=0),
        name="shares",
    )(core, corner, halo, mid, even_odd(lanes), gain, shift)
    lines = (outs * rows * lanes * 2 // LANES, LANES)
    return pl.pallas_call(
        assemble_kernel,
        out_shape=jax.ShapeDtypeStruct(lines, BF16),
        in_specs=inputs(6),
        scratch_shapes=[pltpu.VMEM(lines, F32)],
        compiler_params=pltpu.CompilerParams(vmem_limit_bytes=16 * MIB),
        name="assemble",
    )(core, own, got, halo, fix, scales, swapped(shares))


def handed_on(message):
    count = lax.axis_size("sp")
    pairs = [(2 * b, 2 * (b + 1) + 1) for b in range(count) if b % ROW_BLOCKS != ROW_BLOCKS - 1]
    pairs += [(2 * b + 1, 2 * (b + ROW_BLOCKS)) for b in range(count - ROW_BLOCKS)]
    return lax.ppermute(message, ("sp", "fl"), pairs)


def swapped(value):
    return lax.ppermute(value, "fl", [(0, 1), (1, 0)])


def shards(volume, kernel_three, gain_three, shift_three, kernel_four, gain_four, shift_four):
    core = lax.axis_index("fl").reshape(1)
    own_scales = jnp.concatenate([gain_three, shift_three, gain_four, shift_four]).reshape(-1, LANES)
    picked, prior = three_picks(volume, core)
    others = lax.optimization_barrier((swapped(kernel_three), swapped(own_scales), swapped(kernel_four)))
    message, weights_three, gain, shift, scales = three_edges(
        picked, kernel_three, others[0], own_scales, others[1], core
    )
    weights_three, kernel_four = lax.optimization_barrier((weights_three, kernel_four))
    halo = handed_on(message)
    *thirds, local = layer_three(volume, prior, weights_three, gain, shift, core)
    planes = thirds[0].shape[0]
    passed = jnp.where(core[0] == 1, halo[:planes], local[planes : 2 * planes])
    local = swapped(lax.dynamic_update_slice(local, passed, (planes, 0, 0)))
    thirds = (*thirds, halo, gain, shift)
    weights_four = four_weights(kernel_four, others[2], core)
    message, mid = four_edges(core, thirds, local, weights_four)
    halo = handed_on(message)
    own, theirs, corner = layer_four(core, thirds, local, weights_four)
    lines = last_stage(core, own, theirs, corner, halo, mid, gain, shift, scales)
    out_rows, outs, lanes = own.shape
    fourth = lines.reshape(outs, out_rows, 2 * lanes // LANES, LANES)
    return jnp.transpose(fourth, (0, 2, 1, 3))[None]


def solution(mesh):
    return jax.shard_map(
        shards,
        mesh=mesh,
        in_specs=(
            P("sp", None, None, None, None),
            P("fl", None),
            P("fl"),
            P("fl"),
            P("fl", None),
            P("fl"),
            P("fl"),
        ),
        out_specs=P("sp", "fl", None, None, None),
        check_vma=False,
    )
```

```python
import functools

import jax
import jax.numpy as jnp
import numpy as np
from jax import lax
from jax.experimental import pallas as pl
from jax.experimental.pallas import tpu as pltpu
from jax.sharding import PartitionSpec as P

F32 = jnp.float32
BF16 = jnp.bfloat16
LANES = 128
ROW_BLOCKS = 8
SUB = 8
TAPS = 27
RIM_TAPS = tuple(9 * a + e for a in range(3) for e in range(3))
GROUP = 16
MIB = 2**20


def even_odd(width):
    half = width // 2
    place = np.zeros((width, width), np.float32)
    place[np.arange(0, width, 2), np.arange(half)] = 1
    place[np.arange(1, width, 2), half + np.arange(half)] = 1
    return jnp.asarray(place, BF16)


def activate(total, gain, shift):
    return jnp.maximum(total * gain + shift, 0.0)


def shifted(odd):
    lane = lax.broadcasted_iota(jnp.int32, odd.shape, 1)
    return jnp.where(lane == 0, 0.0, pltpu.roll(odd, 1, 1))


def spread(sides, place):
    quarter = place.shape[0] // 2
    split = [jnp.dot(side, place, preferred_element_type=F32) for side in sides]
    even = jnp.concatenate([part[:, :quarter] for part in split], 1)
    odd = jnp.concatenate([part[:, quarter:] for part in split], 1)
    return shifted(odd), even, odd


def separate(x_ref, plane, place_ref, split_refs, store):
    chans, rows, width = x_ref.shape[1], x_ref.shape[3], x_ref.shape[4]
    half = width // 2
    quarter = half // 2
    for index, first in enumerate(range(0, chans, GROUP)):
        split_ref = split_refs[index % len(split_refs)]
        x = x_ref[0, pl.ds(first, GROUP), plane]
        x = x.astype(F32).reshape(GROUP * rows, width).astype(BF16)
        for side in range(2):
            parts = jnp.dot(
                x[:, side * half : (side + 1) * half], place_ref[...], preferred_element_type=F32
            )
            for block in range(half // LANES):
                odd, at = divmod(block, quarter // LANES)
                split_ref[odd, side * (quarter // LANES) + at] = parts[:, block * LANES : (block + 1) * LANES]
        for row in range(rows):
            even, odd = (
                jnp.concatenate(
                    [split_ref[odd, at, pl.ds(row, GROUP, stride=rows), :] for at in range(half // LANES)], 1
                )
                for odd in range(2)
            )
            for tap, value in enumerate((shifted(odd), even, odd)):
                store(tap, row, first, value.astype(BF16))
        yield


def inputs(count):
    return [pl.BlockSpec(memory_space=pltpu.SMEM)] + [pl.BlockSpec(memory_space=pltpu.VMEM)] * count


def whole(own, other, core):
    first = jnp.where(core == 0, own, other)
    second = jnp.where(core == 0, other, own)
    return jnp.concatenate([first, second], 0)


def turn(kernel, turned_ref):
    columns = kernel.shape[1]
    for at in range(0, columns, LANES):
        size = min(LANES, columns - at)
        turned_ref[at : at + size, :] = kernel[:, at : at + size].T


def tap_major(turned_ref, taps, w_ref, first):
    chans = turned_ref.shape[0] // TAPS
    at = 0
    for index in range(0, len(taps), LANES // chans):
        parts = [turned_ref[pl.ds(tap, chans, stride=TAPS), :] for tap in taps[index : index + LANES // chans]]
        block = jnp.concatenate(parts, 0).T.astype(BF16)
        w_ref[first : first + LANES, at : at + block.shape[1]] = block
        at += block.shape[1]


def four_weights_kernel(core_ref, own_ref, other_ref, w_ref, *turned_refs):
    core = core_ref[0]
    for index, turned_ref in enumerate(turned_refs):
        turn(jnp.where(core == index, own_ref[...].astype(F32), other_ref[...].astype(F32)), turned_ref)
        tap_major(turned_ref, range(TAPS), w_ref, index * LANES)


def four_weights(own, other, core):
    outs, columns = own.shape
    return pl.pallas_call(
        four_weights_kernel,
        out_shape=jax.ShapeDtypeStruct((2 * outs, columns), BF16),
        in_specs=[
            pl.BlockSpec(memory_space=pltpu.SMEM),
            pl.BlockSpec(memory_space=pltpu.VMEM),
            pl.BlockSpec(memory_space=pltpu.VMEM),
        ],
        scratch_shapes=[pltpu.VMEM((columns, LANES), F32)] * 2,
        compiler_params=pltpu.CompilerParams(vmem_limit_bytes=16 * MIB),
        cost_estimate=pl.CostEstimate(flops=10**3, bytes_accessed=10**3, transcendentals=0),
        name="four_weights",
    )(core, own, other)


def three_picks_kernel(core_ref, last_ref, before_ref, rim_ref, picked_ref, prior_ref, *scratch):
    *split_refs, pick_ref, place_ref = scratch
    core, step, last = core_ref[0], pl.program_id(0), pl.num_programs(0) - 1
    chans, block, width = rim_ref.shape[1], rim_ref.shape[2], rim_ref.shape[4]
    rows, part = last_ref.shape[3], last_ref.shape[1]
    planes = block * 4
    half = width // 2
    rim = (rows - 1) % SUB

    @pl.when(step == 0)
    def _():
        source = lax.broadcasted_iota(jnp.int32, place_ref.shape, 0)
        target = lax.broadcasted_iota(jnp.int32, place_ref.shape, 1)
        quarter = half // 2
        wanted = jnp.where(target < quarter, 2 * target, 2 * (target - quarter) + 1)
        place_ref[...] = jnp.where(source == wanted, 1.0, 0.0).astype(BF16)

    def picked(spots):
        values, held = [], None
        for plane, row in spots:
            if plane != held:
                x = rim_ref[0, :, plane, :SUB].astype(F32).reshape(chans * SUB, width)
                for at in range(width // LANES):
                    pick_ref[plane % 2, at] = x[:, at * LANES : (at + 1) * LANES]
                held = plane
            values.append(
                jnp.concatenate(
                    [pick_ref[plane % 2, at, pl.ds(row, chans, stride=SUB), :] for at in range(width // LANES)], 1
                ).astype(BF16)
            )
        values = jnp.concatenate(values, 0)
        parts = [part.astype(BF16) for part in spread((values[:, :half], values[:, half:]), place_ref[...])]
        return [
            jnp.concatenate([part[at * chans : (at + 1) * chans] for part in parts], 0) for at in range(len(spots))
        ]

    @pl.when(core == 0)
    def _():
        for plane, data in enumerate(picked([(plane, rim) for plane in range(block)])):
            picked_ref[step * block + plane] = data

    @pl.when((core == 0) & (step == last))
    def _():
        spots = [(plane, row) for plane in range(block - 3, block) for row in range(rim - 2, rim + 1)]
        for index, data in enumerate(picked(spots)):
            picked_ref[planes + index] = data
        prior_ref[...] = jnp.zeros_like(prior_ref)

    @pl.when(core == 1)
    def _():
        for source_ref, to_ref in ((last_ref, picked_ref), (before_ref, prior_ref)):

            def store(tap, row, first, value):
                at = pl.multiple_of(tap * chans + step * part + first, GROUP)
                to_ref[row + 1, pl.ds(at, GROUP), :] = value

            for _ in separate(source_ref, 0, place_ref, split_refs, store):
                pass

    @pl.when((core == 1) & (step == last))
    def _():
        for ref in (picked_ref, prior_ref):
            ref[0] = jnp.zeros_like(ref[0])


def three_picks(volume, core):
    _, chans, planes, rows, width = volume.shape
    half = width // 2
    block, steps = planes // 4, 4
    shape = (rows + 1, 3 * chans, half)
    full = lambda *shape: pl.BlockSpec(shape, lambda i, core: (0,) * len(shape))
    return pl.pallas_call(
        three_picks_kernel,
        grid_spec=pltpu.PrefetchScalarGridSpec(
            num_scalar_prefetch=1,
            grid=(steps,),
            in_specs=[
                pl.BlockSpec((1, chans // steps, 1, rows, width), lambda i, core: (0, i * core[0], planes - 1, 0, 0)),
                pl.BlockSpec(
                    (1, chans // steps, 1, rows, width), lambda i, core: (0, i * core[0], planes // 2 - 1, 0, 0)
                ),
                pl.BlockSpec(
                    (1, chans, block, 2 * SUB, width),
                    lambda i, core: (0, 0, i + core[0] * (steps - 1 - i), (rows - 1) // (2 * SUB), 0),
                ),
            ],
            out_specs=[full(*shape), full(*shape)],
            scratch_shapes=[pltpu.VMEM((2, half // LANES, GROUP * rows, LANES), F32)] * 2
            + [pltpu.VMEM((2, width // LANES, chans * SUB, LANES), F32), pltpu.VMEM((half, half), BF16)],
        ),
        out_shape=[jax.ShapeDtypeStruct(shape, BF16)] * 2,
        compiler_params=pltpu.CompilerParams(vmem_limit_bytes=28 * MIB),
        cost_estimate=pl.CostEstimate(flops=10**9, bytes_accessed=10**7, transcendentals=0),
        name="three_picks",
    )(core, volume, volume, volume)


def three_edges_kernel(
    core_ref, picked_ref, own_ref, other_ref, own_scales_ref, other_scales_ref,
    message_ref, w_ref, gain_ref, shift_ref, scales_ref,
    turned_ref, rim_w_ref,
):
    core = core_ref[0]
    count, taps, half = picked_ref.shape
    out_rows = message_ref.shape[0]
    planes = count - 9
    turn(whole(own_ref[...].astype(F32), other_ref[...].astype(F32), core), turned_ref)
    tap_major(turned_ref, range(TAPS), w_ref, 0)
    own_scales, other_scales = own_scales_ref[...], other_scales_ref[...]
    lines = own_scales.shape[0]
    scales = jnp.concatenate([own_scales, other_scales, jnp.zeros((LANES - 2 * lines, LANES), F32)], 0).T
    scales_ref[...] = scales
    share = own_ref.shape[0]
    for ref, at in ((gain_ref, 0), (shift_ref, share)):
        ref[...] = whole(scales[at : at + share, 0:1], scales[at : at + share, lines : lines + 1], core)

    @pl.when(core == 0)
    def _():
        tap_major(turned_ref, RIM_TAPS, rim_w_ref, 0)
        none = jnp.zeros((taps, half), BF16)
        for index in range(planes // 2 + 1):
            pieces = [
                picked_ref[plane] if 0 <= plane < planes else none for plane in range(2 * index - 1, 2 * index + 2)
            ]
            total = jnp.dot(rim_w_ref[...], jnp.concatenate(pieces, 0), preferred_element_type=F32)
            message_ref[index] = total.astype(BF16)
        data = picked_ref[planes:].reshape(9 * taps, half)
        total = jnp.dot(w_ref[...], data, preferred_element_type=F32)
        message_ref[planes // 2 + 1] = activate(total, gain_ref[...], shift_ref[...]).astype(BF16)
        for index in range(planes // 2 + 2, out_rows):
            message_ref[index] = jnp.zeros_like(message_ref[index])

    @pl.when(core == 1)
    def _():
        for row in range(out_rows):
            total = jnp.dot(
                w_ref[:, : 3 * taps],
                picked_ref[2 * row : 2 * row + 3].reshape(3 * taps, half),
                preferred_element_type=F32,
            )
            message_ref[row] = total.astype(BF16)


def three_edges(picked, own, other, own_scales, other_scales, core):
    outs, columns = 2 * own.shape[0], own.shape[1]
    out_rows, half = picked.shape[0] // 2, picked.shape[2]
    shapes = [
        ((out_rows, outs, half), BF16),
        ((outs, columns), BF16),
        ((outs, 1), F32),
        ((outs, 1), F32),
        ((LANES, LANES), F32),
    ]
    return pl.pallas_call(
        three_edges_kernel,
        in_specs=inputs(5),
        out_shape=[jax.ShapeDtypeStruct(*shape) for shape in shapes],
        scratch_shapes=[pltpu.VMEM((columns, LANES), F32), pltpu.VMEM((outs, columns // 3), BF16)],
        compiler_params=pltpu.CompilerParams(vmem_limit_bytes=16 * MIB),
        cost_estimate=pl.CostEstimate(flops=10**9, bytes_accessed=10**6, transcendentals=0),
        name="three_edges",
    )(core, picked, own, other, own_scales, other_scales)


def three_kernel(
    core_ref, x_ref, before_ref, w_ref, place_ref, gain_ref, shift_ref,
    third_ref, plane_ref, row_ref, local_ref,
    *scratch,
):
    *split_refs, even_ref, odd_ref = scratch
    core, step, last = core_ref[0], pl.program_id(0), pl.num_programs(0) - 1
    chans, rows, width = x_ref.shape[1], x_ref.shape[3], x_ref.shape[4]
    half = width // 2
    out_rows = rows // 2
    taps = 3 * chans
    prior, new = (step + 1) % 2, step % 2

    @pl.when(step == 0)
    def _():
        odd_ref[1] = before_ref[...]
        even_ref[0] = jnp.zeros_like(even_ref[0])
        odd_ref[0, 0] = jnp.zeros_like(even_ref[0])

    def store_even(tap, row, first, value):
        even_ref[row + 1, tap * chans + first : tap * chans + first + GROUP, :] = value

    def store_odd(tap, row, first, value):
        odd_ref[new, row + 1, tap * chans + first : tap * chans + first + GROUP, :] = value

    for plane, store in enumerate((store_even, store_odd)):
        for _ in separate(x_ref, plane, place_ref, split_refs, store):
            pass

    def summing(keep):
        gain, shift = gain_ref[...], shift_ref[...]
        for row in range(out_rows):
            span = slice(2 * row, 2 * row + 3)
            parts = [odd_ref[prior, span], even_ref[span], odd_ref[new, span]]
            data = jnp.concatenate([part.reshape(3 * taps, half) for part in parts], 0)
            total = jnp.dot(w_ref[...], data, preferred_element_type=F32)
            third_ref[0, row] = activate(total, gain, shift).astype(BF16)
            if keep:
                plane_ref[row] = total
            if not row:
                row_ref[0] = total

    @pl.when(step == 0)
    def _():
        summing(True)

    @pl.when(step > 0)
    def _():
        summing(False)

    @pl.when(core == 1)
    def _():
        local_ref[step] = third_ref[0, out_rows - 1]

    @pl.when((step == last) & (core == 0))
    def _():
        local_ref[...] = third_ref[0]
        local_ref[0] = row_ref[0].astype(BF16)


def layer_three(volume, prior, weights, gain, shift, core):
    _, chans, planes, rows, width = volume.shape
    outs = weights.shape[0]
    half = width // 2
    steps, out_rows = planes // 4, rows // 2
    full = lambda *shape: pl.BlockSpec(shape, lambda i, core: (0,) * len(shape))
    return pl.pallas_call(
        three_kernel,
        grid_spec=pltpu.PrefetchScalarGridSpec(
            num_scalar_prefetch=1,
            grid=(steps,),
            in_specs=[
                pl.BlockSpec((1, chans, 2, rows, width), lambda i, core: (0, 0, core[0] * steps + i, 0, 0)),
                pl.BlockSpec(prior.shape, lambda i, core: (0, 0, 0), pipeline_mode=pl.Buffered(1)),
                full(*weights.shape),
                full(half, half),
                full(outs, 1),
                full(outs, 1),
            ],
            out_specs=[
                pl.BlockSpec((1, out_rows, outs, half), lambda i, core: (i, 0, 0, 0)),
                full(out_rows, outs, half),
                pl.BlockSpec((1, outs, half), lambda i, core: (i, 0, 0)),
                full(out_rows, outs, half),
            ],
            scratch_shapes=[pltpu.VMEM((2, half // LANES, GROUP * rows, LANES), F32)] * 4
            + [
                pltpu.VMEM((rows + 1, 3 * chans, half), BF16),
                pltpu.VMEM((2, rows + 1, 3 * chans, half), BF16),
            ],
        ),
        out_shape=[
            jax.ShapeDtypeStruct((steps, out_rows, outs, half), BF16),
            jax.ShapeDtypeStruct((out_rows, outs, half), F32),
            jax.ShapeDtypeStruct((steps, outs, half), F32),
            jax.ShapeDtypeStruct((out_rows, outs, half), BF16),
        ],
        compiler_params=pltpu.CompilerParams(vmem_limit_bytes=34 * MIB),
        cost_estimate=pl.CostEstimate(flops=10**10, bytes_accessed=2 * 10**7, transcendentals=0),
        name="layer_three",
    )(core, volume, prior, weights, even_odd(half), gain, shift)


def corner_total(core, refs, rows_ref):
    third_ref, plane_ref, _, halo_ref, _, _ = refs
    planes = third_ref.shape[0]
    first = jnp.where(core == 0, rows_ref[0].astype(F32), halo_ref[planes].astype(F32))
    return plane_ref[0] + jnp.where(core == 0, halo_ref[0].astype(F32), 0.0) + first


def third_value(core, refs, plane, row, rows_ref=None):
    third_ref, plane_ref, row_ref, halo_ref, gain_ref, shift_ref = refs
    planes = third_ref.shape[0]
    if plane and row:
        return third_ref[plane, row]
    if plane:
        share = halo_ref[planes + plane].astype(F32)
        if rows_ref is not None:
            share = jnp.where(core == 0, rows_ref[plane].astype(F32), share)
        total = row_ref[plane] + share
    elif row:
        total = plane_ref[row] + jnp.where(core == 0, halo_ref[row].astype(F32), 0.0)
    else:
        total = corner_total(core, refs, rows_ref)
    value = activate(total, gain_ref[...], shift_ref[...])
    if not plane and not row:
        value = jnp.where(core == 0, 0.0, value)
    return value.astype(BF16)


def four_edges_kernel(core_ref, *refs):
    *thirds, local_ref, w_ref, place_ref, message_ref, mid_ref, rows_ref = refs
    core = core_ref[0]
    planes, rows, chans, width = thirds[0].shape
    rows_ref[...] = thirds[3][:planes]
    half = width // 2
    out_rows = rows // 2
    taps = 3 * chans
    mid_ref[...] = w_ref[:, 4 * taps : 5 * taps]

    def data(values):
        parts = [part.astype(BF16) for part in spread((jnp.concatenate(values, 0),), place_ref[...])]
        return [
            jnp.concatenate([part[at * chans : (at + 1) * chans] for part in parts], 0) for at in range(len(values))
        ]

    @pl.when(core == 0)
    def _():
        none = jnp.zeros((taps, half), BF16)
        rim = [none] + data(
            [third_value(core, thirds, plane, rows - 1) for plane in range(planes)]
            + [local_ref[plane] for plane in range(planes)]
        )
        pieces = [jnp.concatenate([rim[2 * m + slot] for m in range(planes)], 1) for slot in range(3)]
        weights = jnp.concatenate([w_ref[:, 3 * slot * taps : (3 * slot + 1) * taps] for slot in range(3)], 1)
        total = jnp.dot(weights, jnp.concatenate(pieces, 0), preferred_element_type=F32).astype(BF16)
        for m in range(planes):
            message_ref[m] = total[:, m * half : (m + 1) * half]
        for index in range(planes, message_ref.shape[0]):
            message_ref[index] = jnp.zeros_like(message_ref[index])

    @pl.when(core == 1)
    def _():
        halo_ref = thirds[3]
        last = data(
            [halo_ref[2 * planes + 1]] + [third_value(core, thirds, planes - 1, row) for row in range(rows)]
        )
        for row in range(0, out_rows, 2):
            pieces = [jnp.concatenate([last[2 * row + at], last[2 * row + 2 + at]], 1) for at in range(3)]
            both = jnp.dot(w_ref[:, : 3 * taps], jnp.concatenate(pieces, 0), preferred_element_type=F32)
            both = both.astype(BF16)
            message_ref[row] = both[:, :half]
            message_ref[row + 1] = both[:, half:]
        corner = halo_ref[2 * planes]
        message_ref[out_rows, :chans] = corner[:, :half]
        message_ref[out_rows, chans:] = corner[:, half:]


def four_edges(core, thirds, local, weights):
    planes, rows, chans, width = thirds[0].shape
    outs = weights.shape[0]
    half = width // 2
    return pl.pallas_call(
        four_edges_kernel,
        out_shape=[
            jax.ShapeDtypeStruct((rows // 2 + 1, outs, half), BF16),
            jax.ShapeDtypeStruct((outs, 3 * chans), BF16),
            jax.ShapeDtypeStruct((planes, chans, width), BF16),
        ],
        in_specs=inputs(len(thirds) + 3),
        compiler_params=pltpu.CompilerParams(vmem_limit_bytes=24 * MIB),
        cost_estimate=pl.CostEstimate(flops=10**9, bytes_accessed=10**6, transcendentals=0),
        name="four_edges",
    )(core, *thirds, local, weights, even_odd(width))


def four_kernel(core_ref, *refs):
    *thirds, rows_ref, local_ref, w_ref, place_ref, own_ref, theirs_ref, corner_ref, data_ref = refs
    core = core_ref[0]
    planes, rows, chans, width = thirds[0].shape
    halo_ref, gain_ref, shift_ref = thirds[3:]
    half = width // 2
    out_rows, count = rows // 2, planes // 2
    taps = 3 * chans
    batch = 4
    data_ref[:, 0] = jnp.zeros_like(data_ref[:, 0])
    corner_ref[...] = corner_total(core, thirds, rows_ref)

    def put(values, first, spots):
        for tap, part in enumerate(spread((jnp.concatenate(values, 0),), place_ref[...])):
            part = part.astype(BF16)
            for at in range(len(values)):
                for slot, lanes in spots:
                    data_ref[
                        slot, first + at + 1, tap * chans : (tap + 1) * chans, lanes * half : (lanes + 1) * half
                    ] = part[at * chans : (at + 1) * chans]

    @pl.when(core == 0)
    def _():
        data_ref[0, :, :, :half] = jnp.zeros_like(data_ref[0, :, :, :half])

    @pl.when(core == 1)
    def _():
        total = local_ref[0].astype(F32) + halo_ref[planes - 1].astype(F32)
        prior = [activate(total, gain_ref[...], shift_ref[...]).astype(BF16)]
        prior += [local_ref[row] for row in range(1, rows)]
        for first in range(0, rows, batch):
            put(prior[first : first + batch], first, [(0, 0)])

    for plane in range(planes):
        spots = [(1 + plane % 2, plane // 2)]
        if plane % 2 and plane // 2 + 1 < count:
            spots.append((0, plane // 2 + 1))
        for first in range(0, rows, batch):
            put([third_value(core, thirds, plane, row, rows_ref) for row in range(first, first + batch)], first, spots)
    for row in range(out_rows):
        parts = [data_ref[slot, 2 * row : 2 * row + 3].reshape(3 * taps, count * half) for slot in range(3)]
        total = jnp.dot(w_ref[...], jnp.concatenate(parts, 0), preferred_element_type=F32)
        own_ref[row] = jnp.where(core == 0, total[:LANES], total[LANES:])
        theirs_ref[row] = jnp.where(core == 0, total[LANES:], total[:LANES])


def layer_four(core, thirds, rows_before, local, weights):
    planes, rows, chans, width = thirds[0].shape
    outs = weights.shape[0]
    half = width // 2
    out_rows, count = rows // 2, planes // 2
    return pl.pallas_call(
        four_kernel,
        out_shape=[
            jax.ShapeDtypeStruct((out_rows, outs // 2, count * half), F32),
            jax.ShapeDtypeStruct((out_rows, outs // 2, count * half), F32),
            jax.ShapeDtypeStruct((chans, width), F32),
        ],
        in_specs=inputs(len(thirds) + 4),
        scratch_shapes=[pltpu.VMEM((3, rows + 1, 3 * chans, count * half), BF16)],
        compiler_params=pltpu.CompilerParams(vmem_limit_bytes=32 * MIB),
        cost_estimate=pl.CostEstimate(flops=4 * 10**9, bytes_accessed=4 * 10**6, transcendentals=0),
        name="layer_four",
    )(core, *thirds, rows_before, local, weights, even_odd(width))


def shares_kernel(core_ref, corner_ref, halo_ref, mid_ref, place_ref, gain_ref, shift_ref, shares_ref, fix_ref):
    core = core_ref[0]
    rows = halo_ref.shape[0] - 1

    @pl.when(core == 0)
    def _():
        corner = halo_ref[rows].astype(F32)
        total = corner_ref[...] + jnp.concatenate([corner[:LANES], corner[LANES:]], 1)
        value = activate(total, gain_ref[...], shift_ref[...]).astype(BF16)
        data = jnp.concatenate([part.astype(BF16) for part in spread((value,), place_ref[...])], 0)
        fix = jnp.dot(mid_ref[...], data, preferred_element_type=F32)
        fix_ref[...] = fix[:LANES]
        shares_ref[...] = halo_ref[:rows, LANES:].astype(F32)
        shares_ref[0] += fix[LANES:]

    @pl.when(core == 1)
    def _():
        fix_ref[...] = jnp.zeros_like(fix_ref)
        shares_ref[...] = halo_ref[:rows, :LANES].astype(F32)


def assemble_kernel(
    core_ref, own_ref, got_ref, halo_ref, fix_ref, scales_ref, shares_ref, out_ref, lines_ref
):
    core = core_ref[0]
    gain, shift = scales_ref[:, 1:2], scales_ref[:, 2:3]
    rows, width = halo_ref.shape[0] - 1, halo_ref.shape[2]
    count = own_ref.shape[2] // width

    def put(row, parts):
        for at, total in enumerate(parts):
            value = activate(total, gain, shift)
            for m in range(count):
                place = row * 2 * count + at * count + m
                lines_ref[pl.ds(place, LANES, stride=rows * 2 * count), :] = value[:, m * width : (m + 1) * width]

    def with_edge(total, edge):
        return jnp.concatenate([total[:, :width] + edge, total[:, width:]], 1)

    @pl.when(core == 0)
    def _():
        for row in range(rows):
            edge = halo_ref[row, :LANES].astype(F32)
            if not row:
                edge = edge + fix_ref[...]
            total, got = with_edge(own_ref[row], edge), got_ref[row]
            if not row:
                first = [shares_ref[m] for m in range(2 * count)]
                total = total + jnp.concatenate(first[:count], 1)
                got = got + jnp.concatenate(first[count:], 1)
            put(row, (total, got))

    @pl.when(core == 1)
    def _():
        for row in range(rows):
            total, got = own_ref[row], with_edge(got_ref[row], shares_ref[row])
            if not row:
                first = [halo_ref[m, LANES:].astype(F32) for m in range(2 * count)]
                total = total + jnp.concatenate(first[count:], 1)
                got = got + jnp.concatenate(first[:count], 1)
            put(row, (got, total))

    out_ref[...] = lines_ref[...].astype(BF16)


def last_stage(core, own, theirs, corner, halo, mid, gain, shift, scales):
    rows, outs, lanes = own.shape
    got = swapped(theirs)
    shares, fix = pl.pallas_call(
        shares_kernel,
        out_shape=[
            jax.ShapeDtypeStruct((rows, outs, halo.shape[2]), F32),
            jax.ShapeDtypeStruct((outs, halo.shape[2]), F32),
        ],
        in_specs=inputs(6),
        compiler_params=pltpu.CompilerParams(vmem_limit_bytes=16 * MIB),
        cost_estimate=pl.CostEstimate(flops=10**8, bytes_accessed=10**6, transcendentals=0),
        name="shares",
    )(core, corner, halo, mid, even_odd(lanes), gain, shift)
    lines = (outs * rows * lanes * 2 // LANES, LANES)
    return pl.pallas_call(
        assemble_kernel,
        out_shape=jax.ShapeDtypeStruct(lines, BF16),
        in_specs=inputs(6),
        scratch_shapes=[pltpu.VMEM(lines, F32)],
        compiler_params=pltpu.CompilerParams(vmem_limit_bytes=16 * MIB),
        name="assemble",
    )(core, own, got, halo, fix, scales, swapped(shares))


def handed_on(message):
    count = lax.axis_size("sp")
    pairs = [(2 * b, 2 * (b + 1) + 1) for b in range(count) if b % ROW_BLOCKS != ROW_BLOCKS - 1]
    pairs += [(2 * b + 1, 2 * (b + ROW_BLOCKS)) for b in range(count - ROW_BLOCKS)]
    return lax.ppermute(message, ("sp", "fl"), pairs)


def swapped(value):
    return lax.ppermute(value, "fl", [(0, 1), (1, 0)])


def shards(volume, kernel_three, gain_three, shift_three, kernel_four, gain_four, shift_four):
    core = lax.axis_index("fl").reshape(1)
    own_scales = jnp.concatenate([gain_three, shift_three, gain_four, shift_four]).reshape(-1, LANES)
    picked, prior = three_picks(volume, core)
    others = lax.optimization_barrier((swapped(kernel_three), swapped(own_scales), swapped(kernel_four)))
    message, weights_three, gain, shift, scales = three_edges(
        picked, kernel_three, others[0], own_scales, others[1], core
    )
    halo = handed_on(message)
    *thirds, local = layer_three(volume, prior, weights_three, gain, shift, core)
    halo, local = lax.optimization_barrier((halo, local))
    thirds = (*thirds, halo, gain, shift)
    local = swapped(local)
    weights_four = four_weights(kernel_four, others[2], core)
    message, mid, rows = four_edges(core, thirds, local, weights_four)
    halo = handed_on(message)
    rows = lax.ppermute(rows, "fl", [(1, 0)])
    own, theirs, corner = layer_four(core, thirds, rows, local, weights_four)
    lines = last_stage(core, own, theirs, corner, halo, mid, gain, shift, scales)
    out_rows, outs, lanes = own.shape
    fourth = lines.reshape(outs, out_rows, 2 * lanes // LANES, LANES)
    return jnp.transpose(fourth, (0, 2, 1, 3))[None]


def solution(mesh):
    return jax.shard_map(
        shards,
        mesh=mesh,
        in_specs=(
            P("sp", None, None, None, None),
            P("fl", None),
            P("fl"),
            P("fl"),
            P("fl", None),
            P("fl"),
            P("fl"),
        ),
        out_specs=P("sp", "fl", None, None, None),
        check_vma=False,
    )
```

```python
import functools

import jax
import jax.numpy as jnp
import numpy as np
from jax import lax
from jax.experimental import pallas as pl
from jax.experimental.pallas import tpu as pltpu
from jax.sharding import PartitionSpec as P

F32 = jnp.float32
BF16 = jnp.bfloat16
LANES = 128
ROW_BLOCKS = 8
SUB = 8
TAPS = 27
RIM_TAPS = tuple(9 * a + e for a in range(3) for e in range(3))
GROUP = 16
MIB = 2**20


def even_odd(width):
    half = width // 2
    place = np.zeros((width, width), np.float32)
    place[np.arange(0, width, 2), np.arange(half)] = 1
    place[np.arange(1, width, 2), half + np.arange(half)] = 1
    return jnp.asarray(place, BF16)


def activate(total, gain, shift):
    return jnp.maximum(total * gain + shift, 0.0)


def shifted(odd):
    lane = lax.broadcasted_iota(jnp.int32, odd.shape, 1)
    return jnp.where(lane == 0, 0.0, pltpu.roll(odd, 1, 1))


def spread(sides, place):
    quarter = place.shape[0] // 2
    split = [jnp.dot(side, place, preferred_element_type=F32) for side in sides]
    even = jnp.concatenate([part[:, :quarter] for part in split], 1)
    odd = jnp.concatenate([part[:, quarter:] for part in split], 1)
    return shifted(odd), even, odd


def separate(x_ref, plane, place_ref, split_refs, store):
    chans, rows, width = x_ref.shape[1], x_ref.shape[3], x_ref.shape[4]
    half = width // 2
    quarter = half // 2
    for index, first in enumerate(range(0, chans, GROUP)):
        split_ref = split_refs[index % len(split_refs)]
        x = x_ref[0, pl.ds(first, GROUP), plane]
        x = x.astype(F32).reshape(GROUP * rows, width).astype(BF16)
        for side in range(2):
            parts = jnp.dot(
                x[:, side * half : (side + 1) * half], place_ref[...], preferred_element_type=F32
            )
            for block in range(half // LANES):
                odd, at = divmod(block, quarter // LANES)
                split_ref[odd, side * (quarter // LANES) + at] = parts[:, block * LANES : (block + 1) * LANES]
        for row in range(rows):
            even, odd = (
                jnp.concatenate(
                    [split_ref[odd, at, pl.ds(row, GROUP, stride=rows), :] for at in range(half // LANES)], 1
                )
                for odd in range(2)
            )
            for tap, value in enumerate((shifted(odd), even, odd)):
                store(tap, row, first, value.astype(BF16))
        yield


def inputs(count):
    return [pl.BlockSpec(memory_space=pltpu.SMEM)] + [pl.BlockSpec(memory_space=pltpu.VMEM)] * count


def whole(own, other, core):
    first = jnp.where(core == 0, own, other)
    second = jnp.where(core == 0, other, own)
    return jnp.concatenate([first, second], 0)


def turn(kernel, turned_ref):
    columns = kernel.shape[1]
    for at in range(0, columns, LANES):
        size = min(LANES, columns - at)
        turned_ref[at : at + size, :] = kernel[:, at : at + size].T


def tap_major(turned_ref, taps, w_ref, first):
    chans = turned_ref.shape[0] // TAPS
    at = 0
    for index in range(0, len(taps), LANES // chans):
        parts = [turned_ref[pl.ds(tap, chans, stride=TAPS), :] for tap in taps[index : index + LANES // chans]]
        block = jnp.concatenate(parts, 0).T.astype(BF16)
        w_ref[first : first + LANES, at : at + block.shape[1]] = block
        at += block.shape[1]


def four_weights_kernel(core_ref, own_ref, other_ref, w_ref, *turned_refs):
    core = core_ref[0]
    for index, turned_ref in enumerate(turned_refs):
        turn(jnp.where(core == index, own_ref[...].astype(F32), other_ref[...].astype(F32)), turned_ref)
        tap_major(turned_ref, range(TAPS), w_ref, index * LANES)


def four_weights(own, other, core):
    outs, columns = own.shape
    return pl.pallas_call(
        four_weights_kernel,
        out_shape=jax.ShapeDtypeStruct((2 * outs, columns), BF16),
        in_specs=[
            pl.BlockSpec(memory_space=pltpu.SMEM),
            pl.BlockSpec(memory_space=pltpu.VMEM),
            pl.BlockSpec(memory_space=pltpu.VMEM),
        ],
        scratch_shapes=[pltpu.VMEM((columns, LANES), F32)] * 2,
        compiler_params=pltpu.CompilerParams(vmem_limit_bytes=16 * MIB),
        cost_estimate=pl.CostEstimate(flops=10**3, bytes_accessed=10**3, transcendentals=0),
        name="four_weights",
    )(core, own, other)


def three_picks_kernel(core_ref, last_ref, before_ref, rim_ref, picked_ref, prior_ref, *scratch):
    *split_refs, pick_ref, place_ref = scratch
    core, step, last = core_ref[0], pl.program_id(0), pl.num_programs(0) - 1
    chans, block, width = rim_ref.shape[1], rim_ref.shape[2], rim_ref.shape[4]
    rows, part = last_ref.shape[3], last_ref.shape[1]
    planes = block * 4
    half = width // 2
    rim = (rows - 1) % SUB

    @pl.when(step == 0)
    def _():
        source = lax.broadcasted_iota(jnp.int32, place_ref.shape, 0)
        target = lax.broadcasted_iota(jnp.int32, place_ref.shape, 1)
        quarter = half // 2
        wanted = jnp.where(target < quarter, 2 * target, 2 * (target - quarter) + 1)
        place_ref[...] = jnp.where(source == wanted, 1.0, 0.0).astype(BF16)

    def picked(spots):
        values, held = [], None
        for plane, row in spots:
            if plane != held:
                x = rim_ref[0, :, plane, :SUB].astype(F32).reshape(chans * SUB, width)
                for at in range(width // LANES):
                    pick_ref[plane % 2, at] = x[:, at * LANES : (at + 1) * LANES]
                held = plane
            values.append(
                jnp.concatenate(
                    [pick_ref[plane % 2, at, pl.ds(row, chans, stride=SUB), :] for at in range(width // LANES)], 1
                ).astype(BF16)
            )
        values = jnp.concatenate(values, 0)
        parts = [part.astype(BF16) for part in spread((values[:, :half], values[:, half:]), place_ref[...])]
        return [
            jnp.concatenate([part[at * chans : (at + 1) * chans] for part in parts], 0) for at in range(len(spots))
        ]

    @pl.when(core == 0)
    def _():
        for plane, data in enumerate(picked([(plane, rim) for plane in range(block)])):
            picked_ref[step * block + plane] = data

    @pl.when((core == 0) & (step == last))
    def _():
        spots = [(plane, row) for plane in range(block - 3, block) for row in range(rim - 2, rim + 1)]
        for index, data in enumerate(picked(spots)):
            picked_ref[planes + index] = data
        prior_ref[...] = jnp.zeros_like(prior_ref)

    @pl.when(core == 1)
    def _():
        for source_ref, to_ref in ((last_ref, picked_ref), (before_ref, prior_ref)):

            def store(tap, row, first, value):
                at = pl.multiple_of(tap * chans + step * part + first, GROUP)
                to_ref[row + 1, pl.ds(at, GROUP), :] = value

            for _ in separate(source_ref, 0, place_ref, split_refs, store):
                pass

    @pl.when((core == 1) & (step == last))
    def _():
        for ref in (picked_ref, prior_ref):
            ref[0] = jnp.zeros_like(ref[0])


def three_picks(volume, core):
    _, chans, planes, rows, width = volume.shape
    half = width // 2
    block, steps = planes // 4, 4
    shape = (rows + 1, 3 * chans, half)
    full = lambda *shape: pl.BlockSpec(shape, lambda i, core: (0,) * len(shape))
    return pl.pallas_call(
        three_picks_kernel,
        grid_spec=pltpu.PrefetchScalarGridSpec(
            num_scalar_prefetch=1,
            grid=(steps,),
            in_specs=[
                pl.BlockSpec((1, chans // steps, 1, rows, width), lambda i, core: (0, i * core[0], planes - 1, 0, 0)),
                pl.BlockSpec(
                    (1, chans // steps, 1, rows, width), lambda i, core: (0, i * core[0], planes // 2 - 1, 0, 0)
                ),
                pl.BlockSpec(
                    (1, chans, block, 2 * SUB, width),
                    lambda i, core: (0, 0, i + core[0] * (steps - 1 - i), (rows - 1) // (2 * SUB), 0),
                ),
            ],
            out_specs=[full(*shape), full(*shape)],
            scratch_shapes=[pltpu.VMEM((2, half // LANES, GROUP * rows, LANES), F32)] * 2
            + [pltpu.VMEM((2, width // LANES, chans * SUB, LANES), F32), pltpu.VMEM((half, half), BF16)],
        ),
        out_shape=[jax.ShapeDtypeStruct(shape, BF16)] * 2,
        compiler_params=pltpu.CompilerParams(vmem_limit_bytes=28 * MIB),
        cost_estimate=pl.CostEstimate(flops=10**9, bytes_accessed=10**7, transcendentals=0),
        name="three_picks",
    )(core, volume, volume, volume)


def three_edges_kernel(
    core_ref, picked_ref, own_ref, other_ref, own_scales_ref, other_scales_ref,
    message_ref, w_ref, gain_ref, shift_ref, scales_ref,
    turned_ref, rim_w_ref,
):
    core = core_ref[0]
    count, taps, half = picked_ref.shape
    out_rows = message_ref.shape[0]
    planes = count - 9
    turn(whole(own_ref[...].astype(F32), other_ref[...].astype(F32), core), turned_ref)
    tap_major(turned_ref, range(TAPS), w_ref, 0)
    own_scales, other_scales = own_scales_ref[...], other_scales_ref[...]
    lines = own_scales.shape[0]
    scales = jnp.concatenate([own_scales, other_scales, jnp.zeros((LANES - 2 * lines, LANES), F32)], 0).T
    scales_ref[...] = scales
    share = own_ref.shape[0]
    for ref, at in ((gain_ref, 0), (shift_ref, share)):
        ref[...] = whole(scales[at : at + share, 0:1], scales[at : at + share, lines : lines + 1], core)

    @pl.when(core == 0)
    def _():
        tap_major(turned_ref, RIM_TAPS, rim_w_ref, 0)
        none = jnp.zeros((taps, half), BF16)
        for index in range(planes // 2 + 1):
            pieces = [
                picked_ref[plane] if 0 <= plane < planes else none for plane in range(2 * index - 1, 2 * index + 2)
            ]
            total = jnp.dot(rim_w_ref[...], jnp.concatenate(pieces, 0), preferred_element_type=F32)
            message_ref[index] = total.astype(BF16)
        data = picked_ref[planes:].reshape(9 * taps, half)
        total = jnp.dot(w_ref[...], data, preferred_element_type=F32)
        message_ref[planes // 2 + 1] = activate(total, gain_ref[...], shift_ref[...]).astype(BF16)
        for index in range(planes // 2 + 2, out_rows):
            message_ref[index] = jnp.zeros_like(message_ref[index])

    @pl.when(core == 1)
    def _():
        for row in range(out_rows):
            total = jnp.dot(
                w_ref[:, : 3 * taps],
                picked_ref[2 * row : 2 * row + 3].reshape(3 * taps, half),
                preferred_element_type=F32,
            )
            message_ref[row] = total.astype(BF16)


def three_edges(picked, own, other, own_scales, other_scales, core):
    outs, columns = 2 * own.shape[0], own.shape[1]
    out_rows, half = picked.shape[0] // 2, picked.shape[2]
    shapes = [
        ((out_rows, outs, half), BF16),
        ((outs, columns), BF16),
        ((outs, 1), F32),
        ((outs, 1), F32),
        ((LANES, LANES), F32),
    ]
    return pl.pallas_call(
        three_edges_kernel,
        in_specs=inputs(5),
        out_shape=[jax.ShapeDtypeStruct(*shape) for shape in shapes],
        scratch_shapes=[pltpu.VMEM((columns, LANES), F32), pltpu.VMEM((outs, columns // 3), BF16)],
        compiler_params=pltpu.CompilerParams(vmem_limit_bytes=16 * MIB),
        cost_estimate=pl.CostEstimate(flops=10**9, bytes_accessed=10**6, transcendentals=0),
        name="three_edges",
    )(core, picked, own, other, own_scales, other_scales)


def three_kernel(
    core_ref, x_ref, before_ref, w_ref, place_ref, gain_ref, shift_ref,
    third_ref, plane_ref, row_ref, local_ref,
    *scratch,
):
    *split_refs, even_ref, odd_ref = scratch
    core, step, last = core_ref[0], pl.program_id(0), pl.num_programs(0) - 1
    chans, rows, width = x_ref.shape[1], x_ref.shape[3], x_ref.shape[4]
    half = width // 2
    out_rows = rows // 2
    taps = 3 * chans
    prior, new = (step + 1) % 2, step % 2

    @pl.when(step == 0)
    def _():
        odd_ref[1] = before_ref[...]
        even_ref[0] = jnp.zeros_like(even_ref[0])
        odd_ref[0, 0] = jnp.zeros_like(even_ref[0])

    def store_even(tap, row, first, value):
        even_ref[row + 1, tap * chans + first : tap * chans + first + GROUP, :] = value

    def store_odd(tap, row, first, value):
        odd_ref[new, row + 1, tap * chans + first : tap * chans + first + GROUP, :] = value

    for plane, store in enumerate((store_even, store_odd)):
        for _ in separate(x_ref, plane, place_ref, split_refs, store):
            pass

    def summing(keep):
        gain, shift = gain_ref[...], shift_ref[...]
        for row in range(out_rows):
            span = slice(2 * row, 2 * row + 3)
            parts = [odd_ref[prior, span], even_ref[span], odd_ref[new, span]]
            data = jnp.concatenate([part.reshape(3 * taps, half) for part in parts], 0)
            total = jnp.dot(w_ref[...], data, preferred_element_type=F32)
            third_ref[0, row] = activate(total, gain, shift).astype(BF16)
            if keep:
                plane_ref[row] = total
            if not row:
                row_ref[0] = total

    @pl.when(step == 0)
    def _():
        summing(True)

    @pl.when(step > 0)
    def _():
        summing(False)

    @pl.when(core == 1)
    def _():
        local_ref[step] = third_ref[0, out_rows - 1]

    @pl.when((step == last) & (core == 0))
    def _():
        local_ref[...] = third_ref[0]
        local_ref[0] = row_ref[0].astype(BF16)


def layer_three(volume, prior, weights, gain, shift, core):
    _, chans, planes, rows, width = volume.shape
    outs = weights.shape[0]
    half = width // 2
    steps, out_rows = planes // 4, rows // 2
    full = lambda *shape: pl.BlockSpec(shape, lambda i, core: (0,) * len(shape))
    return pl.pallas_call(
        three_kernel,
        grid_spec=pltpu.PrefetchScalarGridSpec(
            num_scalar_prefetch=1,
            grid=(steps,),
            in_specs=[
                pl.BlockSpec((1, chans, 2, rows, width), lambda i, core: (0, 0, core[0] * steps + i, 0, 0)),
                pl.BlockSpec(prior.shape, lambda i, core: (0, 0, 0), pipeline_mode=pl.Buffered(1)),
                full(*weights.shape),
                full(half, half),
                full(outs, 1),
                full(outs, 1),
            ],
            out_specs=[
                pl.BlockSpec((1, out_rows, outs, half), lambda i, core: (i, 0, 0, 0)),
                full(out_rows, outs, half),
                pl.BlockSpec((1, outs, half), lambda i, core: (i, 0, 0)),
                full(out_rows, outs, half),
            ],
            scratch_shapes=[pltpu.VMEM((2, half // LANES, GROUP * rows, LANES), F32)] * 4
            + [
                pltpu.VMEM((rows + 1, 3 * chans, half), BF16),
                pltpu.VMEM((2, rows + 1, 3 * chans, half), BF16),
            ],
        ),
        out_shape=[
            jax.ShapeDtypeStruct((steps, out_rows, outs, half), BF16),
            jax.ShapeDtypeStruct((out_rows, outs, half), F32),
            jax.ShapeDtypeStruct((steps, outs, half), F32),
            jax.ShapeDtypeStruct((out_rows, outs, half), BF16),
        ],
        compiler_params=pltpu.CompilerParams(vmem_limit_bytes=34 * MIB),
        cost_estimate=pl.CostEstimate(flops=10**10, bytes_accessed=2 * 10**7, transcendentals=0),
        name="layer_three",
    )(core, volume, prior, weights, even_odd(half), gain, shift)


def corner_total(core, refs, rows_ref):
    third_ref, plane_ref, _, halo_ref, _, _ = refs
    planes = third_ref.shape[0]
    first = jnp.where(core == 0, rows_ref[0].astype(F32), halo_ref[planes].astype(F32))
    return plane_ref[0] + jnp.where(core == 0, halo_ref[0].astype(F32), 0.0) + first


def third_value(core, refs, plane, row, rows_ref=None):
    third_ref, plane_ref, row_ref, halo_ref, gain_ref, shift_ref = refs
    planes = third_ref.shape[0]
    if plane and row:
        return third_ref[plane, row]
    if plane:
        share = halo_ref[planes + plane].astype(F32)
        if rows_ref is not None:
            share = jnp.where(core == 0, rows_ref[plane].astype(F32), share)
        total = row_ref[plane] + share
    elif row:
        total = plane_ref[row] + jnp.where(core == 0, halo_ref[row].astype(F32), 0.0)
    else:
        total = corner_total(core, refs, rows_ref)
    value = activate(total, gain_ref[...], shift_ref[...])
    if not plane and not row:
        value = jnp.where(core == 0, 0.0, value)
    return value.astype(BF16)


def four_edges_kernel(core_ref, *refs):
    *thirds, local_ref, w_ref, place_ref, message_ref, mid_ref, rows_ref = refs
    core = core_ref[0]
    planes, rows, chans, width = thirds[0].shape
    rows_ref[...] = thirds[3][:planes]
    half = width // 2
    out_rows = rows // 2
    taps = 3 * chans
    mid_ref[...] = w_ref[:, 4 * taps : 5 * taps]

    def data(values):
        parts = [part.astype(BF16) for part in spread((jnp.concatenate(values, 0),), place_ref[...])]
        return [
            jnp.concatenate([part[at * chans : (at + 1) * chans] for part in parts], 0) for at in range(len(values))
        ]

    @pl.when(core == 0)
    def _():
        none = jnp.zeros((taps, half), BF16)
        rim = [none] + data(
            [third_value(core, thirds, plane, rows - 1) for plane in range(planes)]
            + [local_ref[plane] for plane in range(planes)]
        )
        pieces = [jnp.concatenate([rim[2 * m + slot] for m in range(planes)], 1) for slot in range(3)]
        weights = jnp.concatenate([w_ref[:, 3 * slot * taps : (3 * slot + 1) * taps] for slot in range(3)], 1)
        total = jnp.dot(weights, jnp.concatenate(pieces, 0), preferred_element_type=F32).astype(BF16)
        for m in range(planes):
            message_ref[m] = total[:, m * half : (m + 1) * half]
        for index in range(planes, message_ref.shape[0]):
            message_ref[index] = jnp.zeros_like(message_ref[index])

    @pl.when(core == 1)
    def _():
        halo_ref = thirds[3]
        last = data(
            [halo_ref[2 * planes + 1]] + [third_value(core, thirds, planes - 1, row) for row in range(rows)]
        )
        for row in range(0, out_rows, 2):
            pieces = [jnp.concatenate([last[2 * row + at], last[2 * row + 2 + at]], 1) for at in range(3)]
            both = jnp.dot(w_ref[:, : 3 * taps], jnp.concatenate(pieces, 0), preferred_element_type=F32)
            both = both.astype(BF16)
            message_ref[row] = both[:, :half]
            message_ref[row + 1] = both[:, half:]
        corner = halo_ref[2 * planes]
        message_ref[out_rows, :chans] = corner[:, :half]
        message_ref[out_rows, chans:] = corner[:, half:]


def four_edges(core, thirds, local, weights):
    planes, rows, chans, width = thirds[0].shape
    outs = weights.shape[0]
    half = width // 2
    return pl.pallas_call(
        four_edges_kernel,
        out_shape=[
            jax.ShapeDtypeStruct((rows // 2 + 1, outs, half), BF16),
            jax.ShapeDtypeStruct((outs, 3 * chans), BF16),
            jax.ShapeDtypeStruct((planes, chans, width), BF16),
        ],
        in_specs=inputs(len(thirds) + 3),
        compiler_params=pltpu.CompilerParams(vmem_limit_bytes=24 * MIB),
        cost_estimate=pl.CostEstimate(flops=10**9, bytes_accessed=10**6, transcendentals=0),
        name="four_edges",
    )(core, *thirds, local, weights, even_odd(width))


def four_kernel(core_ref, *refs):
    *thirds, rows_ref, local_ref, w_ref, place_ref, own_ref, theirs_ref, corner_ref, data_ref = refs
    core = core_ref[0]
    planes, rows, chans, width = thirds[0].shape
    halo_ref, gain_ref, shift_ref = thirds[3:]
    half = width // 2
    out_rows, count = rows // 2, planes // 2
    taps = 3 * chans
    batch = 4
    data_ref[:, 0] = jnp.zeros_like(data_ref[:, 0])
    corner_ref[...] = corner_total(core, thirds, rows_ref)

    def put(values, first, spots):
        for tap, part in enumerate(spread((jnp.concatenate(values, 0),), place_ref[...])):
            part = part.astype(BF16)
            for at in range(len(values)):
                for slot, lanes in spots:
                    data_ref[
                        slot, first + at + 1, tap * chans : (tap + 1) * chans, lanes * half : (lanes + 1) * half
                    ] = part[at * chans : (at + 1) * chans]

    @pl.when(core == 0)
    def _():
        data_ref[0, :, :, :half] = jnp.zeros_like(data_ref[0, :, :, :half])

    @pl.when(core == 1)
    def _():
        total = local_ref[0].astype(F32) + halo_ref[planes - 1].astype(F32)
        prior = [activate(total, gain_ref[...], shift_ref[...]).astype(BF16)]
        prior += [local_ref[row] for row in range(1, rows)]
        for first in range(0, rows, batch):
            put(prior[first : first + batch], first, [(0, 0)])

    for plane in range(planes):
        spots = [(1 + plane % 2, plane // 2)]
        if plane % 2 and plane // 2 + 1 < count:
            spots.append((0, plane // 2 + 1))
        for first in range(0, rows, batch):
            put([third_value(core, thirds, plane, row, rows_ref) for row in range(first, first + batch)], first, spots)
    for row in range(out_rows):
        parts = [data_ref[slot, 2 * row : 2 * row + 3].reshape(3 * taps, count * half) for slot in range(3)]
        total = jnp.dot(w_ref[...], jnp.concatenate(parts, 0), preferred_element_type=F32)
        own_ref[row] = jnp.where(core == 0, total[:LANES], total[LANES:])
        theirs_ref[row] = jnp.where(core == 0, total[LANES:], total[:LANES])


def layer_four(core, thirds, rows_before, local, weights):
    planes, rows, chans, width = thirds[0].shape
    outs = weights.shape[0]
    half = width // 2
    out_rows, count = rows // 2, planes // 2
    return pl.pallas_call(
        four_kernel,
        out_shape=[
            jax.ShapeDtypeStruct((out_rows, outs // 2, count * half), F32),
            jax.ShapeDtypeStruct((out_rows, outs // 2, count * half), F32),
            jax.ShapeDtypeStruct((chans, width), F32),
        ],
        in_specs=inputs(len(thirds) + 4),
        scratch_shapes=[pltpu.VMEM((3, rows + 1, 3 * chans, count * half), BF16)],
        compiler_params=pltpu.CompilerParams(vmem_limit_bytes=32 * MIB),
        cost_estimate=pl.CostEstimate(flops=4 * 10**9, bytes_accessed=4 * 10**6, transcendentals=0),
        name="layer_four",
    )(core, *thirds, rows_before, local, weights, even_odd(width))


def shares_kernel(core_ref, corner_ref, halo_ref, mid_ref, place_ref, gain_ref, shift_ref, shares_ref, fix_ref):
    core = core_ref[0]
    rows = halo_ref.shape[0] - 1

    @pl.when(core == 0)
    def _():
        corner = halo_ref[rows].astype(F32)
        total = corner_ref[...] + jnp.concatenate([corner[:LANES], corner[LANES:]], 1)
        value = activate(total, gain_ref[...], shift_ref[...]).astype(BF16)
        data = jnp.concatenate([part.astype(BF16) for part in spread((value,), place_ref[...])], 0)
        fix = jnp.dot(mid_ref[...], data, preferred_element_type=F32)
        fix_ref[...] = fix[:LANES]
        shares_ref[...] = halo_ref[:rows, LANES:].astype(F32)
        shares_ref[0] += fix[LANES:]

    @pl.when(core == 1)
    def _():
        fix_ref[...] = jnp.zeros_like(fix_ref)
        shares_ref[...] = halo_ref[:rows, :LANES].astype(F32)


def assemble_kernel(
    core_ref, own_ref, got_ref, halo_ref, fix_ref, scales_ref, shares_ref, out_ref, lines_ref
):
    core = core_ref[0]
    gain, shift = scales_ref[:, 1:2], scales_ref[:, 2:3]
    rows, width = halo_ref.shape[0] - 1, halo_ref.shape[2]
    count = own_ref.shape[2] // width

    def put(row, parts):
        for at, total in enumerate(parts):
            value = activate(total, gain, shift)
            for m in range(count):
                place = row * 2 * count + at * count + m
                lines_ref[pl.ds(place, LANES, stride=rows * 2 * count), :] = value[:, m * width : (m + 1) * width]

    def with_edge(total, edge):
        return jnp.concatenate([total[:, :width] + edge, total[:, width:]], 1)

    @pl.when(core == 0)
    def _():
        for row in range(rows):
            edge = halo_ref[row, :LANES].astype(F32)
            if not row:
                edge = edge + fix_ref[...]
            total, got = with_edge(own_ref[row], edge), got_ref[row]
            if not row:
                first = [shares_ref[m] for m in range(2 * count)]
                total = total + jnp.concatenate(first[:count], 1)
                got = got + jnp.concatenate(first[count:], 1)
            put(row, (total, got))

    @pl.when(core == 1)
    def _():
        for row in range(rows):
            total, got = own_ref[row], with_edge(got_ref[row], shares_ref[row])
            if not row:
                first = [halo_ref[m, LANES:].astype(F32) for m in range(2 * count)]
                total = total + jnp.concatenate(first[count:], 1)
                got = got + jnp.concatenate(first[:count], 1)
            put(row, (got, total))

    out_ref[...] = lines_ref[...].astype(BF16)


def last_stage(core, own, theirs, corner, halo, mid, gain, shift, scales):
    rows, outs, lanes = own.shape
    got = swapped(theirs)
    shares, fix = pl.pallas_call(
        shares_kernel,
        out_shape=[
            jax.ShapeDtypeStruct((rows, outs, halo.shape[2]), F32),
            jax.ShapeDtypeStruct((outs, halo.shape[2]), F32),
        ],
        in_specs=inputs(6),
        compiler_params=pltpu.CompilerParams(vmem_limit_bytes=16 * MIB),
        cost_estimate=pl.CostEstimate(flops=10**8, bytes_accessed=10**6, transcendentals=0),
        name="shares",
    )(core, corner, halo, mid, even_odd(lanes), gain, shift)
    lines = (outs * rows * lanes * 2 // LANES, LANES)
    return pl.pallas_call(
        assemble_kernel,
        out_shape=jax.ShapeDtypeStruct(lines, BF16),
        in_specs=inputs(6),
        scratch_shapes=[pltpu.VMEM(lines, F32)],
        compiler_params=pltpu.CompilerParams(vmem_limit_bytes=16 * MIB),
        name="assemble",
    )(core, own, got, halo, fix, scales, swapped(shares))


def handed_on(message):
    count = lax.axis_size("sp")
    pairs = [(2 * b, 2 * (b + 1) + 1) for b in range(count) if b % ROW_BLOCKS != ROW_BLOCKS - 1]
    pairs += [(2 * b + 1, 2 * (b + ROW_BLOCKS)) for b in range(count - ROW_BLOCKS)]
    return lax.ppermute(message, ("sp", "fl"), pairs)


def swapped(value):
    return lax.ppermute(value, "fl", [(0, 1), (1, 0)])


def shards(volume, kernel_three, gain_three, shift_three, kernel_four, gain_four, shift_four):
    core = lax.axis_index("fl").reshape(1)
    own_scales = jnp.concatenate([gain_three, shift_three, gain_four, shift_four]).reshape(-1, LANES)
    picked, prior = three_picks(volume, core)
    others = lax.optimization_barrier((swapped(kernel_three), swapped(own_scales), swapped(kernel_four)))
    message, weights_three, gain, shift, scales = three_edges(
        picked, kernel_three, others[0], own_scales, others[1], core
    )
    halo = handed_on(message)
    *thirds, local = layer_three(volume, prior, weights_three, gain, shift, core)
    halo, other_four = lax.optimization_barrier((halo, others[2]))
    thirds = (*thirds, halo, gain, shift)
    local = swapped(local)
    weights_four = four_weights(kernel_four, other_four, core)
    message, mid, rows = four_edges(core, thirds, local, weights_four)
    halo = handed_on(message)
    rows = lax.ppermute(rows, "fl", [(1, 0)])
    own, theirs, corner = layer_four(core, thirds, rows, local, weights_four)
    lines = last_stage(core, own, theirs, corner, halo, mid, gain, shift, scales)
    out_rows, outs, lanes = own.shape
    fourth = lines.reshape(outs, out_rows, 2 * lanes // LANES, LANES)
    return jnp.transpose(fourth, (0, 2, 1, 3))[None]


def solution(mesh):
    return jax.shard_map(
        shards,
        mesh=mesh,
        in_specs=(
            P("sp", None, None, None, None),
            P("fl", None),
            P("fl"),
            P("fl"),
            P("fl", None),
            P("fl"),
            P("fl"),
        ),
        out_specs=P("sp", "fl", None, None, None),
        check_vma=False,
    )
```

```python
import functools

import jax
import jax.numpy as jnp
import numpy as np
from jax import lax
from jax.experimental import pallas as pl
from jax.experimental.pallas import tpu as pltpu
from jax.sharding import PartitionSpec as P

F32 = jnp.float32
BF16 = jnp.bfloat16
LANES = 128
ROW_BLOCKS = 8
SUB = 8
TAPS = 27
RIM_TAPS = tuple(9 * a + e for a in range(3) for e in range(3))
GROUP = 16
MIB = 2**20


def even_odd(width):
    half = width // 2
    place = np.zeros((width, width), np.float32)
    place[np.arange(0, width, 2), np.arange(half)] = 1
    place[np.arange(1, width, 2), half + np.arange(half)] = 1
    return jnp.asarray(place, BF16)


def activate(total, gain, shift):
    return jnp.maximum(total * gain + shift, 0.0)


def shifted(odd):
    lane = lax.broadcasted_iota(jnp.int32, odd.shape, 1)
    return jnp.where(lane == 0, 0.0, pltpu.roll(odd, 1, 1))


def spread(sides, place):
    quarter = place.shape[0] // 2
    split = [jnp.dot(side, place, preferred_element_type=F32) for side in sides]
    even = jnp.concatenate([part[:, :quarter] for part in split], 1)
    odd = jnp.concatenate([part[:, quarter:] for part in split], 1)
    return shifted(odd), even, odd


def separate(x_ref, plane, place_ref, split_refs, store):
    chans, rows, width = x_ref.shape[1], x_ref.shape[3], x_ref.shape[4]
    half = width // 2
    quarter = half // 2
    for index, first in enumerate(range(0, chans, GROUP)):
        split_ref = split_refs[index % len(split_refs)]
        x = x_ref[0, pl.ds(first, GROUP), plane]
        x = x.astype(F32).reshape(GROUP * rows, width).astype(BF16)
        for side in range(2):
            parts = jnp.dot(
                x[:, side * half : (side + 1) * half], place_ref[...], preferred_element_type=F32
            )
            for block in range(half // LANES):
                odd, at = divmod(block, quarter // LANES)
                split_ref[odd, side * (quarter // LANES) + at] = parts[:, block * LANES : (block + 1) * LANES]
        for row in range(rows):
            even, odd = (
                jnp.concatenate(
                    [split_ref[odd, at, pl.ds(row, GROUP, stride=rows), :] for at in range(half // LANES)], 1
                )
                for odd in range(2)
            )
            for tap, value in enumerate((shifted(odd), even, odd)):
                store(tap, row, first, value.astype(BF16))
        yield


def inputs(count):
    return [pl.BlockSpec(memory_space=pltpu.SMEM)] + [pl.BlockSpec(memory_space=pltpu.VMEM)] * count


def whole(own, other, core):
    first = jnp.where(core == 0, own, other)
    second = jnp.where(core == 0, other, own)
    return jnp.concatenate([first, second], 0)


def turn(kernel, turned_ref):
    columns = kernel.shape[1]
    for at in range(0, columns, LANES):
        size = min(LANES, columns - at)
        turned_ref[at : at + size, :] = kernel[:, at : at + size].T


def tap_major(turned_ref, taps, w_ref, first):
    chans = turned_ref.shape[0] // TAPS
    at = 0
    for index in range(0, len(taps), LANES // chans):
        parts = [turned_ref[pl.ds(tap, chans, stride=TAPS), :] for tap in taps[index : index + LANES // chans]]
        block = jnp.concatenate(parts, 0).T.astype(BF16)
        w_ref[first : first + LANES, at : at + block.shape[1]] = block
        at += block.shape[1]


def four_weights_kernel(core_ref, own_ref, other_ref, w_ref, *turned_refs):
    core = core_ref[0]
    for index, turned_ref in enumerate(turned_refs):
        turn(jnp.where(core == index, own_ref[...].astype(F32), other_ref[...].astype(F32)), turned_ref)
        tap_major(turned_ref, range(TAPS), w_ref, index * LANES)


def four_weights(own, other, core):
    outs, columns = own.shape
    return pl.pallas_call(
        four_weights_kernel,
        out_shape=jax.ShapeDtypeStruct((2 * outs, columns), BF16),
        in_specs=[
            pl.BlockSpec(memory_space=pltpu.SMEM),
            pl.BlockSpec(memory_space=pltpu.VMEM),
            pl.BlockSpec(memory_space=pltpu.VMEM),
        ],
        scratch_shapes=[pltpu.VMEM((columns, LANES), F32)] * 2,
        compiler_params=pltpu.CompilerParams(vmem_limit_bytes=16 * MIB),
        cost_estimate=pl.CostEstimate(flops=10**3, bytes_accessed=10**3, transcendentals=0),
        name="four_weights",
    )(core, own, other)


def three_picks_kernel(core_ref, last_ref, before_ref, rim_ref, picked_ref, prior_ref, *scratch):
    *split_refs, pick_ref, place_ref = scratch
    core, step, last = core_ref[0], pl.program_id(0), pl.num_programs(0) - 1
    chans, block, width = rim_ref.shape[1], rim_ref.shape[2], rim_ref.shape[4]
    rows, part = last_ref.shape[3], last_ref.shape[1]
    planes = block * 4
    half = width // 2
    rim = (rows - 1) % SUB

    @pl.when(step == 0)
    def _():
        source = lax.broadcasted_iota(jnp.int32, place_ref.shape, 0)
        target = lax.broadcasted_iota(jnp.int32, place_ref.shape, 1)
        quarter = half // 2
        wanted = jnp.where(target < quarter, 2 * target, 2 * (target - quarter) + 1)
        place_ref[...] = jnp.where(source == wanted, 1.0, 0.0).astype(BF16)

    def picked(spots):
        values, held = [], None
        for plane, row in spots:
            if plane != held:
                x = rim_ref[0, :, plane, :SUB].astype(F32).reshape(chans * SUB, width)
                for at in range(width // LANES):
                    pick_ref[plane % 2, at] = x[:, at * LANES : (at + 1) * LANES]
                held = plane
            values.append(
                jnp.concatenate(
                    [pick_ref[plane % 2, at, pl.ds(row, chans, stride=SUB), :] for at in range(width // LANES)], 1
                ).astype(BF16)
            )
        values = jnp.concatenate(values, 0)
        parts = [part.astype(BF16) for part in spread((values[:, :half], values[:, half:]), place_ref[...])]
        return [
            jnp.concatenate([part[at * chans : (at + 1) * chans] for part in parts], 0) for at in range(len(spots))
        ]

    @pl.when((core == 0) & (step < last))
    def _():
        for plane, data in enumerate(picked([(plane, rim) for plane in range(block)])):
            picked_ref[step * block + plane] = data

    @pl.when((core == 0) & (step == last))
    def _():
        spots = [(plane, row) for plane in range(block - 3, block) for row in range(rim - 2, rim + 1)]
        alone = [(plane, rim) for plane in range(block - 3)]
        for index, ((plane, row), data) in enumerate(zip(spots + alone, picked(spots + alone))):
            if index < len(spots):
                picked_ref[planes + index] = data
            if row == rim:
                picked_ref[planes - block + plane] = data
        prior_ref[...] = jnp.zeros_like(prior_ref)

    @pl.when(core == 1)
    def _():
        for source_ref, to_ref in ((last_ref, picked_ref), (before_ref, prior_ref)):

            def store(tap, row, first, value):
                at = pl.multiple_of(tap * chans + step * part + first, GROUP)
                to_ref[row + 1, pl.ds(at, GROUP), :] = value

            for _ in separate(source_ref, 0, place_ref, split_refs, store):
                pass

    @pl.when((core == 1) & (step == last))
    def _():
        for ref in (picked_ref, prior_ref):
            ref[0] = jnp.zeros_like(ref[0])


def three_picks(volume, core):
    _, chans, planes, rows, width = volume.shape
    half = width // 2
    block, steps = planes // 4, 4
    shape = (rows + 1, 3 * chans, half)
    full = lambda *shape: pl.BlockSpec(shape, lambda i, core: (0,) * len(shape))
    return pl.pallas_call(
        three_picks_kernel,
        grid_spec=pltpu.PrefetchScalarGridSpec(
            num_scalar_prefetch=1,
            grid=(steps,),
            in_specs=[
                pl.BlockSpec((1, chans // steps, 1, rows, width), lambda i, core: (0, i * core[0], planes - 1, 0, 0)),
                pl.BlockSpec(
                    (1, chans // steps, 1, rows, width), lambda i, core: (0, i * core[0], planes // 2 - 1, 0, 0)
                ),
                pl.BlockSpec(
                    (1, chans, block, 2 * SUB, width),
                    lambda i, core: (0, 0, i + core[0] * (steps - 1 - i), (rows - 1) // (2 * SUB), 0),
                ),
            ],
            out_specs=[full(*shape), full(*shape)],
            scratch_shapes=[pltpu.VMEM((2, half // LANES, GROUP * rows, LANES), F32)] * 2
            + [pltpu.VMEM((2, width // LANES, chans * SUB, LANES), F32), pltpu.VMEM((half, half), BF16)],
        ),
        out_shape=[jax.ShapeDtypeStruct(shape, BF16)] * 2,
        compiler_params=pltpu.CompilerParams(vmem_limit_bytes=28 * MIB),
        cost_estimate=pl.CostEstimate(flops=10**9, bytes_accessed=10**7, transcendentals=0),
        name="three_picks",
    )(core, volume, volume, volume)


def three_edges_kernel(
    core_ref, picked_ref, own_ref, other_ref, own_scales_ref, other_scales_ref,
    message_ref, w_ref, gain_ref, shift_ref, scales_ref,
    turned_ref, rim_w_ref,
):
    core = core_ref[0]
    count, taps, half = picked_ref.shape
    out_rows = message_ref.shape[0]
    planes = count - 9
    turn(whole(own_ref[...].astype(F32), other_ref[...].astype(F32), core), turned_ref)
    tap_major(turned_ref, range(TAPS), w_ref, 0)
    own_scales, other_scales = own_scales_ref[...], other_scales_ref[...]
    lines = own_scales.shape[0]
    scales = jnp.concatenate([own_scales, other_scales, jnp.zeros((LANES - 2 * lines, LANES), F32)], 0).T
    scales_ref[...] = scales
    share = own_ref.shape[0]
    for ref, at in ((gain_ref, 0), (shift_ref, share)):
        ref[...] = whole(scales[at : at + share, 0:1], scales[at : at + share, lines : lines + 1], core)

    @pl.when(core == 0)
    def _():
        tap_major(turned_ref, RIM_TAPS, rim_w_ref, 0)
        none = jnp.zeros((taps, half), BF16)
        for index in range(planes // 2 + 1):
            pieces = [
                picked_ref[plane] if 0 <= plane < planes else none for plane in range(2 * index - 1, 2 * index + 2)
            ]
            total = jnp.dot(rim_w_ref[...], jnp.concatenate(pieces, 0), preferred_element_type=F32)
            message_ref[index] = total.astype(BF16)
        data = picked_ref[planes:].reshape(9 * taps, half)
        total = jnp.dot(w_ref[...], data, preferred_element_type=F32)
        message_ref[planes // 2 + 1] = activate(total, gain_ref[...], shift_ref[...]).astype(BF16)
        for index in range(planes // 2 + 2, out_rows):
            message_ref[index] = jnp.zeros_like(message_ref[index])

    @pl.when(core == 1)
    def _():
        for row in range(out_rows):
            total = jnp.dot(
                w_ref[:, : 3 * taps],
                picked_ref[2 * row : 2 * row + 3].reshape(3 * taps, half),
                preferred_element_type=F32,
            )
            message_ref[row] = total.astype(BF16)


def three_edges(picked, own, other, own_scales, other_scales, core):
    outs, columns = 2 * own.shape[0], own.shape[1]
    out_rows, half = picked.shape[0] // 2, picked.shape[2]
    shapes = [
        ((out_rows, outs, half), BF16),
        ((outs, columns), BF16),
        ((outs, 1), F32),
        ((outs, 1), F32),
        ((LANES, LANES), F32),
    ]
    return pl.pallas_call(
        three_edges_kernel,
        in_specs=inputs(5),
        out_shape=[jax.ShapeDtypeStruct(*shape) for shape in shapes],
        scratch_shapes=[pltpu.VMEM((columns, LANES), F32), pltpu.VMEM((outs, columns // 3), BF16)],
        compiler_params=pltpu.CompilerParams(vmem_limit_bytes=16 * MIB),
        cost_estimate=pl.CostEstimate(flops=10**9, bytes_accessed=10**6, transcendentals=0),
        name="three_edges",
    )(core, picked, own, other, own_scales, other_scales)


def three_kernel(
    core_ref, x_ref, before_ref, w_ref, place_ref, gain_ref, shift_ref,
    third_ref, plane_ref, row_ref, local_ref,
    *scratch,
):
    *split_refs, even_ref, odd_ref = scratch
    core, step, last = core_ref[0], pl.program_id(0), pl.num_programs(0) - 1
    chans, rows, width = x_ref.shape[1], x_ref.shape[3], x_ref.shape[4]
    half = width // 2
    out_rows = rows // 2
    taps = 3 * chans
    prior, new = (step + 1) % 2, step % 2

    @pl.when(step == 0)
    def _():
        odd_ref[1] = before_ref[...]
        even_ref[0] = jnp.zeros_like(even_ref[0])
        odd_ref[0, 0] = jnp.zeros_like(even_ref[0])

    def store_even(tap, row, first, value):
        even_ref[row + 1, tap * chans + first : tap * chans + first + GROUP, :] = value

    def store_odd(tap, row, first, value):
        odd_ref[new, row + 1, tap * chans + first : tap * chans + first + GROUP, :] = value

    for plane, store in enumerate((store_even, store_odd)):
        for _ in separate(x_ref, plane, place_ref, split_refs, store):
            pass

    def summing(keep):
        gain, shift = gain_ref[...], shift_ref[...]
        for row in range(out_rows):
            span = slice(2 * row, 2 * row + 3)
            parts = [odd_ref[prior, span], even_ref[span], odd_ref[new, span]]
            data = jnp.concatenate([part.reshape(3 * taps, half) for part in parts], 0)
            total = jnp.dot(w_ref[...], data, preferred_element_type=F32)
            third_ref[0, row] = activate(total, gain, shift).astype(BF16)
            if keep:
                plane_ref[row] = total
            if not row:
                row_ref[0] = total

    @pl.when(step == 0)
    def _():
        summing(True)

    @pl.when(step > 0)
    def _():
        summing(False)

    @pl.when(core == 1)
    def _():
        local_ref[step] = third_ref[0, out_rows - 1]

    @pl.when((step == last) & (core == 0))
    def _():
        local_ref[...] = third_ref[0]
        local_ref[0] = row_ref[0].astype(BF16)


def layer_three(volume, prior, weights, gain, shift, core):
    _, chans, planes, rows, width = volume.shape
    outs = weights.shape[0]
    half = width // 2
    steps, out_rows = planes // 4, rows // 2
    full = lambda *shape: pl.BlockSpec(shape, lambda i, core: (0,) * len(shape))
    return pl.pallas_call(
        three_kernel,
        grid_spec=pltpu.PrefetchScalarGridSpec(
            num_scalar_prefetch=1,
            grid=(steps,),
            in_specs=[
                pl.BlockSpec((1, chans, 2, rows, width), lambda i, core: (0, 0, core[0] * steps + i, 0, 0)),
                pl.BlockSpec(prior.shape, lambda i, core: (0, 0, 0), pipeline_mode=pl.Buffered(1)),
                full(*weights.shape),
                full(half, half),
                full(outs, 1),
                full(outs, 1),
            ],
            out_specs=[
                pl.BlockSpec((1, out_rows, outs, half), lambda i, core: (i, 0, 0, 0)),
                full(out_rows, outs, half),
                pl.BlockSpec((1, outs, half), lambda i, core: (i, 0, 0)),
                full(out_rows, outs, half),
            ],
            scratch_shapes=[pltpu.VMEM((2, half // LANES, GROUP * rows, LANES), F32)] * 4
            + [
                pltpu.VMEM((rows + 1, 3 * chans, half), BF16),
                pltpu.VMEM((2, rows + 1, 3 * chans, half), BF16),
            ],
        ),
        out_shape=[
            jax.ShapeDtypeStruct((steps, out_rows, outs, half), BF16),
            jax.ShapeDtypeStruct((out_rows, outs, half), F32),
            jax.ShapeDtypeStruct((steps, outs, half), F32),
            jax.ShapeDtypeStruct((out_rows, outs, half), BF16),
        ],
        compiler_params=pltpu.CompilerParams(vmem_limit_bytes=34 * MIB),
        cost_estimate=pl.CostEstimate(flops=10**10, bytes_accessed=2 * 10**7, transcendentals=0),
        name="layer_three",
    )(core, volume, prior, weights, even_odd(half), gain, shift)


def corner_total(core, refs, rows_ref):
    third_ref, plane_ref, _, halo_ref, _, _ = refs
    planes = third_ref.shape[0]
    first = jnp.where(core == 0, rows_ref[0].astype(F32), halo_ref[planes].astype(F32))
    return plane_ref[0] + jnp.where(core == 0, halo_ref[0].astype(F32), 0.0) + first


def third_value(core, refs, plane, row, rows_ref=None):
    third_ref, plane_ref, row_ref, halo_ref, gain_ref, shift_ref = refs
    planes = third_ref.shape[0]
    if plane and row:
        return third_ref[plane, row]
    if plane:
        share = halo_ref[planes + plane].astype(F32)
        if rows_ref is not None:
            share = jnp.where(core == 0, rows_ref[plane].astype(F32), share)
        total = row_ref[plane] + share
    elif row:
        total = plane_ref[row] + jnp.where(core == 0, halo_ref[row].astype(F32), 0.0)
    else:
        total = corner_total(core, refs, rows_ref)
    value = activate(total, gain_ref[...], shift_ref[...])
    if not plane and not row:
        value = jnp.where(core == 0, 0.0, value)
    return value.astype(BF16)


def four_edges_kernel(core_ref, *refs):
    *thirds, local_ref, w_ref, place_ref, message_ref, mid_ref, rows_ref = refs
    core = core_ref[0]
    planes, rows, chans, width = thirds[0].shape
    rows_ref[...] = thirds[3][:planes]
    half = width // 2
    out_rows = rows // 2
    taps = 3 * chans
    mid_ref[...] = w_ref[:, 4 * taps : 5 * taps]

    def data(values):
        parts = [part.astype(BF16) for part in spread((jnp.concatenate(values, 0),), place_ref[...])]
        return [
            jnp.concatenate([part[at * chans : (at + 1) * chans] for part in parts], 0) for at in range(len(values))
        ]

    @pl.when(core == 0)
    def _():
        none = jnp.zeros((taps, half), BF16)
        rim = [none] + data(
            [third_value(core, thirds, plane, rows - 1) for plane in range(planes)]
            + [local_ref[plane] for plane in range(planes)]
        )
        pieces = [jnp.concatenate([rim[2 * m + slot] for m in range(planes)], 1) for slot in range(3)]
        weights = jnp.concatenate([w_ref[:, 3 * slot * taps : (3 * slot + 1) * taps] for slot in range(3)], 1)
        total = jnp.dot(weights, jnp.concatenate(pieces, 0), preferred_element_type=F32).astype(BF16)
        for m in range(planes):
            message_ref[m] = total[:, m * half : (m + 1) * half]
        for index in range(planes, message_ref.shape[0]):
            message_ref[index] = jnp.zeros_like(message_ref[index])

    @pl.when(core == 1)
    def _():
        halo_ref = thirds[3]
        last = data(
            [halo_ref[2 * planes + 1]] + [third_value(core, thirds, planes - 1, row) for row in range(rows)]
        )
        for row in range(0, out_rows, 2):
            pieces = [jnp.concatenate([last[2 * row + at], last[2 * row + 2 + at]], 1) for at in range(3)]
            both = jnp.dot(w_ref[:, : 3 * taps], jnp.concatenate(pieces, 0), preferred_element_type=F32)
            both = both.astype(BF16)
            message_ref[row] = both[:, :half]
            message_ref[row + 1] = both[:, half:]
        corner = halo_ref[2 * planes]
        message_ref[out_rows, :chans] = corner[:, :half]
        message_ref[out_rows, chans:] = corner[:, half:]


def four_edges(core, thirds, local, weights):
    planes, rows, chans, width = thirds[0].shape
    outs = weights.shape[0]
    half = width // 2
    return pl.pallas_call(
        four_edges_kernel,
        out_shape=[
            jax.ShapeDtypeStruct((rows // 2 + 1, outs, half), BF16),
            jax.ShapeDtypeStruct((outs, 3 * chans), BF16),
            jax.ShapeDtypeStruct((planes, chans, width), BF16),
        ],
        in_specs=inputs(len(thirds) + 3),
        compiler_params=pltpu.CompilerParams(vmem_limit_bytes=24 * MIB),
        cost_estimate=pl.CostEstimate(flops=10**9, bytes_accessed=10**6, transcendentals=0),
        name="four_edges",
    )(core, *thirds, local, weights, even_odd(width))


def four_kernel(core_ref, *refs):
    *thirds, rows_ref, local_ref, w_ref, place_ref, own_ref, theirs_ref, corner_ref, data_ref = refs
    core = core_ref[0]
    planes, rows, chans, width = thirds[0].shape
    halo_ref, gain_ref, shift_ref = thirds[3:]
    half = width // 2
    out_rows, count = rows // 2, planes // 2
    taps = 3 * chans
    batch = 4
    data_ref[:, 0] = jnp.zeros_like(data_ref[:, 0])
    corner_ref[...] = corner_total(core, thirds, rows_ref)

    def put(values, first, spots):
        for tap, part in enumerate(spread((jnp.concatenate(values, 0),), place_ref[...])):
            part = part.astype(BF16)
            for at in range(len(values)):
                for slot, lanes in spots:
                    data_ref[
                        slot, first + at + 1, tap * chans : (tap + 1) * chans, lanes * half : (lanes + 1) * half
                    ] = part[at * chans : (at + 1) * chans]

    @pl.when(core == 0)
    def _():
        data_ref[0, :, :, :half] = jnp.zeros_like(data_ref[0, :, :, :half])

    @pl.when(core == 1)
    def _():
        total = local_ref[0].astype(F32) + halo_ref[planes - 1].astype(F32)
        prior = [activate(total, gain_ref[...], shift_ref[...]).astype(BF16)]
        prior += [local_ref[row] for row in range(1, rows)]
        for first in range(0, rows, batch):
            put(prior[first : first + batch], first, [(0, 0)])

    for plane in range(planes):
        spots = [(1 + plane % 2, plane // 2)]
        if plane % 2 and plane // 2 + 1 < count:
            spots.append((0, plane // 2 + 1))
        for first in range(0, rows, batch):
            put([third_value(core, thirds, plane, row, rows_ref) for row in range(first, first + batch)], first, spots)
    for row in range(out_rows):
        parts = [data_ref[slot, 2 * row : 2 * row + 3].reshape(3 * taps, count * half) for slot in range(3)]
        total = jnp.dot(w_ref[...], jnp.concatenate(parts, 0), preferred_element_type=F32)
        own_ref[row] = jnp.where(core == 0, total[:LANES], total[LANES:])
        theirs_ref[row] = jnp.where(core == 0, total[LANES:], total[:LANES])


def layer_four(core, thirds, rows_before, local, weights):
    planes, rows, chans, width = thirds[0].shape
    outs = weights.shape[0]
    half = width // 2
    out_rows, count = rows // 2, planes // 2
    return pl.pallas_call(
        four_kernel,
        out_shape=[
            jax.ShapeDtypeStruct((out_rows, outs // 2, count * half), F32),
            jax.ShapeDtypeStruct((out_rows, outs // 2, count * half), F32),
            jax.ShapeDtypeStruct((chans, width), F32),
        ],
        in_specs=inputs(len(thirds) + 4),
        scratch_shapes=[pltpu.VMEM((3, rows + 1, 3 * chans, count * half), BF16)],
        compiler_params=pltpu.CompilerParams(vmem_limit_bytes=32 * MIB),
        cost_estimate=pl.CostEstimate(flops=4 * 10**9, bytes_accessed=4 * 10**6, transcendentals=0),
        name="layer_four",
    )(core, *thirds, rows_before, local, weights, even_odd(width))


def shares_kernel(core_ref, corner_ref, halo_ref, mid_ref, place_ref, gain_ref, shift_ref, shares_ref, fix_ref):
    core = core_ref[0]
    rows = halo_ref.shape[0] - 1

    @pl.when(core == 0)
    def _():
        corner = halo_ref[rows].astype(F32)
        total = corner_ref[...] + jnp.concatenate([corner[:LANES], corner[LANES:]], 1)
        value = activate(total, gain_ref[...], shift_ref[...]).astype(BF16)
        data = jnp.concatenate([part.astype(BF16) for part in spread((value,), place_ref[...])], 0)
        fix = jnp.dot(mid_ref[...], data, preferred_element_type=F32)
        fix_ref[...] = fix[:LANES]
        shares_ref[...] = halo_ref[:rows, LANES:].astype(F32)
        shares_ref[0] += fix[LANES:]

    @pl.when(core == 1)
    def _():
        fix_ref[...] = jnp.zeros_like(fix_ref)
        shares_ref[...] = halo_ref[:rows, :LANES].astype(F32)


def assemble_kernel(
    core_ref, own_ref, got_ref, halo_ref, fix_ref, scales_ref, shares_ref, out_ref, lines_ref
):
    core = core_ref[0]
    gain, shift = scales_ref[:, 1:2], scales_ref[:, 2:3]
    rows, width = halo_ref.shape[0] - 1, halo_ref.shape[2]
    count = own_ref.shape[2] // width

    def put(row, parts):
        for at, total in enumerate(parts):
            value = activate(total, gain, shift)
            for m in range(count):
                place = row * 2 * count + at * count + m
                lines_ref[pl.ds(place, LANES, stride=rows * 2 * count), :] = value[:, m * width : (m + 1) * width]

    def with_edge(total, edge):
        return jnp.concatenate([total[:, :width] + edge, total[:, width:]], 1)

    @pl.when(core == 0)
    def _():
        for row in range(rows):
            edge = halo_ref[row, :LANES].astype(F32)
            if not row:
                edge = edge + fix_ref[...]
            total, got = with_edge(own_ref[row], edge), got_ref[row]
            if not row:
                first = [shares_ref[m] for m in range(2 * count)]
                total = total + jnp.concatenate(first[:count], 1)
                got = got + jnp.concatenate(first[count:], 1)
            put(row, (total, got))

    @pl.when(core == 1)
    def _():
        for row in range(rows):
            total, got = own_ref[row], with_edge(got_ref[row], shares_ref[row])
            if not row:
                first = [halo_ref[m, LANES:].astype(F32) for m in range(2 * count)]
                total = total + jnp.concatenate(first[count:], 1)
                got = got + jnp.concatenate(first[:count], 1)
            put(row, (got, total))

    out_ref[...] = lines_ref[...].astype(BF16)


def last_stage(core, own, theirs, corner, halo, mid, gain, shift, scales):
    rows, outs, lanes = own.shape
    got = swapped(theirs)
    shares, fix = pl.pallas_call(
        shares_kernel,
        out_shape=[
            jax.ShapeDtypeStruct((rows, outs, halo.shape[2]), F32),
            jax.ShapeDtypeStruct((outs, halo.shape[2]), F32),
        ],
        in_specs=inputs(6),
        compiler_params=pltpu.CompilerParams(vmem_limit_bytes=16 * MIB),
        cost_estimate=pl.CostEstimate(flops=10**8, bytes_accessed=10**6, transcendentals=0),
        name="shares",
    )(core, corner, halo, mid, even_odd(lanes), gain, shift)
    lines = (outs * rows * lanes * 2 // LANES, LANES)
    return pl.pallas_call(
        assemble_kernel,
        out_shape=jax.ShapeDtypeStruct(lines, BF16),
        in_specs=inputs(6),
        scratch_shapes=[pltpu.VMEM(lines, F32)],
        compiler_params=pltpu.CompilerParams(vmem_limit_bytes=16 * MIB),
        name="assemble",
    )(core, own, got, halo, fix, scales, swapped(shares))


def handed_on(message):
    count = lax.axis_size("sp")
    pairs = [(2 * b, 2 * (b + 1) + 1) for b in range(count) if b % ROW_BLOCKS != ROW_BLOCKS - 1]
    pairs += [(2 * b + 1, 2 * (b + ROW_BLOCKS)) for b in range(count - ROW_BLOCKS)]
    return lax.ppermute(message, ("sp", "fl"), pairs)


def swapped(value):
    return lax.ppermute(value, "fl", [(0, 1), (1, 0)])


def shards(volume, kernel_three, gain_three, shift_three, kernel_four, gain_four, shift_four):
    core = lax.axis_index("fl").reshape(1)
    own_scales = jnp.concatenate([gain_three, shift_three, gain_four, shift_four]).reshape(-1, LANES)
    picked, prior = three_picks(volume, core)
    others = lax.optimization_barrier((swapped(kernel_three), swapped(own_scales), swapped(kernel_four)))
    message, weights_three, gain, shift, scales = three_edges(
        picked, kernel_three, others[0], own_scales, others[1], core
    )
    halo = handed_on(message)
    *thirds, local = layer_three(volume, prior, weights_three, gain, shift, core)
    halo, other_four = lax.optimization_barrier((halo, others[2]))
    thirds = (*thirds, halo, gain, shift)
    local = swapped(local)
    weights_four = four_weights(kernel_four, other_four, core)
    message, mid, rows = four_edges(core, thirds, local, weights_four)
    halo = handed_on(message)
    rows = lax.ppermute(rows, "fl", [(1, 0)])
    own, theirs, corner = layer_four(core, thirds, rows, local, weights_four)
    lines = last_stage(core, own, theirs, corner, halo, mid, gain, shift, scales)
    out_rows, outs, lanes = own.shape
    fourth = lines.reshape(outs, out_rows, 2 * lanes // LANES, LANES)
    return jnp.transpose(fourth, (0, 2, 1, 3))[None]


def solution(mesh):
    return jax.shard_map(
        shards,
        mesh=mesh,
        in_specs=(
            P("sp", None, None, None, None),
            P("fl", None),
            P("fl"),
            P("fl"),
            P("fl", None),
            P("fl"),
            P("fl"),
        ),
        out_specs=P("sp", "fl", None, None, None),
        check_vma=False,
    )
```
